32 devices in a mesh: tower: 2 (over core), dp: 16 (over z, y, x).
Axes of the slice: x: 2, y: 2, z: 4, core: 2. Of those that a mesh axis runs over, the one named last changes fastest.
Arguments:
- hidden_in: bfloat16 [2, 32768, 768], P('tower', 'dp'), may hold values from -4 to 4
- segment_ids: int32 [2, 32, 1024], P('tower', 'dp'), may hold values from 0 to 31, never falling along the last dimension, each value on 1 to 64 neighbouring positions
- positives: int32 [1024], replicated, may hold values from 0 to 1023
- w_query: bfloat16 [768, 768], replicated, may hold values from -0.21875 to 0.21875
- b_query: bfloat16 [768], replicated, may hold values from -3 to 3
- w_key: bfloat16 [768, 768], replicated, may hold values from -0.21875 to 0.21875
- w_value: bfloat16 [768, 768], replicated, may hold values from -0.21875 to 0.21875
- b_value: bfloat16 [768], replicated, may hold values from -3 to 3
- w_out: bfloat16 [768, 768], replicated, may hold values from -0.875 to 0.875
- b_out: bfloat16 [768], replicated, may hold values from -3 to 3
- gain_attn: bfloat16 [768], replicated, may hold values from 0.25 to 1.75
- shift_attn: bfloat16 [768], replicated, may hold values from -1 to 1
- w_in: bfloat16 [768, 3072], replicated, may hold values from -0.21875 to 0.21875
- b_in: bfloat16 [3072], replicated, may hold values from -3 to 3
- w_back: bfloat16 [3072, 768], replicated, may hold values from -0.109375 to 0.109375
- b_back: bfloat16 [768], replicated, may hold values from -3 to 3
- gain_ffn: bfloat16 [768], replicated, may hold values from 0.25 to 1.75
- shift_ffn: bfloat16 [768], replicated, may hold values from -1 to 1
Outputs:
- encoded: bfloat16 [2, 32768, 768], P('tower', 'dp')
- scores: float32 [1024, 1024], P(None, 'dp')
- losses: float32 [1024], replicated
- grad_hidden: float32 [2, 32768, 768], P('tower', 'dp')
- grad_w_query: float32 [768, 768], P(('tower', 'dp'))
- grad_b_query: float32 [768], P(('tower', 'dp'))
- grad_w_key: float32 [768, 768], P(('tower', 'dp'))
- grad_w_value: float32 [768, 768], P(('tower', 'dp'))
- grad_b_value: float32 [768], P(('tower', 'dp'))
- grad_w_out: float32 [768, 768], P(('tower', 'dp'))
- grad_b_out: float32 [768], P(('tower', 'dp'))
- grad_gain_attn: float32 [768], P(('tower', 'dp'))
- grad_shift_attn: float32 [768], P(('tower', 'dp'))
- grad_w_in: float32 [768, 3072], P(('tower', 'dp'))
- grad_b_in: float32 [3072], P(('tower', 'dp'))
- grad_w_back: float32 [3072, 768], P(('tower', 'dp'))
- grad_b_back: float32 [768], P(('tower', 'dp'))
- grad_gain_ffn: float32 [768], P(('tower', 'dp'))
- grad_shift_ffn: float32 [768], P(('tower', 'dp'))
The draws below stay inside these ranges and needn't reach their ends.
Inputs may be any that keep to these rules, and one draw needn't show every extreme that they name: `segment_ids`: in each row the ids never fall, each of 0 to 31 holds 1 to 64 tokens and one holds exactly 64; a segment is one query (tower index 0) or one passage (tower index 1), and its first token is its CLS token.
All inputs are finite; a program needn't handle non-finite values.
Results may differ from the reference program's by a relative error of at most 0.015.
The reference program's roundings to bfloat16 on the way count: a program that leaves them out, or rounds other values in their place, can miss the bound.
Values may be sent and summed in bfloat16 or wider, within the bound.
No kernel may reach another device: no remote copies, remote signals or barrier semaphores. Data moves between devices by JAX's collectives and lax.ppermute only.
A program may use at most 256 MiB of HBM per device.

```python
import math
import jax
import jax.numpy as jnp
import numpy as np
from jax import lax

D = 768
HEAD_DIM = 64
FF = 3072
ROW_LEN = 1024
SEGS = 32
MOST = 64
ROWS_DEV = 2
TOKENS = 32768
QUERIES = 1024
N_DP = 16


def place_ends(entries, stream_key, smallest, high):
    longest = entries.shape.index(max(entries.shape))
    spots = []
    for shift in (0, 1):
        where = [jax.random.randint(jax.random.fold_in(stream_key, axis), (), 0, length) for axis, length in enumerate(entries.shape)]
        where[longest] = (where[longest] + shift) % entries.shape[longest]
        spots.append(tuple(where))
    return entries.at[spots[0]].set(smallest).at[spots[1]].set(high)


def block_scale(stream_key, dims, shards, low, top_value):
    gain = 1.0
    for dim, shards_of in shards:
        steps = jax.random.uniform(jax.random.fold_in(jax.random.fold_in(stream_key, 6), dim), (shards_of,), jnp.float32, low / len(shards), top_value / len(shards))
        gain = gain * jnp.repeat(jnp.exp(steps), dims[dim] // shards_of).reshape((-1,) + (1,) * (len(dims) - 1 - dim))
    return gain


def profile(amount, total, limit, slope):
    portions = [(1 << 20) // math.isqrt(rank ** slope) + 1 for rank in range(2, amount + 1)]
    spare, counts = total - limit - (amount - 1), [1] * (amount - 1)
    while spare > 0:
        free = [i for i in range(amount - 1) if counts[i] < limit]
        whole, left = sum([portions[i] for i in free]), spare
        for i in free:
            more = min(limit - counts[i], max(1, left * portions[i] // whole), spare)
            counts[i] = counts[i] + more
            spare = spare - more
    return np.array([limit] + counts)


def ragged_sizes(stream_key, amount, total, most, slope):
    if amount == 2:
        one = jax.random.randint(stream_key, (), max(1, total - most), min(most, total - 1) + 1)
        return jnp.stack([one, total - one])
    sizes = jnp.asarray(profile(amount, total, most, slope), jnp.int32)
    twos = (amount - 1) // 2
    donor, taker = sizes[1:1 + 2 * twos:2], sizes[2:2 + 2 * twos:2]
    margin = jnp.minimum(donor - 1, most - taker)
    shifted = jax.random.randint(jax.random.fold_in(stream_key, 1), (twos,), 0, 1 << 20) % (margin + 1)
    sizes = sizes.at[1:1 + 2 * twos:2].set(donor - shifted).at[2:2 + 2 * twos:2].set(taker + shifted)
    return sizes[jax.random.permutation(jax.random.fold_in(stream_key, 2), amount)]


def bell_draw(stream_key, shape, width, bound, split=(), kind=jnp.bfloat16):
    drawn = width * jax.random.normal(stream_key, shape, jnp.float32)
    if split:
        drawn = drawn * block_scale(stream_key, shape, split, -0.22, 0.18)
    return jnp.clip(drawn, -bound, bound).astype(kind)


def setup_inputs(seed: int = 0) -> dict:
    key_of = jax.random.split(jax.random.key(seed), 19)
    hidden_in = bell_draw(key_of[0], (2, TOKENS, D), 1.0, 4.0, ((0, 2), (1, 16)))
    segment_ids = jax.vmap(lambda own: jnp.searchsorted(jnp.cumsum(ragged_sizes(own, SEGS, ROW_LEN, MOST, 2)), jnp.arange(ROW_LEN), side="right"))(jax.random.split(key_of[1], 2 * (ROWS_DEV * N_DP))).reshape((2, ROWS_DEV * N_DP, ROW_LEN)).astype(jnp.int32)
    positives = place_ends(jax.random.randint(key_of[2], (QUERIES,), 0, QUERIES), jax.random.fold_in(key_of[2], 1), 0, QUERIES - 1).astype(jnp.int32)
    w_query = bell_draw(key_of[3], (D, D), D ** -0.5, 0.21875)
    b_query = bell_draw(key_of[4], (D,), 0.5, 3.0)
    w_key = bell_draw(key_of[5], (D, D), D ** -0.5, 0.21875)
    w_value = bell_draw(key_of[6], (D, D), D ** -0.5, 0.21875)
    b_value = bell_draw(key_of[7], (D,), 0.5, 3.0)
    w_out = bell_draw(key_of[8], (D, D), (D // 16) ** -0.5, 0.875)
    b_out = bell_draw(key_of[9], (D,), 0.5, 3.0)
    gain_attn = jnp.clip(1.0 + 0.15 * jax.random.normal(key_of[10], (D,), jnp.float32), 0.25, 1.75).astype(jnp.bfloat16)
    shift_attn = bell_draw(key_of[11], (D,), 0.2, 1.0)
    w_in = bell_draw(key_of[12], (D, FF), D ** -0.5, 0.21875)
    b_in = bell_draw(key_of[13], (FF,), 0.5, 3.0)
    w_back = bell_draw(key_of[14], (FF, D), FF ** -0.5, 0.109375)
    b_back = bell_draw(key_of[15], (D,), 0.5, 3.0)
    gain_ffn = jnp.clip(1.0 + 0.15 * jax.random.normal(key_of[16], (D,), jnp.float32), 0.25, 1.75).astype(jnp.bfloat16)
    shift_ffn = bell_draw(key_of[17], (D,), 0.2, 1.0)
    return dict(hidden_in=hidden_in, segment_ids=segment_ids, positives=positives, w_query=w_query, b_query=b_query, w_key=w_key, w_value=w_value, b_value=b_value, w_out=w_out, b_out=b_out, gain_attn=gain_attn, shift_attn=shift_attn, w_in=w_in, b_in=b_in, w_back=w_back, b_back=b_back, gain_ffn=gain_ffn, shift_ffn=shift_ffn)


@jax.custom_vjp
def low(v):
    return lax.optimization_barrier(v.astype(jnp.bfloat16)).astype(jnp.float32)

@jax.custom_vjp
def low_back(v):
    return v

def low_keep(v):
    return (low(v), None)

def low_pass(kept, grad):
    return (grad,)

def back_keep(v):
    return (v, None)

def back_low(kept, grad):
    return (low(grad),)
low.defvjp(low_keep, low_pass)
low_back.defvjp(back_keep, back_low)

def layer_norm(values, gain_in, shift_in):
    average = lax.optimization_barrier(jnp.mean(values, axis=-1, keepdims=True))
    centered = values - average
    spread = lax.optimization_barrier(jnp.mean(centered * centered, axis=-1, keepdims=True))
    return centered * lax.rsqrt(spread + 1e-12) * gain_in + shift_in

def gelu_exact(values):
    return jax.nn.gelu(values, approximate=False)

def row_layer(params, row_x, row_seg):
    w_query, b_query, w_key, w_value, b_value, w_out, b_out, gain_attn, shift_attn, w_in, b_in, w_back, b_back, gain_ffn, shift_ffn = params
    highest = lax.Precision.HIGHEST
    length = row_x.shape[0]
    feature_dim = row_x.shape[1]
    head_count = feature_dim // HEAD_DIM
    query_x = low_back(low(jnp.dot(row_x, w_query, precision=highest) + b_query))
    key_x = low_back(low(jnp.dot(row_x, w_key, precision=highest)))
    value_x = low_back(low(jnp.dot(row_x, w_value, precision=highest) + b_value))
    query_h = query_x.reshape(length, head_count, HEAD_DIM)
    key_h = key_x.reshape(length, head_count, HEAD_DIM)
    value_h = value_x.reshape(length, head_count, HEAD_DIM)
    logits = jnp.einsum('qhd,khd->hqk', query_h, key_h, precision=highest) * HEAD_DIM ** (-0.5)
    logits = low_back(logits)
    same_seg = row_seg[:, None] == row_seg[None, :]
    logits = jnp.where(same_seg[None], logits, -1000000000.0)
    attn_probs = jax.nn.softmax(logits, axis=-1)
    context = jnp.einsum('hqk,khd->qhd', low(attn_probs), value_h, precision=highest).reshape(length, feature_dim)
    context = low_back(low(context))
    attended = low_back(jnp.dot(context, w_out, precision=highest) + b_out)
    normed = low(layer_norm(row_x + attended, gain_attn, shift_attn))
    up_proj = low_back(jnp.dot(normed, w_in, precision=highest) + b_in)
    active = low(gelu_exact(up_proj))
    down_proj = low_back(jnp.dot(active, w_back, precision=highest) + b_back)
    return low(layer_norm(normed + down_proj, gain_ffn, shift_ffn))

def forward(hidden, params, segment_ids, positives):
    highest = lax.Precision.HIGHEST
    feature_dim = hidden.shape[2]
    rows_x = hidden.reshape(-1, ROW_LEN, feature_dim)
    rows_seg = segment_ids.reshape(-1, ROW_LEN)
    row_fn = jax.checkpoint(row_layer)
    encoded = lax.map(lambda row_item: row_fn(params, row_item[0], row_item[1]), (rows_x, rows_seg))
    flat_rows = encoded.reshape(-1, feature_dim)
    seg_ids = jnp.arange(SEGS, dtype=jnp.int32)
    starts = lax.optimization_barrier(jnp.sum((rows_seg[:, None, :] < seg_ids[None, :, None]).astype(jnp.int32), axis=2))
    places = (jnp.arange(rows_seg.shape[0], dtype=jnp.int32)[:, None] * ROW_LEN + starts).reshape(-1)
    cls_rows = jnp.take(flat_rows, places, axis=0)
    half_count = cls_rows.shape[0] // 2
    queries = cls_rows[:half_count]
    passages = cls_rows[half_count:]
    scores = low_back(jnp.dot(queries, passages.T, precision=highest) * feature_dim ** (-0.5))
    log_sum = jax.nn.logsumexp(scores, axis=1)
    picked = jnp.take_along_axis(scores, positives[:, None].astype(jnp.int32), axis=1)[:, 0]
    return (encoded.reshape(hidden.shape), scores, log_sum - picked)

def reference(hidden_in, segment_ids, positives, w_query, b_query, w_key, w_value, b_value, w_out, b_out, gain_attn, shift_attn, w_in, b_in, w_back, b_back, gain_ffn, shift_ffn):
    params = tuple((param.astype(jnp.float32) for param in (w_query, b_query, w_key, w_value, b_value, w_out, b_out, gain_attn, shift_attn, w_in, b_in, w_back, b_back, gain_ffn, shift_ffn)))
    hidden = hidden_in.astype(jnp.float32)
    outputs, pullback = jax.vjp(lambda hidden_x, param_list: forward(hidden_x, param_list, segment_ids, positives), hidden, params)
    encoded, scores, losses = outputs
    grad_hidden, grad_list = pullback((jnp.zeros_like(encoded), jnp.zeros_like(scores), jnp.ones_like(losses)))
    return (encoded.astype(jnp.bfloat16), scores, losses, grad_hidden, grad_list[0], grad_list[1], grad_list[2], grad_list[3], grad_list[4], grad_list[5], grad_list[6], grad_list[7], grad_list[8], grad_list[9], grad_list[10], grad_list[11], grad_list[12], grad_list[13], grad_list[14])
```

```python
import functools

import jax
import jax.numpy as jnp
from jax import lax
from jax.experimental import pallas as pl
from jax.experimental.pallas import tpu as pltpu
from jax.sharding import PartitionSpec as P

HEAD_DIM = 64
SEGS = 32
GROUP = 4
FAR = float(2**30)
VMEM_BYTES = 60 * 1024 * 1024
F32 = jnp.float32
BF16 = jnp.bfloat16


def moved(value, axis, mask):
    pairs = [(source, source ^ mask) for source in range(lax.axis_size(axis))]
    return lax.ppermute(value, axis, pairs)


def dot_nn(a, b):
    return lax.dot_general(a, b, (((1,), (0,)), ((), ())), preferred_element_type=F32)


def dot_nt(a, b):
    return lax.dot_general(a, b, (((1,), (1,)), ((), ())), preferred_element_type=F32)


def dot_tn(a, b):
    return lax.dot_general(a, b, (((0,), (0,)), ((), ())), preferred_element_type=F32)


def iota(shape, dim):
    return lax.broadcasted_iota(jnp.int32, shape, dim)


def row_of(ref):
    return ref[...].astype(F32).reshape(1, -1)


def norm_parts(values):
    average = jnp.mean(values, axis=-1, keepdims=True)
    centered = values - average
    spread = jnp.mean(centered * centered, axis=-1, keepdims=True)
    inverse = lax.rsqrt(spread + 1e-12)
    return centered * inverse, inverse


def layer_norm(values, gain, shift):
    scaled, _ = norm_parts(values)
    return scaled * gain + shift


def layer_norm_back(values, gain, grad):
    scaled, inverse = norm_parts(values)
    inner = grad * gain
    mean_inner = jnp.mean(inner, axis=-1, keepdims=True)
    mean_scaled = jnp.mean(inner * scaled, axis=-1, keepdims=True)
    back = inverse * (inner - mean_inner - scaled * mean_scaled)
    return back, jnp.sum(grad * scaled, axis=0, keepdims=True), jnp.sum(grad, axis=0, keepdims=True)


def phi_of(values):
    return 0.5 * (1.0 + lax.erf(values * (2.0**-0.5)))


def gelu_exact(values):
    return values * phi_of(values)


def gelu_slope(values):
    bell = jnp.exp(-0.5 * values * values) * 0.3989422804014327
    return phi_of(values) + values * bell


def block_heads(rows, head_count, segs, feature_dim):
    tiled = jnp.concatenate([rows] * head_count, axis=0)
    shape = (head_count * segs, feature_dim)
    inside = jnp.floor(iota(shape, 0).astype(F32) * (1.0 / segs)) == jnp.floor(
        iota(shape, 1).astype(F32) * (1.0 / HEAD_DIM)
    )
    return jnp.where(inside, tiled.astype(F32), 0.0), inside


def heads_to_rows(wide, inside, head_count, segs):
    kept = jnp.where(inside, wide, 0.0)
    total = kept[:segs]
    for head in range(1, head_count):
        total = total + kept[head * segs : (head + 1) * segs]
    return total


def cls_onehot(seg_row, segs):
    shape = (segs, seg_row.shape[1])
    before = (seg_row < iota(shape, 0)).astype(F32)
    starts = jnp.sum(before, axis=1, keepdims=True).astype(jnp.int32)
    return iota(shape, 1) == starts


def cls_probs(query_wide, key_row, seg_row, head_count, segs):
    logits = dot_nt(query_wide, key_row) * (HEAD_DIM**-0.5)
    member = jnp.where(seg_row == iota((segs, seg_row.shape[1]), 0), 1.0, 0.0)
    member = jnp.concatenate([member] * head_count, axis=0)
    logits = jnp.where(member > 0.5, logits, -1000000000.0)
    top = jnp.max(logits, axis=1, keepdims=True)
    exponent = jnp.exp(logits - top)
    return exponent / jnp.sum(exponent, axis=1, keepdims=True)


def front_kernel(
    x_ref, seg_ref, wq, bq, wk, wv, bv, wo, bo, ga, sa, w_in_hbm, b_in, w_back_hbm, bb, gf, sf,
    k_out, v_out, pack_out, qc_out, pre_attn_out, up_out, pre_ffn_out, enc_out,
    ctx_s, xc_s, w_in_v, w_back_v, sems,
):
    feature_dim = x_ref.shape[2]
    ff_dim = w_in_v.shape[1]
    head_count = feature_dim // HEAD_DIM
    step = pl.program_id(0)
    copy_in = pltpu.make_async_copy(w_in_hbm, w_in_v, sems.at[0])
    copy_back = pltpu.make_async_copy(w_back_hbm, w_back_v, sems.at[1])

    @pl.when(step == 0)
    def _():
        copy_in.start()
        copy_back.start()

    x = x_ref[0]
    key_row = dot_nn(x, wk[...]).astype(BF16)
    k_out[0] = key_row
    value_row = (dot_nn(x, wv[...]) + row_of(bv)).astype(BF16)
    v_out[0] = value_row
    seg_row = seg_ref[0]
    first = cls_onehot(seg_row, SEGS).astype(F32).astype(BF16)
    x_cls = dot_nn(first, x).astype(BF16)
    query_cls = (dot_nn(x_cls, wq[...]) + row_of(bq)).astype(BF16)
    query_wide, inside = block_heads(query_cls, head_count, SEGS, feature_dim)
    probs = cls_probs(query_wide.astype(BF16), key_row, seg_row, head_count, SEGS)
    context = heads_to_rows(dot_nn(probs.astype(BF16), value_row), inside, head_count, SEGS)
    here = pl.ds(pl.multiple_of(step * SEGS, SEGS), SEGS)
    ctx_s[here, :] = context.astype(BF16)
    xc_s[here, :] = x_cls
    qc_out[here, :] = query_cls

    @pl.when(step == pl.num_programs(0) - 1)
    def _():
        copy_in.wait()
        copy_back.wait()
        context_all = ctx_s[...]
        x_all = xc_s[...]
        pre_attn = x_all.astype(F32) + (dot_nn(context_all, wo[...]) + row_of(bo))
        pre_attn_out[...] = pre_attn
        normed = layer_norm(pre_attn, row_of(ga), row_of(sa)).astype(BF16)
        up = dot_nn(normed, w_in_v[...]) + row_of(b_in)
        up_out[...] = up
        active = gelu_exact(up).astype(BF16)
        pre_ffn = normed.astype(F32) + (dot_nn(active, w_back_v[...]) + row_of(bb))
        pre_ffn_out[...] = pre_ffn
        enc_out[...] = layer_norm(pre_ffn, row_of(gf), row_of(sf)).astype(BF16)
        pack_out[:, :ff_dim] = active
        pack_out[:, ff_dim : ff_dim + feature_dim] = normed
        pack_out[:, ff_dim + feature_dim : ff_dim + 2 * feature_dim] = context_all
        pack_out[:, ff_dim + 2 * feature_dim :] = x_all


def full(shape):
    zeros = (0,) * len(shape)
    return pl.BlockSpec(shape, lambda *_: zeros)


ANY = pl.BlockSpec(memory_space=pl.ANY)


def front(x_rows, seg_rows, wq, bq, wk, wv, bv, wo, bo, ga, sa, w_in, b_in, w_back, bb, gf, sf):
    rows, length, feature_dim = x_rows.shape
    ff_dim = w_in.shape[1]
    cls = rows * SEGS
    row_block = pl.BlockSpec((1, length, feature_dim), lambda i: (i, 0, 0))
    seg_block = pl.BlockSpec((1, 1, length), lambda i: (i, 0, 0))
    shapes = (
        ((rows, length, feature_dim), BF16),
        ((rows, length, feature_dim), BF16),
        ((cls, ff_dim + 3 * feature_dim), BF16),
        ((cls, feature_dim), BF16),
        ((cls, feature_dim), F32),
        ((cls, ff_dim), F32),
        ((cls, feature_dim), F32),
        ((cls, feature_dim), BF16),
    )
    rest = (wq, bq, wk, wv, bv, wo, bo, ga, sa)
    tail = (bb, gf, sf)
    return pl.pallas_call(
        front_kernel,
        grid=(rows,),
        in_specs=[row_block, seg_block]
        + [full(a.shape) for a in rest]
        + [ANY, full(b_in.shape), ANY]
        + [full(a.shape) for a in tail],
        out_specs=[row_block, row_block] + [full(s) for s, _ in shapes[2:]],
        out_shape=[jax.ShapeDtypeStruct(s, d) for s, d in shapes],
        scratch_shapes=[
            pltpu.VMEM((cls, feature_dim), BF16),
            pltpu.VMEM((cls, feature_dim), BF16),
            pltpu.VMEM(w_in.shape, BF16),
            pltpu.VMEM(w_back.shape, BF16),
            pltpu.SemaphoreType.DMA((2,)),
        ],
        compiler_params=pltpu.CompilerParams(vmem_limit_bytes=VMEM_BYTES),
        cost_estimate=pl.CostEstimate(
            flops=2 * rows * length * feature_dim * feature_dim * 3,
            bytes_accessed=30_000_000,
            transcendentals=rows * length * 384,
        ),
        name="front",
    )(x_rows, seg_rows, *rest, w_in, b_in, w_back, *tail)


def full_kernel(
    x_ref, k_ref, v_ref, hot_ref, wq, bq, wo, bo, ga, sa, w_in, b_in, w_back, bb, gf, sf, *outs
):
    enc_out = outs[-1]
    block, feature_dim = x_ref.shape[1], x_ref.shape[2]
    length = k_ref.shape[1]
    ff_dim = w_in.shape[1]
    part, window = 128, 256
    step = pl.program_id(0)
    x = x_ref[0]
    query = ((dot_nn(x, wq[...]) + row_of(bq)).astype(BF16) * (HEAD_DIM**-0.5)).astype(BF16)
    left = iota((part, 128), 1) < HEAD_DIM
    contexts = []
    for sub in range(block // part):
        base = step * block + sub * part
        start = pl.multiple_of(jnp.clip(base - 64, 0, length - window), 64)
        keys = k_ref[0, pl.ds(start, window), :]
        values = v_ref[0, pl.ds(start, window), :]
        hot_keys = hot_ref[0, pl.ds(start, window), :]
        apart = ((hot_keys.astype(F32) - 1.0) * FAR).astype(BF16)
        hot_query = hot_ref[0, pl.ds(pl.multiple_of(base, part), part), :]
        pieces = []
        for pair in range(feature_dim // 128):
            lanes = slice(pair * 128, pair * 128 + 128)
            both = query[sub * part : (sub + 1) * part, lanes]
            zero = jnp.zeros_like(both)
            wide = jnp.concatenate(
                [
                    jnp.concatenate([jnp.where(left, both, zero), hot_query], axis=1),
                    jnp.concatenate([jnp.where(left, zero, both), hot_query], axis=1),
                ],
                axis=0,
            )
            logits = dot_nt(wide, jnp.concatenate([keys[:, lanes], apart], axis=1))
            top = jnp.max(logits, axis=1, keepdims=True)
            exponent = jnp.exp(logits - top)
            total = jnp.sum(exponent, axis=1, keepdims=True)
            probs = (exponent * (1.0 / total)).astype(BF16)
            out = dot_nn(probs, values[:, lanes])
            pieces.append(jnp.where(left, out[:part], out[part:]).astype(BF16))
        contexts.append(jnp.concatenate(pieces, axis=1))
    context = jnp.concatenate(contexts, axis=0)
    pre_attn = x.astype(F32) + (dot_nn(context, wo[...]) + row_of(bo))
    normed = layer_norm(pre_attn, row_of(ga), row_of(sa)).astype(BF16)
    bias_in = row_of(b_in)
    total = normed.astype(F32) + row_of(bb)
    chunk = 768
    for first in range(0, ff_dim, chunk):
        cols = slice(first, first + chunk)
        up = dot_nn(normed, w_in[:, cols]) + bias_in[:, cols]
        total = total + dot_nn(gelu_exact(up).astype(BF16), w_back[cols, :])
    enc_out[0] = layer_norm(total, row_of(gf), row_of(sf)).astype(BF16)


def full_row(row, x_rows, keys, values, hot, params, before):
    rows, length, feature_dim = x_rows.shape
    block = 256
    tile = pl.BlockSpec((1, block, feature_dim), lambda i: (row, i, 0))
    whole_row = pl.BlockSpec((1, length, feature_dim), lambda i: (row, 0, 0))
    hot_row = pl.BlockSpec((1, length, hot.shape[2]), lambda i: (row, 0, 0))
    extra = [] if before is None else [before]
    ff_dim = params[6].shape[1]
    return pl.pallas_call(
        full_kernel,
        grid=(length // block,),
        in_specs=[tile, whole_row, whole_row, hot_row]
        + [full(a.shape) for a in params]
        + [ANY for _ in extra],
        out_specs=tile,
        out_shape=jax.ShapeDtypeStruct((rows, length, feature_dim), BF16),
        input_output_aliases={} if before is None else {4 + len(params): 0},
        compiler_params=pltpu.CompilerParams(vmem_limit_bytes=VMEM_BYTES),
        cost_estimate=pl.CostEstimate(
            flops=2 * length * feature_dim * (2 * feature_dim + 2 * ff_dim) + 4 * length * 2048 * 1024,
            bytes_accessed=25_000_000,
            transcendentals=length * (ff_dim + 3072),
        ),
        name="encode_row",
    )(x_rows, keys, values, hot, *params, *extra)


def middle_kernel(
    idx_ref, *refs
):
    own = refs[:GROUP]
    other = refs[GROUP : 2 * GROUP]
    (
        positives, pack, pre_attn_ref, up_ref, pre_ffn_ref, w_back_hbm, w_in_hbm, wo, ga, gf,
        scores_out, losses_out, late_out, gctx_out, gpa_out, vec_out,
        both, w_in_v, w_back_v, sems, wsems,
    ) = refs[2 * GROUP :]
    tower, place = idx_ref[0], idx_ref[1]
    far, cls, feature_dim = own[0].shape
    ff_dim = w_in_v.shape[1]
    copy_back = pltpu.make_async_copy(w_back_hbm, w_back_v, wsems.at[0])
    copy_in = pltpu.make_async_copy(w_in_hbm, w_in_v, wsems.at[1])
    copies = []
    for side, group in ((tower, own), (1 - tower, other)):
        for near in range(GROUP):
            for slot in range(far):
                to = both.at[side, place ^ (slot * GROUP + near)]
                copies.append(
                    pltpu.make_async_copy(group[near].at[slot], to, sems.at[len(copies)])
                )
    for copy in copies:
        copy.start()
    copy_back.start()
    copy_in.start()
    for copy in copies:
        copy.wait()
    count = far * GROUP * cls
    scale = feature_dim**-0.5
    queries = both[0].reshape(count, feature_dim)
    positive_row = positives[...]
    block = min(count, max(64, (1 << 20) // count))

    def partial_of(first):
        passages = both[1, pl.ds(first // cls, block // cls)].reshape(block, feature_dim)
        scored = dot_nt(passages, queries) * scale
        top = jnp.max(scored, axis=0, keepdims=True)
        total = jnp.sum(jnp.exp(scored - top), axis=0, keepdims=True)
        hit = iota((block, count), 0) + first == positive_row
        return top, total, jnp.sum(jnp.where(hit, scored, 0.0), axis=0, keepdims=True)

    def joined(index, state):
        top, total, picked = partial_of(index * block)
        joint = jnp.maximum(state[0], top)
        return (
            joint,
            state[1] * jnp.exp(state[0] - joint) + total * jnp.exp(top - joint),
            state[2] + picked,
        )

    state = partial_of(0)
    if count // block > 1:
        state = lax.fori_loop(1, count // block, joined, state)
    row_log = state[0] + jnp.log(state[1])
    losses_out[...] = row_log - state[2]
    scores_out[...] = dot_nt(both[1, place], queries) * scale
    mine = both[tower, place]
    opposite = both[1 - tower].reshape(count, feature_dim)
    own_scores = dot_nt(mine, opposite) * scale
    own_top = jnp.max(own_scores, axis=1, keepdims=True)
    own_log = own_top + jnp.log(jnp.sum(jnp.exp(own_scores - own_top), axis=1, keepdims=True))
    lanes = iota((cls, count), 1)
    mine_index = iota((cls, count), 0) + place * cls
    spread_positive = jnp.broadcast_to(positive_row, (cls, count))
    own_positive = jnp.sum(
        jnp.where(lanes == mine_index, spread_positive.astype(F32), 0.0), axis=1, keepdims=True
    ).astype(jnp.int32)
    is_query = tower == 0
    log_used = jnp.where(is_query, jnp.broadcast_to(own_log, (cls, count)), row_log)
    hit_query = (lanes == own_positive).astype(F32)
    hit_passage = (spread_positive == mine_index).astype(F32)
    hit = jnp.where(is_query, hit_query, hit_passage)
    grad_scores = (jnp.exp(own_scores - log_used) - hit).astype(BF16)
    grad_cls = dot_nn(grad_scores, opposite) * scale
    grad_pre_ffn, grad_gf, grad_sf = layer_norm_back(pre_ffn_ref[...], row_of(gf), grad_cls)
    vec_out[0:1, :] = grad_gf
    vec_out[1:2, :] = grad_sf
    grad_down = grad_pre_ffn.astype(BF16)
    vec_out[2:3, :] = jnp.sum(grad_down.astype(F32), axis=0, keepdims=True)
    copy_back.wait()
    grad_up = (dot_nt(grad_down, w_back_v[...]) * gelu_slope(up_ref[...])).astype(BF16)
    late_out[:, :ff_dim] = grad_up
    late_out[:, ff_dim : ff_dim + feature_dim] = grad_down
    bias_up = jnp.sum(grad_up.astype(F32), axis=0, keepdims=True)
    for piece in range(ff_dim // feature_dim):
        vec_out[6 + piece : 7 + piece, :] = bias_up[:, piece * feature_dim : (piece + 1) * feature_dim]
    copy_in.wait()
    grad_normed = grad_pre_ffn + dot_nt(grad_up, w_in_v[...])
    grad_pre_attn, grad_ga, grad_sa = layer_norm_back(pre_attn_ref[...], row_of(ga), grad_normed)
    vec_out[3:4, :] = grad_ga
    vec_out[4:5, :] = grad_sa
    gpa_out[...] = grad_pre_attn
    grad_attended = grad_pre_attn.astype(BF16)
    late_out[:, ff_dim + feature_dim :] = grad_attended
    vec_out[5:6, :] = jnp.sum(grad_attended.astype(F32), axis=0, keepdims=True)
    gctx_out[...] = dot_nt(grad_attended, wo[...]).astype(BF16)


def middle(idx, own, other, positives, pack, pre_attn, up, pre_ffn, w_back, w_in, wo, ga, gf):
    far, cls, feature_dim = own[0].shape
    ff_dim = w_in.shape[1]
    places = far * GROUP
    count = places * cls
    shapes = (
        ((cls, count), F32),
        ((1, count), F32),
        ((cls, ff_dim + 2 * feature_dim), BF16),
        ((cls, feature_dim), BF16),
        ((cls, feature_dim), F32),
        ((6 + ff_dim // feature_dim, feature_dim), F32),
    )
    smalls = (positives, pack, pre_attn, up, pre_ffn)
    lasts = (wo, ga, gf)
    return pl.pallas_call(
        middle_kernel,
        in_specs=[pl.BlockSpec(memory_space=pltpu.SMEM)]
        + [ANY] * (2 * GROUP)
        + [full(a.shape) for a in smalls]
        + [ANY, ANY]
        + [full(a.shape) for a in lasts],
        out_specs=[full(s) for s, _ in shapes],
        out_shape=[jax.ShapeDtypeStruct(s, d) for s, d in shapes],
        grid=(1,),
        scratch_shapes=[
            pltpu.VMEM((2, places, cls, feature_dim), BF16),
            pltpu.VMEM(w_in.shape, BF16),
            pltpu.VMEM(w_back.shape, BF16),
            pltpu.SemaphoreType.DMA((2 * places,)),
            pltpu.SemaphoreType.DMA((2,)),
        ],
        compiler_params=pltpu.CompilerParams(vmem_limit_bytes=VMEM_BYTES),
        cost_estimate=pl.CostEstimate(
            flops=2 * count * count * feature_dim, bytes_accessed=20_000_000, transcendentals=count * count
        ),
        name="loss",
    )(idx, *own, *other, *smalls, w_back, w_in, *lasts)


def spread_rows(shape, sizes, strides, masks):
    rest = iota(shape, 0)
    total = jnp.zeros(shape, jnp.int32)
    for size, stride, mask in zip(reversed(sizes), reversed(strides), reversed(masks)):
        above = jnp.floor((rest.astype(F32) + 0.5) * (1.0 / size)).astype(jnp.int32)
        digit = rest - above * size
        total = total + (digit ^ mask) * stride
        rest = above
    return total


def attn_back_kernel(
    idx_ref, x_ref, seg_ref, k_ref, v_ref, qc_ref, gctx_ref, gpa_ref, wq, wk, wv,
    back_out, send_out, keep_out, vec_out,
    acc_k, acc_v, gq_s, xc_s,
):
    step = pl.program_id(0)
    tower, place = idx_ref[0], idx_ref[1]
    towers, places = 2, idx_ref[2]
    feature_dim = x_ref.shape[2]
    head_count = feature_dim // HEAD_DIM
    x = x_ref[0]
    key_row, value_row, seg_row = k_ref[0], v_ref[0], seg_ref[0]
    here = pl.ds(pl.multiple_of(step * SEGS, SEGS), SEGS)
    first = cls_onehot(seg_row, SEGS).astype(F32).astype(BF16)
    x_cls = dot_nn(first, x).astype(BF16)
    query_wide, inside = block_heads(qc_ref[here, :], head_count, SEGS, feature_dim)
    query_wide = query_wide.astype(BF16)
    gctx_wide, _ = block_heads(gctx_ref[here, :], head_count, SEGS, feature_dim)
    gctx_wide = gctx_wide.astype(BF16)
    probs = cls_probs(query_wide, key_row, seg_row, head_count, SEGS)
    grad_probs = dot_nt(gctx_wide, value_row)
    inner = jnp.sum(probs * grad_probs, axis=1, keepdims=True)
    grad_logits = (probs * (grad_probs - inner)).astype(BF16)
    scale = HEAD_DIM**-0.5
    grad_query = heads_to_rows(dot_nn(grad_logits, key_row), inside, head_count, SEGS)
    grad_query = (grad_query * scale).astype(BF16)
    gq_s[here, :] = grad_query
    xc_s[here, :] = x_cls
    grad_key = (dot_tn(grad_logits, query_wide) * scale).astype(BF16)
    grad_value = dot_tn(probs.astype(BF16), gctx_wide).astype(BF16)
    shape = (feature_dim, feature_dim)
    far = feature_dim // (towers * GROUP * keep_out.shape[3])
    block = keep_out.shape[3]
    source = spread_rows(
        shape,
        (towers, GROUP, far, block),
        (far * GROUP * block, block, GROUP * block, 1),
        (tower, place & (GROUP - 1), place // GROUP, 0),
    )
    order = (iota(shape, 1) == source).astype(F32).astype(BF16)
    x_turned = dot_nt(order, x).astype(BF16)
    part_k = dot_nn(x_turned, grad_key)
    part_v = dot_nn(x_turned, grad_value)
    bias_v = jnp.sum(grad_value.astype(F32), axis=0, keepdims=True)
    bias_q = jnp.sum(grad_query.astype(F32), axis=0, keepdims=True)

    @pl.when(step == 0)
    def _():
        acc_k[...] = part_k
        acc_v[...] = part_v
        vec_out[0:1, :] = bias_q
        vec_out[1:2, :] = bias_v

    @pl.when(step > 0)
    def _():
        acc_k[...] += part_k
        acc_v[...] += part_v
        vec_out[0:1, :] += bias_q
        vec_out[1:2, :] += bias_v

    cls_back = gpa_ref[here, :] + dot_nt(grad_query, wq[...])
    high = cls_back.astype(BF16)
    rest = cls_back - high.astype(F32)
    middle_part = rest.astype(BF16)
    low = (rest - middle_part.astype(F32)).astype(BF16)
    back = dot_nt(grad_key, wk[...]) + dot_nt(grad_value, wv[...])
    back_out[0] = back + (dot_tn(first, high) + (dot_tn(first, middle_part) + dot_tn(first, low)))

    @pl.when(step == pl.num_programs(0) - 1)
    def _():
        xc_turned = dot_nt(order, xc_s[...]).astype(BF16)
        grads = (dot_nn(xc_turned, gq_s[...]), acc_k[...], acc_v[...])
        half = feature_dim // towers
        for which in range(3):
            keep_out[which] = grads[which][:half].reshape(keep_out.shape[1:])
            send_out[which] = grads[which][half:].astype(BF16).reshape(send_out.shape[1:])


def attn_back(idx, x_rows, seg_rows, keys, values, qc, gctx, gpa, wq, wk, wv, places):
    rows, length, feature_dim = x_rows.shape
    cls = rows * SEGS
    block = feature_dim // (2 * places)
    row_block = pl.BlockSpec((1, length, feature_dim), lambda i: (i, 0, 0))
    seg_block = pl.BlockSpec((1, 1, length), lambda i: (i, 0, 0))
    half = (3, GROUP, places // GROUP, block, feature_dim)
    shapes = (
        ((rows, length, feature_dim), F32),
        (half, BF16),
        (half, F32),
        ((2, feature_dim), F32),
    )
    consts = (qc, gctx, gpa, wq, wk, wv)
    return pl.pallas_call(
        attn_back_kernel,
        grid=(rows,),
        in_specs=[pl.BlockSpec(memory_space=pltpu.SMEM), row_block, seg_block, row_block, row_block]
        + [full(a.shape) for a in consts],
        out_specs=[row_block] + [full(s) for s, _ in shapes[1:]],
        out_shape=[jax.ShapeDtypeStruct(s, d) for s, d in shapes],
        scratch_shapes=[
            pltpu.VMEM((feature_dim, feature_dim), F32),
            pltpu.VMEM((feature_dim, feature_dim), F32),
            pltpu.VMEM((cls, feature_dim), BF16),
            pltpu.VMEM((cls, feature_dim), BF16),
        ],
        compiler_params=pltpu.CompilerParams(vmem_limit_bytes=VMEM_BYTES),
        cost_estimate=pl.CostEstimate(
            flops=2 * rows * length * feature_dim * feature_dim * 8,
            bytes_accessed=30_000_000,
            transcendentals=rows * length * 384,
        ),
        name="attention_back",
    )(idx, x_rows, seg_rows, keys, values, *consts)


def weights_kernel(idx_ref, *refs):
    early = refs[: 2 * GROUP]
    late = refs[2 * GROUP : 4 * GROUP]
    in_out, back_out, out_out = refs[4 * GROUP :]
    tower, place = idx_ref[0], idx_ref[1]
    far, block_ff = back_out.shape[0], back_out.shape[1]
    block = in_out.shape[1]
    feature_dim = back_out.shape[2]
    ff_dim = in_out.shape[2]

    def pick(rows_of, width):
        shape = (far * rows_of, width)
        source = spread_rows(
            shape, (far, rows_of), (GROUP * rows_of, 1), (place // GROUP, 0)
        )
        source = source + (tower * far * GROUP + (place & (GROUP - 1))) * rows_of
        return (iota(shape, 1) == source).astype(F32).astype(BF16)

    def stacked(parts, first, width):
        return jnp.concatenate([ref[:, first : first + width] for ref in parts], axis=0)

    narrow, wide = pick(block, feature_dim), pick(block_ff, ff_dim)
    grad_up = stacked(late, 0, ff_dim)
    grad_down = stacked(late, ff_dim, feature_dim)
    grad_attended = stacked(late, ff_dim + feature_dim, feature_dim)
    active = dot_nt(wide, stacked(early, 0, ff_dim)).astype(BF16)
    normed = dot_nt(narrow, stacked(early, ff_dim, feature_dim)).astype(BF16)
    context = dot_nt(narrow, stacked(early, ff_dim + feature_dim, feature_dim)).astype(BF16)
    back_out[...] = dot_nn(active, grad_down).reshape(back_out.shape)
    in_out[...] = dot_nn(normed, grad_up).reshape(in_out.shape)
    out_out[...] = dot_nn(context, grad_attended).reshape(out_out.shape)


def weights(idx, early, late, places, feature_dim, ff_dim):
    far = places // GROUP
    block, block_ff = feature_dim // (2 * places), ff_dim // (2 * places)
    shapes = ((far, block, ff_dim), (far, block_ff, feature_dim), (far, block, feature_dim))
    return pl.pallas_call(
        weights_kernel,
        grid=(1,),
        in_specs=[pl.BlockSpec(memory_space=pltpu.SMEM)] + [full(a.shape) for a in (*early, *late)],
        out_specs=[full(s) for s in shapes],
        out_shape=[jax.ShapeDtypeStruct(s, F32) for s in shapes],
        compiler_params=pltpu.CompilerParams(vmem_limit_bytes=VMEM_BYTES),
        cost_estimate=pl.CostEstimate(
            flops=4 * 512 * 384 * (ff_dim + feature_dim), bytes_accessed=14_000_000, transcendentals=0
        ),
        name="weight_grads",
    )(idx, *early, *late)


def far_sum(value):
    far = value.shape[0]
    arrived = [moved(value[m].astype(BF16), "dp", GROUP * m) for m in range(1, far)]
    total = value[0]
    for part in arrived:
        total = total + part.astype(F32)
    return total


def on_device(
    hidden_in, segment_ids, positives, w_query, b_query, w_key, w_value, b_value, w_out, b_out,
    gain_attn, shift_attn, w_in, b_in, w_back, b_back, gain_ffn, shift_ffn,
):
    feature_dim = hidden_in.shape[2]
    ff_dim = w_in.shape[1]
    rows, length = segment_ids.shape[1], segment_ids.shape[2]
    places = lax.axis_size("dp")
    far = places // GROUP
    tower, place = lax.axis_index("tower"), lax.axis_index("dp")
    idx = jnp.stack([tower, place, places]).astype(jnp.int32)
    x_rows = hidden_in.reshape(rows, length, feature_dim)
    seg_rows = segment_ids.reshape(rows, 1, length)
    keys, values, pack, query_cls, pre_attn, up, pre_ffn, enc_cls = front(
        x_rows, seg_rows, w_query, b_query, w_key, w_value, b_value, w_out, b_out, gain_attn,
        shift_attn, w_in, b_in, w_back, b_back, gain_ffn, shift_ffn,
    )
    along = [enc_cls] + [moved(enc_cls, "dp", GROUP * m) for m in range(1, far)]
    own = [jnp.stack(along)]
    own = own + [moved(own[0], "dp", m) for m in range(1, GROUP)]
    other = [moved(quad, "tower", 1) for quad in own]
    hot = (segment_ids[0][:, :, None] == jnp.arange(128, dtype=jnp.int32)).astype(BF16)
    params = (
        w_query, b_query, w_out, b_out, gain_attn, shift_attn, w_in, b_in, w_back, b_back,
        gain_ffn, shift_ffn,
    )
    encoded = None
    for row in range(rows):
        encoded = full_row(row, x_rows, keys, values, hot, params, encoded)
    early = [pack[:, : ff_dim + 2 * feature_dim]]
    early = early + [moved(early[0], "dp", m) for m in range(1, GROUP)]
    early = early + [moved(part, "tower", 1) for part in early]
    scores, losses, late_own, gctx, gpa, vec_mid = middle(
        idx, own, other, positives.reshape(1, -1), pack, pre_attn, up, pre_ffn, w_back, w_in,
        w_out, gain_attn, gain_ffn,
    )
    late = [late_own] + [moved(late_own, "dp", m) for m in range(1, GROUP)]
    late = late + [moved(part, "tower", 1) for part in late]
    back, send, keep, vec_back = attn_back(
        idx, x_rows, seg_rows, keys, values, query_cls, gctx, gpa, w_query, w_key, w_value, places
    )
    grad_in, grad_back, grad_out = weights(idx, early, late, places, feature_dim, ff_dim)
    grad_in, grad_back, grad_out = far_sum(grad_in), far_sum(grad_back), far_sum(grad_out)
    paired = keep + moved(send, "tower", 1).astype(F32)
    near = paired[:, 0]
    for m in range(1, GROUP):
        near = near + moved(paired[:, m].astype(BF16), "dp", m).astype(F32)
    grad_qkv = far_sum(jnp.transpose(near, (1, 0, 2, 3)))
    block, block_ff = feature_dim // (2 * places), ff_dim // (2 * places)
    devices = 2 * places
    small = jnp.concatenate([vec_back, vec_mid[:6]], axis=0).reshape(8, devices, block)
    small = jnp.transpose(small, (1, 0, 2)).reshape(devices, 8 * block)
    small = jnp.concatenate([small, vec_mid[6:].reshape(devices, block_ff)], axis=1)
    small = lax.all_to_all(small, ("tower", "dp"), 0, 0, tiled=False)
    small = jnp.sum(small, axis=0)
    pieces = [small[i * block : (i + 1) * block] for i in range(8)]
    b_q, b_v, g_f, s_f, b_b, g_a, s_a, b_o = pieces
    return (
        encoded.reshape(hidden_in.shape),
        scores.T,
        losses.reshape(-1),
        back.reshape(hidden_in.shape),
        grad_qkv[0],
        b_q,
        grad_qkv[1],
        grad_qkv[2],
        b_v,
        grad_out,
        b_o,
        g_a,
        s_a,
        grad_in,
        small[8 * block :],
        grad_back,
        b_b,
        g_f,
        s_f,
    )


def solution(mesh):
    placed = (P("tower", "dp", None), P("tower", "dp", None)) + (P(),) * 16
    matrix, vector = P(("tower", "dp"), None), P(("tower", "dp"))
    return jax.shard_map(
        on_device,
        mesh=mesh,
        in_specs=placed,
        out_specs=(
            P("tower", "dp", None),
            P(None, "dp"),
            P(),
            P("tower", "dp", None),
            matrix,
            vector,
            matrix,
            matrix,
            vector,
            matrix,
            vector,
            vector,
            vector,
            matrix,
            vector,
            matrix,
            vector,
            vector,
            vector,
        ),
        check_vma=False,
    )
```

```python
import functools

import jax
import jax.numpy as jnp
from jax import lax
from jax.experimental import pallas as pl
from jax.experimental.pallas import tpu as pltpu
from jax.sharding import PartitionSpec as P

HEAD_DIM = 64
SEGS = 32
GROUP = 4
LANES = 128
FAR = float(2**30)
VMEM_BYTES = 60 * 1024 * 1024
F32 = jnp.float32
BF16 = jnp.bfloat16


def moved(value, axis, mask):
    pairs = [(source, source ^ mask) for source in range(lax.axis_size(axis))]
    return lax.ppermute(value, axis, pairs)


def dot_nn(a, b):
    return lax.dot_general(a, b, (((1,), (0,)), ((), ())), preferred_element_type=F32)


def dot_nt(a, b):
    return lax.dot_general(a, b, (((1,), (1,)), ((), ())), preferred_element_type=F32)


def dot_tn(a, b):
    return lax.dot_general(a, b, (((0,), (0,)), ((), ())), preferred_element_type=F32)


def iota(shape, dim):
    return lax.broadcasted_iota(jnp.int32, shape, dim)


def row_of(ref):
    return ref[...].astype(F32).reshape(1, -1)


def norm_parts(values):
    average = jnp.mean(values, axis=-1, keepdims=True)
    centered = values - average
    spread = jnp.mean(centered * centered, axis=-1, keepdims=True)
    inverse = lax.rsqrt(spread + 1e-12)
    return centered * inverse, inverse


def layer_norm(values, gain, shift):
    scaled, _ = norm_parts(values)
    return scaled * gain + shift


def layer_norm_back(values, gain, grad):
    scaled, inverse = norm_parts(values)
    inner = grad * gain
    mean_inner = jnp.mean(inner, axis=-1, keepdims=True)
    mean_scaled = jnp.mean(inner * scaled, axis=-1, keepdims=True)
    back = inverse * (inner - mean_inner - scaled * mean_scaled)
    return back, jnp.sum(grad * scaled, axis=0, keepdims=True), jnp.sum(grad, axis=0, keepdims=True)


def phi_of(values):
    return 0.5 * (1.0 + lax.erf(values * (2.0**-0.5)))


def gelu_exact(values):
    return values * phi_of(values)


def gelu_slope(values):
    bell = jnp.exp(-0.5 * values * values) * 0.3989422804014327
    return phi_of(values) + values * bell


def head_mask(head_count, segs, feature_dim):
    head_row = iota((head_count * segs, 1), 0) >> (segs.bit_length() - 1)
    head_col = iota((1, feature_dim), 1) >> (HEAD_DIM.bit_length() - 1)
    return jnp.where(head_row == head_col, 1.0, 0.0)


def block_heads(rows, mask, head_count):
    return jnp.concatenate([rows] * head_count, axis=0) * mask.astype(BF16)


def heads_to_rows(wide, mask, head_count, segs):
    kept = wide * mask
    total = kept[:segs]
    for head in range(1, head_count):
        total = total + kept[head * segs : (head + 1) * segs]
    return total


def cls_onehot(seg_row, segs):
    shape = (segs, seg_row.shape[1])
    before = (seg_row < iota(shape, 0)).astype(F32)
    starts = jnp.sum(before, axis=1, keepdims=True).astype(jnp.int32)
    return iota(shape, 1) == starts


def cls_probs(query_wide, key_row, seg_row, head_count, segs):
    logits = dot_nt(query_wide, key_row) * (HEAD_DIM**-0.5)
    member = jnp.where(seg_row == iota((segs, seg_row.shape[1]), 0), 1.0, 0.0)
    member = jnp.concatenate([member] * head_count, axis=0)
    logits = jnp.where(member > 0.5, logits, -1000000000.0)
    top = jnp.max(logits, axis=1, keepdims=True)
    exponent = jnp.exp(logits - top)
    return exponent * (1.0 / jnp.sum(exponent, axis=1, keepdims=True))


def front_kernel(
    idx_ref, x_ref, seg_ref, wq, bq, wk, wv, bv, wo, bo, ga, sa, w_in_hbm, b_in, w_back_hbm, bb, gf, sf,
    k_out, v_out, pack_0, pack_1, pack_2, pack_3, qc_out, pre_attn_out, up_out, pre_ffn_out, enc_out,
    ctx_s, xc_s, w_in_v, w_back_v, sems,
):
    feature_dim = x_ref.shape[2]
    ff_dim = w_in_v.shape[1]
    head_count = feature_dim // HEAD_DIM
    step = pl.program_id(0)
    copy_in = pltpu.make_async_copy(w_in_hbm, w_in_v, sems.at[0])
    copy_back = pltpu.make_async_copy(w_back_hbm, w_back_v, sems.at[1])

    @pl.when(step == 0)
    def _():
        copy_in.start()
        copy_back.start()

    x = x_ref[0]
    key_row = dot_nn(x, wk[...]).astype(BF16)
    k_out[0] = key_row
    value_row = (dot_nn(x, wv[...]) + row_of(bv)).astype(BF16)
    v_out[0] = value_row
    seg_row = seg_ref[0]
    first = cls_onehot(seg_row, SEGS).astype(F32).astype(BF16)
    x_cls = dot_nn(first, x).astype(BF16)
    query_cls = (dot_nn(x_cls, wq[...]) + row_of(bq)).astype(BF16)
    mask = head_mask(head_count, SEGS, feature_dim)
    query_wide = block_heads(query_cls, mask, head_count)
    probs = cls_probs(query_wide, key_row, seg_row, head_count, SEGS)
    context = heads_to_rows(dot_nn(probs.astype(BF16), value_row), mask, head_count, SEGS)
    here = pl.ds(pl.multiple_of(step * SEGS, SEGS), SEGS)
    ctx_s[here, :] = context.astype(BF16)
    xc_s[here, :] = x_cls
    qc_out[here, :] = query_cls

    @pl.when(step == pl.num_programs(0) - 1)
    def _():
        copy_in.wait()
        copy_back.wait()
        context_all = ctx_s[...]
        x_all = xc_s[...]
        pre_attn = x_all.astype(F32) + (dot_nn(context_all, wo[...]) + row_of(bo))
        pre_attn_out[...] = pre_attn
        normed = layer_norm(pre_attn, row_of(ga), row_of(sa)).astype(BF16)
        up = dot_nn(normed, w_in_v[...]) + row_of(b_in)
        up_out[...] = up
        active = gelu_exact(up).astype(BF16)
        pre_ffn = normed.astype(F32) + (dot_nn(active, w_back_v[...]) + row_of(bb))
        pre_ffn_out[...] = pre_ffn
        enc_out[...] = layer_norm(pre_ffn, row_of(gf), row_of(sf)).astype(BF16)
        packs = (pack_0, pack_1, pack_2, pack_3)
        fill = pack_0.shape[1] - 2 * feature_dim
        group = ff_dim * LANES // fill
        size = group // GROUP
        if fill == ff_dim:
            for near in range(GROUP):
                packs[near][:, :ff_dim] = active
        else:
            for slot in range(fill // LANES):
                blocks = [
                    active[:, slot * group + size * b : slot * group + size * (b + 1)]
                    for b in range(GROUP)
                ]
                lanes = slot * LANES
                for near in range(GROUP):
                    source = (idx_ref[1] & (GROUP - 1)) ^ near
                    chosen = blocks[0]
                    for b in range(1, GROUP):
                        chosen = jnp.where(source == b, blocks[b], chosen)
                    packs[near][:, lanes : lanes + size] = chosen
                    packs[near][:, lanes + size : lanes + LANES] = jnp.zeros(
                        (active.shape[0], LANES - size), BF16
                    )
        for near in range(GROUP):
            packs[near][:, fill : fill + feature_dim] = normed
            packs[near][:, fill + feature_dim :] = context_all


def full(shape):
    zeros = (0,) * len(shape)
    return pl.BlockSpec(shape, lambda *_: zeros)


ANY = pl.BlockSpec(memory_space=pl.ANY)


def active_width(places, ff_dim):
    group = GROUP * ff_dim // (2 * places)
    return ff_dim // group * LANES if group % LANES == 0 else ff_dim


def front(places, idx, x_rows, seg_rows, wq, bq, wk, wv, bv, wo, bo, ga, sa, w_in, b_in, w_back, bb, gf, sf):
    rows, length, feature_dim = x_rows.shape
    ff_dim = w_in.shape[1]
    cls = rows * SEGS
    row_block = pl.BlockSpec((1, length, feature_dim), lambda i: (i, 0, 0))
    seg_block = pl.BlockSpec((1, 1, length), lambda i: (i, 0, 0))
    shapes = (
        ((rows, length, feature_dim), BF16),
        ((rows, length, feature_dim), BF16),
        *(((cls, active_width(places, ff_dim) + 2 * feature_dim), BF16),) * GROUP,
        ((cls, feature_dim), BF16),
        ((cls, feature_dim), F32),
        ((cls, ff_dim), F32),
        ((cls, feature_dim), F32),
        ((cls, feature_dim), BF16),
    )
    rest = (wq, bq, wk, wv, bv, wo, bo, ga, sa)
    tail = (bb, gf, sf)
    return pl.pallas_call(
        front_kernel,
        grid=(rows,),
        in_specs=[pl.BlockSpec(memory_space=pltpu.SMEM), row_block, seg_block]
        + [full(a.shape) for a in rest]
        + [ANY, full(b_in.shape), ANY]
        + [full(a.shape) for a in tail],
        out_specs=[row_block, row_block] + [full(s) for s, _ in shapes[2:]],
        out_shape=[jax.ShapeDtypeStruct(s, d) for s, d in shapes],
        scratch_shapes=[
            pltpu.VMEM((cls, feature_dim), BF16),
            pltpu.VMEM((cls, feature_dim), BF16),
            pltpu.VMEM(w_in.shape, BF16),
            pltpu.VMEM(w_back.shape, BF16),
            pltpu.SemaphoreType.DMA((2,)),
        ],
        compiler_params=pltpu.CompilerParams(vmem_limit_bytes=VMEM_BYTES),
        cost_estimate=pl.CostEstimate(
            flops=2 * rows * length * feature_dim * feature_dim * 3,
            bytes_accessed=30_000_000,
            transcendentals=rows * length * 384,
        ),
        name="front",
    )(idx, x_rows, seg_rows, *rest, w_in, b_in, w_back, *tail)


def loads(pairs, sems):
    copies = [
        pltpu.make_async_copy(source, target, sems.at[index])
        for index, (source, target) in enumerate(pairs)
    ]
    for copy in copies:
        copy.start()
    return lambda index: copies[index].wait()


def encode_kernel_at(
    row, first, x_hbm, k_hbm, v_hbm, hot_hbm, wq_hbm, wo_hbm, w_in_hbm, w_back_hbm,
    bq, bo, ga, sa, b_in, bb, gf, sf, *refs
):
    enc_out, x_s, k_s, v_s, hot_s, wq, wo, w_in, w_back, sems = refs[-10:]
    tokens, feature_dim = x_s.shape
    held = k_s.shape[0]
    length = k_hbm.shape[1]
    ff_dim = w_in.shape[1]
    part, window = 128, 256
    low = max(0, min(first - 64, length - held))
    near = pl.ds(low, held)
    half = ff_dim // 2
    wait = loads(
        [
            (x_hbm.at[row, pl.ds(first, tokens)], x_s),
            (wq_hbm, wq),
            (hot_hbm.at[row, near], hot_s),
            (k_hbm.at[row, near], k_s),
            (v_hbm.at[row, near], v_s),
            (wo_hbm, wo),
            (w_in_hbm, w_in),
            (w_back_hbm, w_back),
        ],
        sems,
    )
    wait(0)
    wait(1)
    x = x_s[...]
    query = ((dot_nn(x, wq[...]) + row_of(bq)).astype(BF16) * (HEAD_DIM**-0.5)).astype(BF16)
    left = iota((part, 128), 1) < HEAD_DIM
    wait(2)
    wait(3)
    wait(4)
    contexts = []
    for sub in range(tokens // part):
        base = first + sub * part
        start = max(0, min(base - 64, length - window)) - low
        keys = k_s[start : start + window, :]
        values = v_s[start : start + window, :]
        apart = ((hot_s[start : start + window, :].astype(F32) - 1.0) * FAR).astype(BF16)
        hot_query = hot_s[base - low : base - low + part, :]
        pieces = []
        for pair in range(feature_dim // 128):
            lanes = slice(pair * 128, pair * 128 + 128)
            both = query[sub * part : (sub + 1) * part, lanes]
            zero = jnp.zeros_like(both)
            wide = jnp.concatenate(
                [
                    jnp.concatenate([jnp.where(left, both, zero), hot_query], axis=1),
                    jnp.concatenate([jnp.where(left, zero, both), hot_query], axis=1),
                ],
                axis=0,
            )
            logits = dot_nt(wide, jnp.concatenate([keys[:, lanes], apart], axis=1))
            top = jnp.max(logits, axis=1, keepdims=True)
            exponent = jnp.exp(logits - top)
            total = jnp.sum(exponent, axis=1, keepdims=True)
            probs = (exponent * (1.0 / total)).astype(BF16)
            out = dot_nn(probs, values[:, lanes])
            pieces.append(jnp.where(left, out[:part], out[part:]).astype(BF16))
        contexts.append(jnp.concatenate(pieces, axis=1))
    context = jnp.concatenate(contexts, axis=0)
    wait(5)
    pre_attn = x.astype(F32) + (dot_nn(context, wo[...]) + row_of(bo))
    normed = layer_norm(pre_attn, row_of(ga), row_of(sa)).astype(BF16)
    wait(6)
    wait(7)
    bias_in = row_of(b_in)
    total = normed.astype(F32) + row_of(bb)
    chunk = 768
    for start in range(0, ff_dim, chunk):
        cols = slice(start, start + chunk)
        up = dot_nn(normed, w_in[:, cols]) + bias_in[:, cols]
        total = total + dot_nn(gelu_exact(up).astype(BF16), w_back[cols, :])
    enc_out[0] = layer_norm(total, row_of(gf), row_of(sf)).astype(BF16)


def encode_part(part, parts, x_rows, keys, values, hot, mats, smalls, before):
    rows, length, feature_dim = x_rows.shape
    per_row = parts // rows
    row, tokens = part // per_row, length // per_row
    first = (part % per_row) * tokens
    held = min(length, tokens + 128)
    place = part % per_row
    extra = [] if before is None else [before]
    return pl.pallas_call(
        functools.partial(encode_kernel_at, row, first),
        grid=(1,),
        in_specs=[ANY] * (4 + len(mats)) + [full(a.shape) for a in smalls] + [ANY for _ in extra],
        out_specs=pl.BlockSpec((1, tokens, feature_dim), lambda i: (row, place, 0)),
        out_shape=jax.ShapeDtypeStruct((rows, length, feature_dim), BF16),
        input_output_aliases={} if before is None else {4 + len(mats) + len(smalls): 0},
        scratch_shapes=[
            pltpu.VMEM((tokens, feature_dim), BF16),
            pltpu.VMEM((held, feature_dim), BF16),
            pltpu.VMEM((held, feature_dim), BF16),
            pltpu.VMEM((held, hot.shape[2]), BF16),
        ]
        + [pltpu.VMEM(a.shape, BF16) for a in mats]
        + [pltpu.SemaphoreType.DMA((8,))],
        compiler_params=pltpu.CompilerParams(vmem_limit_bytes=VMEM_BYTES),
        cost_estimate=pl.CostEstimate(
            flops=tokens * feature_dim * feature_dim, bytes_accessed=1_000_000, transcendentals=0
        ),
        name="encode_part",
    )(x_rows, keys, values, hot, *mats, *smalls, *extra)


def middle_kernel(
    idx_ref, *refs
):
    own = refs[:GROUP]
    other = refs[GROUP : 2 * GROUP]
    (
        positives, pre_attn_ref, up_ref, pre_ffn_ref, w_back_hbm, w_in_hbm, wo, ga, gf,
        scores_out, losses_out, late_out, gctx_out, gpa_out, vec_out,
        both, w_in_v, w_back_v, sems, wsems,
    ) = refs[2 * GROUP :]
    tower, place = idx_ref[0], idx_ref[1]
    far, cls, feature_dim = own[0].shape
    ff_dim = w_in_v.shape[1]
    copy_back = pltpu.make_async_copy(w_back_hbm, w_back_v, wsems.at[0])
    copy_in = pltpu.make_async_copy(w_in_hbm, w_in_v, wsems.at[1])
    copies = []
    for side, group in ((tower, own), (1 - tower, other)):
        for near in range(GROUP):
            for slot in range(far):
                to = both.at[side, place ^ (slot * GROUP + near)]
                copies.append(
                    pltpu.make_async_copy(group[near].at[slot], to, sems.at[len(copies)])
                )
    for copy in copies:
        copy.start()
    copy_back.start()
    copy_in.start()
    for copy in copies:
        copy.wait()
    count = far * GROUP * cls
    scale = feature_dim**-0.5
    queries = both[0].reshape(count, feature_dim)
    positive_row = positives[...]
    block = min(count, max(64, (1 << 20) // count))

    def partial_of(first):
        passages = both[1, pl.ds(first // cls, block // cls)].reshape(block, feature_dim)
        scored = dot_nt(passages, queries) * scale
        top = jnp.max(scored, axis=0, keepdims=True)
        total = jnp.sum(jnp.exp(scored - top), axis=0, keepdims=True)
        hit = iota((block, count), 0) + first == positive_row
        return top, total, jnp.sum(jnp.where(hit, scored, 0.0), axis=0, keepdims=True)

    def joined(index, state):
        top, total, picked = partial_of(index * block)
        joint = jnp.maximum(state[0], top)
        return (
            joint,
            state[1] * jnp.exp(state[0] - joint) + total * jnp.exp(top - joint),
            state[2] + picked,
        )

    state = partial_of(0)
    if count // block > 1:
        state = lax.fori_loop(1, count // block, joined, state)
    row_log = state[0] + jnp.log(state[1])
    losses_out[...] = row_log - state[2]
    scores_out[...] = dot_nt(both[1, place], queries) * scale
    mine = both[tower, place]
    opposite = both[1 - tower].reshape(count, feature_dim)
    own_scores = dot_nt(mine, opposite) * scale
    own_top = jnp.max(own_scores, axis=1, keepdims=True)
    own_log = own_top + jnp.log(jnp.sum(jnp.exp(own_scores - own_top), axis=1, keepdims=True))
    lanes = iota((cls, count), 1)
    mine_index = iota((cls, count), 0) + place * cls
    spread_positive = jnp.broadcast_to(positive_row, (cls, count))
    own_positive = jnp.sum(
        jnp.where(lanes == mine_index, spread_positive.astype(F32), 0.0), axis=1, keepdims=True
    ).astype(jnp.int32)
    is_query = tower == 0
    log_used = jnp.where(is_query, jnp.broadcast_to(own_log, (cls, count)), row_log)
    hit_query = (lanes == own_positive).astype(F32)
    hit_passage = (spread_positive == mine_index).astype(F32)
    hit = jnp.where(is_query, hit_query, hit_passage)
    grad_scores = (jnp.exp(own_scores - log_used) - hit).astype(BF16)
    grad_cls = dot_nn(grad_scores, opposite) * scale
    grad_pre_ffn, grad_gf, grad_sf = layer_norm_back(pre_ffn_ref[...], row_of(gf), grad_cls)
    vec_out[0:1, :] = grad_gf
    vec_out[1:2, :] = grad_sf
    grad_down = grad_pre_ffn.astype(BF16)
    vec_out[2:3, :] = jnp.sum(grad_down.astype(F32), axis=0, keepdims=True)
    copy_back.wait()
    grad_up = (dot_nt(grad_down, w_back_v[...]) * gelu_slope(up_ref[...])).astype(BF16)
    late_out[:, :ff_dim] = grad_up
    late_out[:, ff_dim : ff_dim + feature_dim] = grad_down
    copy_in.wait()
    grad_normed = grad_pre_ffn + dot_nt(grad_up, w_in_v[...])
    grad_pre_attn, grad_ga, grad_sa = layer_norm_back(pre_attn_ref[...], row_of(ga), grad_normed)
    vec_out[3:4, :] = grad_ga
    vec_out[4:5, :] = grad_sa
    gpa_out[...] = grad_pre_attn
    grad_attended = grad_pre_attn.astype(BF16)
    late_out[:, ff_dim + feature_dim :] = grad_attended
    vec_out[5:6, :] = jnp.sum(grad_attended.astype(F32), axis=0, keepdims=True)
    gctx_out[...] = dot_nt(grad_attended, wo[...]).astype(BF16)


def middle(idx, own, other, positives, pre_attn, up, pre_ffn, w_back, w_in, wo, ga, gf):
    far, cls, feature_dim = own[0].shape
    ff_dim = w_in.shape[1]
    places = far * GROUP
    count = places * cls
    shapes = (
        ((cls, count), F32),
        ((1, count), F32),
        ((cls, ff_dim + 2 * feature_dim), BF16),
        ((cls, feature_dim), BF16),
        ((cls, feature_dim), F32),
        ((8, feature_dim), F32),
    )
    smalls = (positives, pre_attn, up, pre_ffn)
    lasts = (wo, ga, gf)
    return pl.pallas_call(
        middle_kernel,
        in_specs=[pl.BlockSpec(memory_space=pltpu.SMEM)]
        + [ANY] * (2 * GROUP)
        + [full(a.shape) for a in smalls]
        + [ANY, ANY]
        + [full(a.shape) for a in lasts],
        out_specs=[full(s) for s, _ in shapes],
        out_shape=[jax.ShapeDtypeStruct(s, d) for s, d in shapes],
        grid=(1,),
        scratch_shapes=[
            pltpu.VMEM((2, places, cls, feature_dim), BF16),
            pltpu.VMEM(w_in.shape, BF16),
            pltpu.VMEM(w_back.shape, BF16),
            pltpu.SemaphoreType.DMA((2 * places,)),
            pltpu.SemaphoreType.DMA((2,)),
        ],
        compiler_params=pltpu.CompilerParams(vmem_limit_bytes=VMEM_BYTES),
        cost_estimate=pl.CostEstimate(
            flops=2 * count * count * feature_dim, bytes_accessed=20_000_000, transcendentals=count * count
        ),
        name="loss",
    )(idx, *own, *other, *smalls, w_back, w_in, *lasts)


def spread_rows(shape, sizes, strides, masks):
    rest = iota(shape, 0)
    total = jnp.zeros(shape, jnp.int32)
    for size, stride, mask in zip(reversed(sizes), reversed(strides), reversed(masks)):
        above = jnp.floor((rest.astype(F32) + 0.5) * (1.0 / size)).astype(jnp.int32)
        digit = rest - above * size
        total = total + (digit ^ mask) * stride
        rest = above
    return total


def attn_back_kernel(
    idx_ref, x_ref, seg_ref, k_ref, v_ref, qc_ref, gctx_ref, vec_ref,
    gk_out, gv_out, gq_s, send_out, keep_out,
    acc_k, acc_v, xc_s, vec_s,
):
    step = pl.program_id(0)
    tower, place = idx_ref[0], idx_ref[1]
    towers, places = 2, idx_ref[2]
    feature_dim = x_ref.shape[2]
    head_count = feature_dim // HEAD_DIM
    x = x_ref[0]
    key_row, value_row, seg_row = k_ref[0], v_ref[0], seg_ref[0]
    here = pl.ds(pl.multiple_of(step * SEGS, SEGS), SEGS)
    first = cls_onehot(seg_row, SEGS).astype(F32).astype(BF16)
    x_cls = dot_nn(first, x).astype(BF16)
    mask = head_mask(head_count, SEGS, feature_dim)
    query_wide = block_heads(qc_ref[here, :], mask, head_count)
    gctx_wide = block_heads(gctx_ref[here, :], mask, head_count)
    probs = cls_probs(query_wide, key_row, seg_row, head_count, SEGS)
    grad_probs = dot_nt(gctx_wide, value_row)
    inner = jnp.sum(probs * grad_probs, axis=1, keepdims=True)
    grad_logits = (probs * (grad_probs - inner)).astype(BF16)
    scale = HEAD_DIM**-0.5
    grad_query = heads_to_rows(dot_nn(grad_logits, key_row), mask, head_count, SEGS)
    grad_query = (grad_query * scale).astype(BF16)
    gq_s[here, :] = grad_query
    xc_s[here, :] = x_cls
    grad_key = (dot_tn(grad_logits, query_wide) * scale).astype(BF16)
    grad_value = dot_tn(probs.astype(BF16), gctx_wide).astype(BF16)
    shape = (feature_dim, feature_dim)
    far, block = keep_out.shape[1:3]
    source = spread_rows(
        (feature_dim, 1),
        (towers, GROUP, far, block),
        (far * GROUP * block, block, GROUP * block, 1),
        (tower, place & (GROUP - 1), place // GROUP, 0),
    )
    order = (iota(shape, 1) == source).astype(F32).astype(BF16)
    x_turned = dot_nt(order, x).astype(BF16)
    part_k = dot_nn(x_turned, grad_key)
    part_v = dot_nn(x_turned, grad_value)
    bias_v = jnp.sum(grad_value.astype(F32), axis=0, keepdims=True)
    bias_q = jnp.sum(grad_query.astype(F32), axis=0, keepdims=True)

    @pl.when(step == 0)
    def _():
        acc_k[...] = part_k
        acc_v[...] = part_v
        vec_s[...] = jnp.zeros_like(vec_s)
        vec_s[0:6, :] = vec_ref[0:6, :]
        vec_s[6:7, :] = bias_q
        vec_s[7:8, :] = bias_v

    @pl.when(step > 0)
    def _():
        acc_k[...] += part_k
        acc_v[...] += part_v
        vec_s[6:7, :] += bias_q
        vec_s[7:8, :] += bias_v

    gk_out[0] = grad_key
    gv_out[0] = grad_value

    @pl.when(step == pl.num_programs(0) - 1)
    def _():
        xc_turned = dot_nt(order, xc_s[...]).astype(BF16)
        vectors = vec_s[...]
        high = vectors.astype(BF16)
        rest = vectors - high.astype(F32)
        second = rest.astype(BF16)
        third = (rest - second.astype(F32)).astype(BF16)
        columns = dot_nt(order, high) + (dot_nt(order, second) + dot_nt(order, third))
        grads = (dot_nn(xc_turned, gq_s[...]), acc_k[...], acc_v[...], columns)
        half = feature_dim // towers
        place_at = 0
        for grad in grads:
            lanes = slice(place_at, place_at + grad.shape[1])
            shape = (GROUP, far, block, grad.shape[1])
            keep_out[:, :, :, lanes] = grad[:half].astype(BF16).reshape(shape)
            send_out[:, :, :, lanes] = grad[half:].astype(BF16).reshape(shape)
            place_at = lanes.stop


def attn_back(idx, x_rows, seg_rows, keys, values, qc, gctx, vectors, places):
    rows, length, feature_dim = x_rows.shape
    cls = rows * SEGS
    block = feature_dim // (2 * places)
    row_block = pl.BlockSpec((1, length, feature_dim), lambda i: (i, 0, 0))
    seg_block = pl.BlockSpec((1, 1, length), lambda i: (i, 0, 0))
    half = (GROUP, places // GROUP, block, 3 * feature_dim + LANES)
    shapes = (
        ((rows, length, feature_dim), BF16),
        ((rows, length, feature_dim), BF16),
        ((cls, feature_dim), BF16),
        (half, BF16),
        (half, BF16),
    )
    consts = (qc, gctx, vectors)
    return pl.pallas_call(
        attn_back_kernel,
        grid=(rows,),
        in_specs=[pl.BlockSpec(memory_space=pltpu.SMEM), row_block, seg_block, row_block, row_block]
        + [full(a.shape) for a in consts],
        out_specs=[row_block, row_block] + [full(s) for s, _ in shapes[2:]],
        out_shape=[jax.ShapeDtypeStruct(s, d) for s, d in shapes],
        scratch_shapes=[
            pltpu.VMEM((feature_dim, feature_dim), F32),
            pltpu.VMEM((feature_dim, feature_dim), F32),
            pltpu.VMEM((cls, feature_dim), BF16),
            pltpu.VMEM((LANES, feature_dim), F32),
        ],
        compiler_params=pltpu.CompilerParams(vmem_limit_bytes=VMEM_BYTES),
        cost_estimate=pl.CostEstimate(
            flops=2 * rows * length * feature_dim * feature_dim * 6,
            bytes_accessed=30_000_000,
            transcendentals=rows * length * 384,
        ),
        name="attention_back",
    )(idx, x_rows, seg_rows, keys, values, *consts)


def hidden_kernel(seg_ref, gk_ref, gv_ref, gq_ref, gpa_ref, wq, wk, wv, back_out, parts_s):
    row, step = pl.program_id(0), pl.program_id(1)
    block = gk_ref.shape[1]
    here = pl.ds(pl.multiple_of(row * SEGS, SEGS), SEGS)

    @pl.when(step == 0)
    def _():
        cls_back = gpa_ref[here, :] + dot_nt(gq_ref[here, :], wq[...])
        high = cls_back.astype(BF16)
        rest = cls_back - high.astype(F32)
        middle_part = rest.astype(BF16)
        parts_s[:SEGS, :] = high
        parts_s[SEGS : 2 * SEGS, :] = middle_part
        parts_s[2 * SEGS :, :] = (rest - middle_part.astype(F32)).astype(BF16)

    before = jnp.where(seg_ref[0] < iota((SEGS, seg_ref.shape[2]), 0), 1.0, 0.0)
    starts = jnp.sum(before, axis=1, keepdims=True).astype(jnp.int32) - step * block
    first = jnp.where(iota((SEGS, block), 1) == starts, 1.0, 0.0).astype(BF16)
    first = jnp.concatenate([first] * 3, axis=0)
    back = dot_nt(gk_ref[0], wk[...]) + dot_nt(gv_ref[0], wv[...])
    back_out[0] = back + dot_tn(first, parts_s[...])


def hidden_back(seg_rows, gk, gv, gq, gpa, wq, wk, wv):
    rows, length, feature_dim = gk.shape
    block = 256
    tile = pl.BlockSpec((1, block, feature_dim), lambda i, j: (i, j, 0))
    seg_block = pl.BlockSpec((1, 1, length), lambda i, j: (i, 0, 0))
    consts = (gq, gpa, wq, wk, wv)
    return pl.pallas_call(
        hidden_kernel,
        grid=(rows, length // block),
        in_specs=[seg_block, tile, tile] + [full(a.shape) for a in consts],
        out_specs=tile,
        out_shape=jax.ShapeDtypeStruct(gk.shape, F32),
        scratch_shapes=[pltpu.VMEM((3 * SEGS, feature_dim), BF16)],
        compiler_params=pltpu.CompilerParams(vmem_limit_bytes=VMEM_BYTES),
        cost_estimate=pl.CostEstimate(
            flops=2 * rows * length * feature_dim * feature_dim * 2,
            bytes_accessed=18_000_000,
            transcendentals=0,
        ),
        name="hidden_back",
    )(seg_rows, gk, gv, *consts)


def weights_kernel(feature_dim, ff_dim, idx_ref, *refs):
    early = refs[:GROUP]
    late = refs[GROUP : 2 * GROUP]
    keep_out, send_out = refs[2 * GROUP :]
    tower, place = idx_ref[0], idx_ref[1]
    _, pairs, block, _ = send_out.shape
    far = 2 * pairs
    pieces = ff_dim // feature_dim
    fill = early[0].shape[1] - 2 * feature_dim

    def pick(group, near, columns):
        source = spread_rows(
            (2 * far * block, 1),
            (2, 2, pairs, block),
            (far * group, group, 2 * group, 1),
            (tower, place // GROUP & 1, place // (2 * GROUP), 0),
        )
        shape = (2 * far * block, columns)
        return jnp.where(iota(shape, 1) == source + near, 1.0, 0.0).astype(BF16)

    def stacked(parts, first, columns):
        return jnp.concatenate([ref[:, first : first + columns] for ref in parts], axis=0)

    def put(first, grad):
        columns = grad.shape[1]
        half = far * block
        shape = (2, pairs, block, columns)
        keep_out[:, :, :, first : first + columns] = grad[:half].astype(BF16).reshape(shape)
        send_out[:, :, :, first : first + columns] = grad[half:].astype(BF16).reshape(shape)

    near = place & (GROUP - 1)
    narrow = pick(GROUP * block, near * block, feature_dim)
    grad_up = stacked(late, 0, ff_dim)
    grad_down = stacked(late, ff_dim, feature_dim)
    grad_attended = stacked(late, ff_dim + feature_dim, feature_dim)
    active = stacked(early, 0, fill)
    normed = dot_nt(narrow, stacked(early, fill, feature_dim)).astype(BF16)
    context = dot_nt(narrow, stacked(early, fill + feature_dim, feature_dim)).astype(BF16)
    put(0, dot_nn(normed, grad_up))
    for piece in range(pieces):
        if fill == ff_dim:
            chosen = pick(GROUP * pieces * block, (near * pieces + piece) * block, fill)
        else:
            chosen = pick(LANES, piece * block, fill)
        turned = dot_nt(chosen, active).astype(BF16)
        put(ff_dim + piece * feature_dim, dot_nn(turned, grad_down))
    put(2 * ff_dim, dot_nn(context, grad_attended))
    bias = jnp.sum(grad_up.astype(F32), axis=0, keepdims=True)
    high = bias.astype(BF16)
    rest = bias - high.astype(F32)
    second = rest.astype(BF16)
    third = (rest - second.astype(F32)).astype(BF16)
    stack = jnp.concatenate([high, second, third, jnp.zeros((LANES - 3, ff_dim), BF16)], axis=0)
    lane = iota((2 * far * block, LANES), 1)
    columns = jnp.zeros((2 * far * block, LANES), F32)
    for piece in range(pieces):
        chosen = pick(GROUP * pieces * block, (near * pieces + piece) * block, ff_dim)
        total = jnp.sum(dot_nt(chosen, stack), axis=1, keepdims=True)
        columns = jnp.where(lane == piece, total, columns)
    put(2 * ff_dim + feature_dim, columns)


def weights(idx, early, late, places, feature_dim, ff_dim):
    far = places // GROUP
    block = feature_dim // (2 * places)
    packed = 2 * ff_dim + feature_dim + LANES
    half = (2, far // 2, block, packed)
    return pl.pallas_call(
        functools.partial(weights_kernel, feature_dim, ff_dim),
        grid=(1,),
        in_specs=[pl.BlockSpec(memory_space=pltpu.SMEM)] + [full(a.shape) for a in (*early, *late)],
        out_specs=[full(half), full(half)],
        out_shape=[jax.ShapeDtypeStruct(half, BF16), jax.ShapeDtypeStruct(half, BF16)],
        compiler_params=pltpu.CompilerParams(vmem_limit_bytes=VMEM_BYTES),
        cost_estimate=pl.CostEstimate(
            flops=4 * 512 * 384 * (ff_dim + feature_dim), bytes_accessed=14_000_000, transcendentals=0
        ),
        name="weight_grads",
    )(idx, *early, *late)


def tied(values, *after):
    return lax.optimization_barrier((values, after))[0]


def on_device(
    hidden_in, segment_ids, positives, w_query, b_query, w_key, w_value, b_value, w_out, b_out,
    gain_attn, shift_attn, w_in, b_in, w_back, b_back, gain_ffn, shift_ffn,
):
    feature_dim = hidden_in.shape[2]
    ff_dim = w_in.shape[1]
    rows, length = segment_ids.shape[1], segment_ids.shape[2]
    places = lax.axis_size("dp")
    far = places // GROUP
    tower, place = lax.axis_index("tower"), lax.axis_index("dp")
    idx = jnp.stack([tower, place, places]).astype(jnp.int32)
    x_rows = hidden_in.reshape(rows, length, feature_dim)
    seg_rows = segment_ids.reshape(rows, 1, length)
    keys, values, *pack, query_cls, pre_attn, up, pre_ffn, enc_cls = front(
        places, idx, x_rows, seg_rows, w_query, b_query, w_key, w_value, b_value, w_out, b_out, gain_attn,
        shift_attn, w_in, b_in, w_back, b_back, gain_ffn, shift_ffn,
    )
    mats = (w_query, w_out, w_in, w_back)
    smalls = (b_query, b_out, gain_attn, shift_attn, b_in, b_back, gain_ffn, shift_ffn)
    hot = (segment_ids[0][:, :, None] == jnp.arange(128, dtype=jnp.int32)).astype(BF16)

    def encode(part, before, *after):
        held = tied(enc_cls if before is None else before, *after) if after else before
        if before is None:
            held = None
        return encode_part(part, 2 * rows, x_rows, keys, values, hot, mats, smalls, held)

    along = [moved(enc_cls, "dp", GROUP * m) for m in range(1, far)]
    early = [pack[0]] + [moved(pack[m], "dp", m) for m in range(1, GROUP)]
    encoded = encode(0, None)
    along, early[1:3] = tied((along, early[1:3]), encoded)
    own = [jnp.stack([enc_cls] + list(along))]
    crossed = [moved(own[0], "dp", m) for m in range(1, GROUP)]
    encoded = encode(1, encoded, own[0])
    own = own + list(tied(crossed, encoded))
    other = [moved(quad, "tower", 1) for quad in own]
    scores, losses, late_own, gctx, gpa, vec_mid = middle(
        idx, own, other, positives.reshape(1, -1), pre_attn, up, pre_ffn, w_back, w_in,
        w_out, gain_attn, gain_ffn,
    )
    late = [late_own] + [moved(late_own, "dp", m) for m in range(1, GROUP)]
    gk, gv, gq, send, keep = attn_back(
        idx, x_rows, seg_rows, keys, values, query_cls, tied(gctx, early), vec_mid, places
    )
    late = list(tied(late, gk))
    weight_keep, weight_send = weights(idx, early, late, places, feature_dim, ff_dim)
    send, weight_send = moved(send, "tower", 1), moved(weight_send, "tower", 1)
    back = hidden_back(seg_rows, gk, gv, tied(gq, weight_keep), gpa, w_query, w_key, w_value)
    send, weight_send = tied((send, weight_send), back)
    weight_sum = weight_keep.astype(F32) + weight_send.astype(F32)
    paired = keep.astype(F32) + send.astype(F32)
    near_sent = [moved(paired[m].astype(BF16), "dp", m) for m in range(1, GROUP)]
    reach, arrived = 1, moved(weight_sum[1].astype(BF16), "dp", GROUP)
    encoded = encode(2, encoded, weight_sum, paired)
    weight_sum = weight_sum[0] + tied(arrived, encoded).astype(F32)
    near_sent = tied(near_sent, encoded)
    near = paired[0]
    for part in near_sent:
        near = near + part.astype(F32)
    far_sent = [moved(near[m].astype(BF16), "dp", GROUP * m) for m in range(1, far)]
    while weight_sum.shape[0] > 1:
        reach = reach * 2
        half = weight_sum.reshape(weight_sum.shape[0] // 2, 2, *weight_sum.shape[1:])
        arrived = moved(half[:, 1].astype(BF16), "dp", GROUP * reach)
        if reach == far // 2:
            encoded = encode(3, encoded, near)
            arrived = tied(arrived, encoded)
        weight_sum = half[:, 0] + arrived.astype(F32)
    weight_sum = weight_sum[0]
    grad_qkv = near[0]
    for part in tied(far_sent, encoded):
        grad_qkv = grad_qkv + part.astype(F32)
    grad_in = weight_sum[:, :ff_dim]
    grad_back = jnp.concatenate(
        [
            weight_sum[:, first : first + feature_dim]
            for first in range(ff_dim, 2 * ff_dim, feature_dim)
        ],
        axis=0,
    )
    grad_out = weight_sum[:, 2 * ff_dim : 2 * ff_dim + feature_dim]
    first = 2 * ff_dim + feature_dim
    b_i = weight_sum[:, first : first + ff_dim // feature_dim].T.reshape(-1)
    columns = grad_qkv[:, 3 * feature_dim : 3 * feature_dim + 8].T
    g_f, s_f, b_b, g_a, s_a, b_o, b_q, b_v = [columns[i] for i in range(8)]
    return (
        encoded.reshape(hidden_in.shape),
        scores.T,
        losses.reshape(-1),
        back.reshape(hidden_in.shape),
        grad_qkv[:, :feature_dim],
        b_q,
        grad_qkv[:, feature_dim : 2 * feature_dim],
        grad_qkv[:, 2 * feature_dim : 3 * feature_dim],
        b_v,
        grad_out,
        b_o,
        g_a,
        s_a,
        grad_in,
        b_i,
        grad_back,
        b_b,
        g_f,
        s_f,
    )


def solution(mesh):
    placed = (P("tower", "dp", None), P("tower", "dp", None)) + (P(),) * 16
    matrix, vector = P(("tower", "dp"), None), P(("tower", "dp"))
    return jax.shard_map(
        on_device,
        mesh=mesh,
        in_specs=placed,
        out_specs=(
            P("tower", "dp", None),
            P(None, "dp"),
            P(),
            P("tower", "dp", None),
            matrix,
            vector,
            matrix,
            matrix,
            vector,
            matrix,
            vector,
            vector,
            vector,
            matrix,
            vector,
            matrix,
            vector,
            vector,
            vector,
        ),
        check_vma=False,
    )
```

```python
import functools

import jax
import jax.numpy as jnp
from jax import lax
from jax.experimental import pallas as pl
from jax.experimental.pallas import tpu as pltpu
from jax.sharding import PartitionSpec as P

HEAD_DIM = 64
SEGS = 32
GROUP = 4
LANES = 128
FAR = float(2**30)
VMEM_BYTES = 60 * 1024 * 1024
F32 = jnp.float32
BF16 = jnp.bfloat16


def moved(value, axis, mask):
    pairs = [(source, source ^ mask) for source in range(lax.axis_size(axis))]
    return lax.ppermute(value, axis, pairs)


def dot_nn(a, b):
    return lax.dot_general(a, b, (((1,), (0,)), ((), ())), preferred_element_type=F32)


def dot_nt(a, b):
    return lax.dot_general(a, b, (((1,), (1,)), ((), ())), preferred_element_type=F32)


def dot_tn(a, b):
    return lax.dot_general(a, b, (((0,), (0,)), ((), ())), preferred_element_type=F32)


def iota(shape, dim):
    return lax.broadcasted_iota(jnp.int32, shape, dim)


def row_of(ref):
    return ref[...].astype(F32).reshape(1, -1)


def norm_parts(values):
    average = jnp.mean(values, axis=-1, keepdims=True)
    centered = values - average
    spread = jnp.mean(centered * centered, axis=-1, keepdims=True)
    inverse = lax.rsqrt(spread + 1e-12)
    return centered * inverse, inverse


def layer_norm(values, gain, shift):
    scaled, _ = norm_parts(values)
    return scaled * gain + shift


def layer_norm_back(values, gain, grad):
    scaled, inverse = norm_parts(values)
    inner = grad * gain
    mean_inner = jnp.mean(inner, axis=-1, keepdims=True)
    mean_scaled = jnp.mean(inner * scaled, axis=-1, keepdims=True)
    back = inverse * (inner - mean_inner - scaled * mean_scaled)
    return back, jnp.sum(grad * scaled, axis=0, keepdims=True), jnp.sum(grad, axis=0, keepdims=True)


def phi_of(values):
    return 0.5 * (1.0 + lax.erf(values * (2.0**-0.5)))


def gelu_exact(values):
    return values * phi_of(values)


def gelu_slope(values):
    bell = jnp.exp(-0.5 * values * values) * 0.3989422804014327
    return phi_of(values) + values * bell


def head_mask(head_count, segs, feature_dim):
    head_row = iota((head_count * segs, 1), 0) >> (segs.bit_length() - 1)
    head_col = iota((1, feature_dim), 1) >> (HEAD_DIM.bit_length() - 1)
    return jnp.where(head_row == head_col, 1.0, 0.0)


def block_heads(rows, mask, head_count):
    return jnp.concatenate([rows] * head_count, axis=0) * mask.astype(BF16)


def heads_to_rows(wide, mask, head_count, segs):
    kept = wide * mask
    total = kept[:segs]
    for head in range(1, head_count):
        total = total + kept[head * segs : (head + 1) * segs]
    return total


def split(values):
    high = values.astype(BF16)
    rest = values - high.astype(F32)
    second = rest.astype(BF16)
    return high, second, (rest - second.astype(F32)).astype(BF16)


def cls_onehot(seg_row, segs):
    shape = (segs, seg_row.shape[1])
    before = (seg_row < iota(shape, 0)).astype(F32)
    starts = jnp.sum(before, axis=1, keepdims=True).astype(jnp.int32)
    return iota(shape, 1) == starts


def cls_probs(query_wide, key_row, seg_row, head_count, segs):
    logits = dot_nt(query_wide, key_row)
    member = jnp.where(seg_row == iota((segs, seg_row.shape[1]), 0), 1.0, 0.0)
    member = jnp.concatenate([member] * head_count, axis=0)
    logits = jnp.where(member > 0.5, logits, -1000000000.0)
    top = jnp.max(logits, axis=1, keepdims=True)
    exponent = jnp.exp(logits - top)
    return exponent * (1.0 / jnp.sum(exponent, axis=1, keepdims=True))


def loads(pairs, sems):
    copies = [
        pltpu.make_async_copy(source, target, sems.at[index])
        for index, (source, target) in enumerate(pairs)
    ]
    for copy in copies:
        copy.start()
    return lambda index: copies[index].wait()


def front_kernel(
    idx_ref, seg_ref, bq, bv, bo, ga, sa, b_in, bb, gf, sf,
    x_hbm, wk_hbm, wv_hbm, wq_hbm, wo_hbm, w_in_hbm, w_back_hbm,
    k_hbm, v_hbm, pack_0, pack_1, pack_2, pack_3, qc_out, pre_attn_out, up_out, pre_ffn_out, enc_out, hot_out,
    x_s, wk, wv, wq, wo, w_in_v, w_back_v, k_s, v_s, sems, out_sems,
):
    rows, length, feature_dim = x_s.shape
    ff_dim = w_in_v.shape[1]
    head_count = feature_dim // HEAD_DIM
    wait = loads(
        [(x_hbm.at[0], x_s.at[0]), (wk_hbm, wk), (wv_hbm, wv), (wq_hbm, wq)]
        + [(x_hbm.at[row], x_s.at[row]) for row in range(1, rows)]
        + [(wo_hbm, wo), (w_in_hbm, w_in_v), (w_back_hbm, w_back_v)],
        sems,
    )
    mask = head_mask(head_count, SEGS, feature_dim)
    contexts, firsts, copies = [], [], []
    for row in range(rows):
        if row == 0:
            for index in range(3):
                wait(index)
        else:
            wait(3 + row)
        x = x_s[row]
        key_row = dot_nn(x, wk[...]).astype(BF16)
        k_s[row] = key_row
        value_row = (dot_nn(x, wv[...]) + row_of(bv)).astype(BF16)
        v_s[row] = value_row
        for kept, target in ((k_s, k_hbm), (v_s, v_hbm)):
            copy = pltpu.make_async_copy(kept.at[row], target.at[row], out_sems.at[len(copies)])
            copy.start()
            copies.append(copy)
        if row == 0:
            wait(3)
        seg_row = seg_ref[0, row : row + 1, :]
        first = jnp.where(cls_onehot(seg_row, SEGS), 1.0, 0.0).astype(BF16)
        x_cls = dot_nn(first, x).astype(BF16)
        query_cls = (dot_nn(x_cls, wq[...]) + row_of(bq)).astype(BF16)
        query_wide = block_heads((query_cls * (HEAD_DIM**-0.5)).astype(BF16), mask, head_count)
        probs = cls_probs(query_wide, key_row, seg_row, head_count, SEGS)
        context = heads_to_rows(dot_nn(probs.astype(BF16), value_row), mask, head_count, SEGS)
        contexts.append(context.astype(BF16))
        firsts.append(x_cls)
        qc_out[row * SEGS : (row + 1) * SEGS, :] = query_cls
        hot = jnp.where(seg_row == iota((LANES, length), 0), 1.0, 0.0)
        hot_out[row] = hot.T.astype(BF16)
    for index in range(3 + rows, 6 + rows):
        wait(index)
    if True:
        context_all = jnp.concatenate(contexts, axis=0)
        x_all = jnp.concatenate(firsts, axis=0)
        pre_attn = x_all.astype(F32) + (dot_nn(context_all, wo[...]) + row_of(bo))
        pre_attn_out[...] = pre_attn
        normed = layer_norm(pre_attn, row_of(ga), row_of(sa)).astype(BF16)
        up = dot_nn(normed, w_in_v[...]) + row_of(b_in)
        up_out[...] = up
        active = gelu_exact(up).astype(BF16)
        pre_ffn = normed.astype(F32) + (dot_nn(active, w_back_v[...]) + row_of(bb))
        pre_ffn_out[...] = pre_ffn
        enc_out[...] = layer_norm(pre_ffn, row_of(gf), row_of(sf)).astype(BF16)
        packs = (pack_0, pack_1, pack_2, pack_3)
        fill = pack_0.shape[1] - 2 * feature_dim
        group = ff_dim * LANES // fill
        size = group // GROUP
        if fill == ff_dim:
            for near in range(GROUP):
                packs[near][:, :ff_dim] = active
        else:
            for slot in range(fill // LANES):
                blocks = [
                    active[:, slot * group + size * b : slot * group + size * (b + 1)]
                    for b in range(GROUP)
                ]
                lanes = slot * LANES
                for near in range(GROUP):
                    source = (idx_ref[1] & (GROUP - 1)) ^ near
                    chosen = blocks[0]
                    for b in range(1, GROUP):
                        chosen = jnp.where(source == b, blocks[b], chosen)
                    packs[near][:, lanes : lanes + size] = chosen
                    packs[near][:, lanes + size : lanes + LANES] = jnp.zeros(
                        (active.shape[0], LANES - size), BF16
                    )
        for near in range(GROUP):
            packs[near][:, fill : fill + feature_dim] = normed
            packs[near][:, fill + feature_dim :] = context_all
    for copy in copies:
        copy.wait()


def full(shape):
    zeros = (0,) * len(shape)
    return pl.BlockSpec(shape, lambda *_: zeros)


ANY = pl.BlockSpec(memory_space=pl.ANY)


def active_width(places, ff_dim):
    group = GROUP * ff_dim // (2 * places)
    return ff_dim // group * LANES if group % LANES == 0 else ff_dim


def front(places, idx, segs, smalls, x_rows, mats):
    rows, length, feature_dim = x_rows.shape
    ff_dim = mats[-1].shape[0]
    cls = rows * SEGS
    shapes = (
        ((rows, length, feature_dim), BF16),
        ((rows, length, feature_dim), BF16),
        *(((cls, active_width(places, ff_dim) + 2 * feature_dim), BF16),) * GROUP,
        ((cls, feature_dim), BF16),
        ((cls, feature_dim), F32),
        ((cls, ff_dim), F32),
        ((cls, feature_dim), F32),
        ((cls, feature_dim), BF16),
        ((rows, length, LANES), BF16),
    )
    whole = pltpu.VMEM((rows, length, feature_dim), BF16)
    return pl.pallas_call(
        front_kernel,
        grid=(1,),
        in_specs=[pl.BlockSpec(memory_space=pltpu.SMEM)]
        + [full(a.shape) for a in (segs, *smalls)]
        + [ANY] * (1 + len(mats)),
        out_specs=[ANY, ANY] + [full(s) for s, _ in shapes[2:]],
        out_shape=[jax.ShapeDtypeStruct(s, d) for s, d in shapes],
        scratch_shapes=[whole]
        + [pltpu.VMEM(a.shape, BF16) for a in mats]
        + [
            whole,
            whole,
            pltpu.SemaphoreType.DMA((6 + rows,)),
            pltpu.SemaphoreType.DMA((2 * rows,)),
        ],
        compiler_params=pltpu.CompilerParams(vmem_limit_bytes=VMEM_BYTES),
        cost_estimate=pl.CostEstimate(
            flops=2 * rows * length * feature_dim * feature_dim * 3,
            bytes_accessed=30_000_000,
            transcendentals=rows * length * 384,
        ),
        name="front",
    )(idx, segs, *smalls, x_rows, *mats)


def encode_kernel_at(
    row, first, x_hbm, k_hbm, v_hbm, hot_hbm, wq_hbm, wo_hbm, w_in_hbm, w_back_hbm,
    bq, bo, ga, sa, b_in, bb, gf, sf, *refs
):
    enc_out, x_s, k_s, v_s, hot_s, wq, wo, w_in, w_back, sems = refs[-10:]
    tokens, feature_dim = x_s.shape
    held = k_s.shape[0]
    length = k_hbm.shape[1]
    ff_dim = w_in.shape[1]
    part, window = 128, 256
    low = max(0, min(first - 64, length - held))
    near = pl.ds(low, held)
    half = ff_dim // 2
    wait = loads(
        [
            (x_hbm.at[row, pl.ds(first, tokens)], x_s),
            (wq_hbm, wq),
            (hot_hbm.at[row, near], hot_s),
            (k_hbm.at[row, near], k_s),
            (v_hbm.at[row, near], v_s),
            (wo_hbm, wo),
            (w_in_hbm, w_in),
            (w_back_hbm, w_back),
        ],
        sems,
    )
    wait(0)
    wait(1)
    x = x_s[...]
    query = ((dot_nn(x, wq[...]) + row_of(bq)).astype(BF16) * (HEAD_DIM**-0.5)).astype(BF16)
    left = iota((part, 128), 1) < HEAD_DIM
    wait(2)
    wait(3)
    wait(4)
    contexts = []
    for sub in range(tokens // part):
        base = first + sub * part
        start = max(0, min(base - 64, length - window)) - low
        keys = k_s[start : start + window, :]
        values = v_s[start : start + window, :]
        apart = ((hot_s[start : start + window, :].astype(F32) - 1.0) * FAR).astype(BF16)
        hot_query = hot_s[base - low : base - low + part, :]
        pieces = []
        for pair in range(feature_dim // 128):
            lanes = slice(pair * 128, pair * 128 + 128)
            both = query[sub * part : (sub + 1) * part, lanes]
            zero = jnp.zeros_like(both)
            wide = jnp.concatenate(
                [
                    jnp.concatenate([jnp.where(left, both, zero), hot_query], axis=1),
                    jnp.concatenate([jnp.where(left, zero, both), hot_query], axis=1),
                ],
                axis=0,
            )
            logits = dot_nt(wide, jnp.concatenate([keys[:, lanes], apart], axis=1))
            top = jnp.max(logits, axis=1, keepdims=True)
            exponent = jnp.exp(logits - top)
            total = jnp.sum(exponent, axis=1, keepdims=True)
            out = dot_nn(exponent.astype(BF16), values[:, lanes]) * (1.0 / total)
            pieces.append(jnp.where(left, out[:part], out[part:]).astype(BF16))
        contexts.append(jnp.concatenate(pieces, axis=1))
    context = jnp.concatenate(contexts, axis=0)
    wait(5)
    pre_attn = x.astype(F32) + (dot_nn(context, wo[...]) + row_of(bo))
    normed = layer_norm(pre_attn, row_of(ga), row_of(sa)).astype(BF16)
    wait(6)
    wait(7)
    bias_in = row_of(b_in)
    total = normed.astype(F32) + row_of(bb)
    chunk = 768
    for start in range(0, ff_dim, chunk):
        cols = slice(start, start + chunk)
        up = dot_nn(normed, w_in[:, cols]) + bias_in[:, cols]
        total = total + dot_nn(gelu_exact(up).astype(BF16), w_back[cols, :])
    enc_out[0] = layer_norm(total, row_of(gf), row_of(sf)).astype(BF16)


def encode_part(part, parts, x_rows, keys, values, hot, mats, smalls, before):
    rows, length, feature_dim = x_rows.shape
    per_row = parts // rows
    row, tokens = part // per_row, length // per_row
    first = (part % per_row) * tokens
    held = min(length, tokens + 128)
    place = part % per_row
    extra = [] if before is None else [before]
    return pl.pallas_call(
        functools.partial(encode_kernel_at, row, first),
        grid=(1,),
        in_specs=[ANY] * (4 + len(mats)) + [full(a.shape) for a in smalls] + [ANY for _ in extra],
        out_specs=pl.BlockSpec((1, tokens, feature_dim), lambda i: (row, place, 0)),
        out_shape=jax.ShapeDtypeStruct((rows, length, feature_dim), BF16),
        input_output_aliases={} if before is None else {4 + len(mats) + len(smalls): 0},
        scratch_shapes=[
            pltpu.VMEM((tokens, feature_dim), BF16),
            pltpu.VMEM((held, feature_dim), BF16),
            pltpu.VMEM((held, feature_dim), BF16),
            pltpu.VMEM((held, hot.shape[2]), BF16),
        ]
        + [pltpu.VMEM(a.shape, BF16) for a in mats]
        + [pltpu.SemaphoreType.DMA((8,))],
        compiler_params=pltpu.CompilerParams(vmem_limit_bytes=VMEM_BYTES),
        cost_estimate=pl.CostEstimate(
            flops=tokens * feature_dim * feature_dim, bytes_accessed=1_000_000, transcendentals=0
        ),
        name="encode_part",
    )(x_rows, keys, values, hot, *mats, *smalls, *extra)


def middle_kernel(
    idx_ref, *refs
):
    own = refs[:GROUP]
    other = refs[GROUP : 2 * GROUP]
    (
        positives, pre_attn_ref, pre_ffn_ref, ga, gf, w_back_hbm, w_in_hbm, up_hbm, wo_hbm,
        scores_out, losses_out, late_out, gctx_out, gpa_out, vec_out,
        both, w_in_v, w_back_v, up_ref, wo, sems, wsems,
    ) = refs[2 * GROUP :]
    tower, place = idx_ref[0], idx_ref[1]
    far, cls, feature_dim = own[0].shape
    ff_dim = w_in_v.shape[1]
    copy_back = pltpu.make_async_copy(w_back_hbm, w_back_v, wsems.at[0])
    copy_in = pltpu.make_async_copy(w_in_hbm, w_in_v, wsems.at[1])
    copy_up = pltpu.make_async_copy(up_hbm, up_ref, wsems.at[2])
    copy_out = pltpu.make_async_copy(wo_hbm, wo, wsems.at[3])
    copies = []
    for side, group in ((tower, own), (1 - tower, other)):
        for near in range(GROUP):
            for slot in range(far):
                to = both.at[side, place ^ (slot * GROUP + near)]
                copies.append(
                    pltpu.make_async_copy(group[near].at[slot], to, sems.at[len(copies)])
                )
    for copy in copies:
        copy.start()
    copy_back.start()
    copy_up.start()
    copy_in.start()
    copy_out.start()
    for copy in copies:
        copy.wait()
    count = far * GROUP * cls
    scale = feature_dim**-0.5
    queries = both[0].reshape(count, feature_dim)
    positive_row = positives[...]
    block = min(count, max(64, (1 << 20) // count))

    def partial_of(first):
        passages = both[1, pl.ds(first // cls, block // cls)].reshape(block, feature_dim)
        scored = dot_nt(passages, queries) * scale
        top = jnp.max(scored, axis=0, keepdims=True)
        total = jnp.sum(jnp.exp(scored - top), axis=0, keepdims=True)
        hit = iota((block, count), 0) + first == positive_row
        return top, total, jnp.sum(jnp.where(hit, scored, 0.0), axis=0, keepdims=True)

    def joined(index, state):
        top, total, picked = partial_of(index * block)
        joint = jnp.maximum(state[0], top)
        return (
            joint,
            state[1] * jnp.exp(state[0] - joint) + total * jnp.exp(top - joint),
            state[2] + picked,
        )

    state = partial_of(0)
    if count // block > 1:
        state = lax.fori_loop(1, count // block, joined, state)
    row_log = state[0] + jnp.log(state[1])
    losses_out[...] = row_log - state[2]
    scores_out[...] = dot_nt(both[1, place], queries) * scale
    mine = both[tower, place]
    opposite = both[1 - tower].reshape(count, feature_dim)
    own_scores = dot_nt(mine, opposite) * scale
    own_top = jnp.max(own_scores, axis=1, keepdims=True)
    own_log = own_top + jnp.log(jnp.sum(jnp.exp(own_scores - own_top), axis=1, keepdims=True))
    lanes = iota((cls, count), 1)
    mine_index = iota((cls, count), 0) + place * cls
    spread_positive = jnp.broadcast_to(positive_row, (cls, count))
    own_positive = jnp.sum(
        jnp.where(lanes == mine_index, spread_positive.astype(F32), 0.0), axis=1, keepdims=True
    ).astype(jnp.int32)
    is_query = tower == 0
    log_used = jnp.where(is_query, jnp.broadcast_to(own_log, (cls, count)), row_log)
    hit_query = (lanes == own_positive).astype(F32)
    hit_passage = (spread_positive == mine_index).astype(F32)
    hit = jnp.where(is_query, hit_query, hit_passage)
    grad_scores = (jnp.exp(own_scores - log_used) - hit).astype(BF16)
    grad_cls = dot_nn(grad_scores, opposite) * scale
    grad_pre_ffn, grad_gf, grad_sf = layer_norm_back(pre_ffn_ref[...], row_of(gf), grad_cls)
    vec_out[0:1, :] = grad_gf
    vec_out[1:2, :] = grad_sf
    grad_down = grad_pre_ffn.astype(BF16)
    vec_out[2:3, :] = jnp.sum(grad_down.astype(F32), axis=0, keepdims=True)
    copy_back.wait()
    copy_up.wait()
    grad_up = (dot_nt(grad_down, w_back_v[...]) * gelu_slope(up_ref[...])).astype(BF16)
    late_out[:, :ff_dim] = grad_up
    late_out[:, ff_dim : ff_dim + feature_dim] = grad_down
    copy_in.wait()
    grad_normed = grad_pre_ffn + dot_nt(grad_up, w_in_v[...])
    grad_pre_attn, grad_ga, grad_sa = layer_norm_back(pre_attn_ref[...], row_of(ga), grad_normed)
    vec_out[3:4, :] = grad_ga
    vec_out[4:5, :] = grad_sa
    gpa_out[...] = grad_pre_attn
    grad_attended = grad_pre_attn.astype(BF16)
    late_out[:, ff_dim + feature_dim :] = grad_attended
    vec_out[5:6, :] = jnp.sum(grad_attended.astype(F32), axis=0, keepdims=True)
    copy_out.wait()
    gctx_out[...] = dot_nt(grad_attended, wo[...]).astype(BF16)


def middle(idx, own, other, positives, pre_attn, up, pre_ffn, w_back, w_in, wo, ga, gf):
    far, cls, feature_dim = own[0].shape
    ff_dim = w_in.shape[1]
    places = far * GROUP
    count = places * cls
    shapes = (
        ((cls, count), F32),
        ((1, count), F32),
        ((cls, ff_dim + 2 * feature_dim), BF16),
        ((cls, feature_dim), BF16),
        ((cls, feature_dim), F32),
        ((8, feature_dim), F32),
    )
    smalls = (positives, pre_attn, pre_ffn, ga, gf)
    return pl.pallas_call(
        middle_kernel,
        in_specs=[pl.BlockSpec(memory_space=pltpu.SMEM)]
        + [ANY] * (2 * GROUP)
        + [full(a.shape) for a in smalls]
        + [ANY] * 4,
        out_specs=[full(s) for s, _ in shapes],
        out_shape=[jax.ShapeDtypeStruct(s, d) for s, d in shapes],
        grid=(1,),
        scratch_shapes=[
            pltpu.VMEM((2, places, cls, feature_dim), BF16),
            pltpu.VMEM(w_in.shape, BF16),
            pltpu.VMEM(w_back.shape, BF16),
            pltpu.VMEM(up.shape, F32),
            pltpu.VMEM(wo.shape, BF16),
            pltpu.SemaphoreType.DMA((2 * places,)),
            pltpu.SemaphoreType.DMA((4,)),
        ],
        compiler_params=pltpu.CompilerParams(vmem_limit_bytes=VMEM_BYTES),
        cost_estimate=pl.CostEstimate(
            flops=2 * count * count * feature_dim, bytes_accessed=20_000_000, transcendentals=count * count
        ),
        name="loss",
    )(idx, *own, *other, *smalls, w_back, w_in, up, wo)


def spread_rows(shape, sizes, strides, masks):
    rest = iota(shape, 0)
    total = jnp.zeros(shape, jnp.int32)
    for size, stride, mask in zip(reversed(sizes), reversed(strides), reversed(masks)):
        above = jnp.floor((rest.astype(F32) + 0.5) * (1.0 / size)).astype(jnp.int32)
        digit = rest - above * size
        total = total + (digit ^ mask) * stride
        rest = above
    return total


def attn_back_kernel(
    idx_ref, seg_ref, qc_ref, gctx_ref, gpa_ref, vec_ref, x_hbm, k_hbm, v_hbm, wq_hbm, wk_hbm, wv_hbm,
    back_hbm, send_hbm, keep_hbm,
    x_s, k_s, v_s, wq, wk, wv, mixed_s, back_s, send_s, keep_s, sems, out_sems,
):
    tower, place = idx_ref[0], idx_ref[1]
    towers = 2
    rows, length, feature_dim = x_s.shape
    head_count = feature_dim // HEAD_DIM
    pairs = []
    for row in range(rows):
        pairs += [(k_hbm.at[row], k_s.at[row]), (v_hbm.at[row], v_s.at[row]), (x_hbm.at[row], x_s.at[row])]
    pairs += [(wq_hbm, wq), (wk_hbm, wk), (wv_hbm, wv)]
    wait = loads(pairs, sems)
    mask = head_mask(head_count, SEGS, feature_dim)
    scale = HEAD_DIM**-0.5
    shape = (feature_dim, feature_dim)
    wide = head_count * SEGS
    far, block = keep_s.shape[1:3]
    source = spread_rows(
        (feature_dim, 1),
        (towers, GROUP, far, block),
        (far * GROUP * block, block, GROUP * block, 1),
        (tower, place & (GROUP - 1), place // GROUP, 0),
    )
    order = jnp.where(iota(shape, 1) == source, 1.0, 0.0).astype(BF16)
    acc_q = acc_k = acc_v = bias_q = bias_v = None
    scatters, wides = [], []
    for row in range(rows):
        here = slice(row * SEGS, (row + 1) * SEGS)
        seg_row = seg_ref[0, row : row + 1, :]
        query_wide = block_heads((qc_ref[here, :] * scale).astype(BF16), mask, head_count)
        gctx_wide = block_heads(gctx_ref[here, :], mask, head_count)
        wait(3 * row)
        key_row = k_s[row]
        probs = cls_probs(query_wide, key_row, seg_row, head_count, SEGS)
        wait(3 * row + 1)
        grad_probs = dot_nt(gctx_wide, v_s[row])
        inner = jnp.sum(probs * grad_probs, axis=1, keepdims=True)
        grad_logits = (probs * (grad_probs - inner)).astype(BF16)
        grad_query = heads_to_rows(dot_nn(grad_logits, key_row), mask, head_count, SEGS)
        grad_query = (grad_query * scale).astype(BF16)
        mixed = jnp.concatenate([grad_logits, probs.astype(BF16)], axis=0)
        mixed_s[row] = mixed
        wait(3 * row + 2)
        x = x_s[row]
        first = jnp.where(cls_onehot(seg_row, SEGS), 1.0, 0.0).astype(BF16)
        x_turned = dot_nt(order, x).astype(BF16)
        xc_turned = dot_nt(x_turned, first).astype(BF16)
        drawn = dot_nt(x_turned, mixed).astype(BF16)
        bias_of_value = jnp.sum(gctx_wide.astype(F32) * jnp.sum(mixed[wide:].astype(F32), axis=1, keepdims=True), axis=0, keepdims=True)
        parts = (
            dot_nn(xc_turned, grad_query),
            dot_nn(drawn[:, :wide], query_wide),
            dot_nn(drawn[:, wide:], gctx_wide),
            jnp.sum(grad_query.astype(F32), axis=0, keepdims=True),
            bias_of_value,
        )
        if row == 0:
            acc_q, acc_k, acc_v, bias_q, bias_v = parts
            wait(3 * rows)
        else:
            acc_q, acc_k, acc_v = acc_q + parts[0], acc_k + parts[1], acc_v + parts[2]
            bias_q, bias_v = bias_q + parts[3], bias_v + parts[4]
        cls_back = gpa_ref[here, :] + dot_nt(grad_query, wq[...])
        scatters.append((jnp.concatenate([first] * 3, axis=0), jnp.concatenate(split(cls_back), axis=0)))
        wides.append((query_wide, gctx_wide))
    vectors = jnp.concatenate(
        [vec_ref[0:6, :], bias_q, bias_v, jnp.zeros((LANES - 8, feature_dim), F32)], axis=0
    )
    high, second, third = split(vectors)
    columns = dot_nt(order, high) + (dot_nt(order, second) + dot_nt(order, third))
    half = feature_dim // towers
    place_at = 0
    for grad in (acc_q, acc_k, acc_v, columns):
        lanes = slice(place_at, place_at + grad.shape[1])
        cut = (GROUP, far, block, grad.shape[1])
        keep_s[:, :, :, lanes] = grad[:half].astype(BF16).reshape(cut)
        send_s[:, :, :, lanes] = grad[half:].astype(BF16).reshape(cut)
        place_at = lanes.stop
    copies = [
        pltpu.make_async_copy(send_s, send_hbm, out_sems.at[0]),
        pltpu.make_async_copy(keep_s, keep_hbm, out_sems.at[1]),
    ]
    for copy in copies:
        copy.start()
    wait(3 * rows + 1)
    wait(3 * rows + 2)
    part = length // 2
    for row in range(rows):
        first, pieces = scatters[row]
        query_wide, gctx_wide = wides[row]
        spread = jnp.concatenate(
            [dot_nt(query_wide, wk[...]).astype(BF16), dot_nt(gctx_wide, wv[...]).astype(BF16)], axis=0
        )
        for start in range(0, length, part):
            here = slice(start, start + part)
            back = dot_tn(mixed_s[row, :, here], spread)
            back_s[row, here, :] = back + dot_tn(first[:, here], pieces)
            copy = pltpu.make_async_copy(
                back_s.at[row, pl.ds(start, part)],
                back_hbm.at[row, pl.ds(start, part)],
                out_sems.at[len(copies)],
            )
            copy.start()
            copies.append(copy)
    for copy in copies:
        copy.wait()


def attn_back(idx, segs, qc, gctx, gpa, vectors, x_rows, keys, values, wq, wk, wv, places):
    rows, length, feature_dim = x_rows.shape
    block = feature_dim // (2 * places)
    half = (GROUP, places // GROUP, block, 3 * feature_dim + LANES)
    shapes = (((rows, length, feature_dim), F32), (half, BF16), (half, BF16))
    smalls = (segs, qc, gctx, gpa, vectors)
    square = pltpu.VMEM((feature_dim, feature_dim), BF16)
    whole = pltpu.VMEM((rows, length, feature_dim), BF16)
    return pl.pallas_call(
        attn_back_kernel,
        grid=(1,),
        in_specs=[pl.BlockSpec(memory_space=pltpu.SMEM)]
        + [full(a.shape) for a in smalls]
        + [ANY] * 6,
        out_specs=[ANY] * 3,
        out_shape=[jax.ShapeDtypeStruct(s, d) for s, d in shapes],
        scratch_shapes=[whole, whole, whole, square, square, square]
        + [
            pltpu.VMEM((rows, 2 * feature_dim // HEAD_DIM * SEGS, length), BF16),
            pltpu.VMEM((rows, length, feature_dim), F32),
            pltpu.VMEM(half, BF16),
            pltpu.VMEM(half, BF16),
            pltpu.SemaphoreType.DMA((3 * rows + 3,)),
            pltpu.SemaphoreType.DMA((2 + 2 * rows,)),
        ],
        compiler_params=pltpu.CompilerParams(vmem_limit_bytes=VMEM_BYTES),
        cost_estimate=pl.CostEstimate(
            flops=2 * rows * length * feature_dim * feature_dim * 6,
            bytes_accessed=30_000_000,
            transcendentals=rows * length * 384,
        ),
        name="attention_back",
    )(idx, *smalls, x_rows, keys, values, wq, wk, wv)


def weights_kernel(feature_dim, ff_dim, idx_ref, *refs):
    early = refs[:GROUP]
    late = refs[GROUP : 2 * GROUP]
    keep_out, send_out = refs[2 * GROUP :]
    tower, place = idx_ref[0], idx_ref[1]
    _, pairs, block, _ = send_out.shape
    far = 2 * pairs
    pieces = ff_dim // feature_dim
    fill = early[0].shape[1] - 2 * feature_dim

    def pick(group, near, columns):
        source = spread_rows(
            (2 * far * block, 1),
            (2, 2, pairs, block),
            (far * group, group, 2 * group, 1),
            (tower, place // GROUP & 1, place // (2 * GROUP), 0),
        )
        shape = (2 * far * block, columns)
        return jnp.where(iota(shape, 1) == source + near, 1.0, 0.0).astype(BF16)

    def stacked(parts, first, columns):
        return jnp.concatenate([ref[:, first : first + columns] for ref in parts], axis=0)

    def put(first, grad):
        columns = grad.shape[1]
        half = far * block
        shape = (2, pairs, block, columns)
        keep_out[:, :, :, first : first + columns] = grad[:half].astype(BF16).reshape(shape)
        send_out[:, :, :, first : first + columns] = grad[half:].astype(BF16).reshape(shape)

    near = place & (GROUP - 1)
    narrow = pick(GROUP * block, near * block, feature_dim)
    grad_up = stacked(late, 0, ff_dim)
    grad_down = stacked(late, ff_dim, feature_dim)
    grad_attended = stacked(late, ff_dim + feature_dim, feature_dim)
    active = stacked(early, 0, fill)
    normed = dot_nt(narrow, stacked(early, fill, feature_dim)).astype(BF16)
    context = dot_nt(narrow, stacked(early, fill + feature_dim, feature_dim)).astype(BF16)
    put(0, dot_nn(normed, grad_up))
    for piece in range(pieces):
        if fill == ff_dim:
            chosen = pick(GROUP * pieces * block, (near * pieces + piece) * block, fill)
        else:
            chosen = pick(LANES, piece * block, fill)
        turned = dot_nt(chosen, active).astype(BF16)
        put(ff_dim + piece * feature_dim, dot_nn(turned, grad_down))
    put(2 * ff_dim, dot_nn(context, grad_attended))
    bias = jnp.sum(grad_up.astype(F32), axis=0, keepdims=True)
    stack = jnp.concatenate([*split(bias), jnp.zeros((LANES - 3, ff_dim), BF16)], axis=0)
    lane = iota((2 * far * block, LANES), 1)
    columns = jnp.zeros((2 * far * block, LANES), F32)
    for piece in range(pieces):
        chosen = pick(GROUP * pieces * block, (near * pieces + piece) * block, ff_dim)
        total = jnp.sum(dot_nt(chosen, stack), axis=1, keepdims=True)
        columns = jnp.where(lane == piece, total, columns)
    put(2 * ff_dim + feature_dim, columns)


def weights(idx, early, late, places, feature_dim, ff_dim):
    far = places // GROUP
    block = feature_dim // (2 * places)
    packed = 2 * ff_dim + feature_dim + LANES
    half = (2, far // 2, block, packed)
    return pl.pallas_call(
        functools.partial(weights_kernel, feature_dim, ff_dim),
        grid=(1,),
        in_specs=[pl.BlockSpec(memory_space=pltpu.SMEM)] + [full(a.shape) for a in (*early, *late)],
        out_specs=[full(half), full(half)],
        out_shape=[jax.ShapeDtypeStruct(half, BF16), jax.ShapeDtypeStruct(half, BF16)],
        compiler_params=pltpu.CompilerParams(vmem_limit_bytes=VMEM_BYTES),
        cost_estimate=pl.CostEstimate(
            flops=50_000_000_000, bytes_accessed=14_000_000, transcendentals=0
        ),
        name="weight_grads",
    )(idx, *early, *late)


def tied(*values):
    return lax.optimization_barrier(values)


def on_device(
    hidden_in, segment_ids, positives, w_query, b_query, w_key, w_value, b_value, w_out, b_out,
    gain_attn, shift_attn, w_in, b_in, w_back, b_back, gain_ffn, shift_ffn,
):
    feature_dim = hidden_in.shape[2]
    ff_dim = w_in.shape[1]
    rows, length = segment_ids.shape[1], segment_ids.shape[2]
    places = lax.axis_size("dp")
    far = places // GROUP
    tower, place = lax.axis_index("tower"), lax.axis_index("dp")
    idx = jnp.stack([tower, place, places]).astype(jnp.int32)
    x_rows = hidden_in.reshape(rows, length, feature_dim)
    keys, values, *pack, query_cls, pre_attn, up, pre_ffn, enc_cls, hot = front(
        places, idx, segment_ids,
        (b_query, b_value, b_out, gain_attn, shift_attn, b_in, b_back, gain_ffn, shift_ffn),
        x_rows, (w_key, w_value, w_query, w_out, w_in, w_back),
    )
    mats = (w_query, w_out, w_in, w_back)
    smalls = (b_query, b_out, gain_attn, shift_attn, b_in, b_back, gain_ffn, shift_ffn)

    def encode(part, before):
        return encode_part(part, 2 * rows, x_rows, keys, values, hot, mats, smalls, before)

    along = [moved(enc_cls, "dp", GROUP * m) for m in range(1, far)]
    early = [pack[0]] + [moved(pack[m], "dp", m) for m in range(1, GROUP)]
    encoded = encode(0, None)
    along, early[1:3], encoded = tied(along, early[1:3], encoded)
    own, encoded = tied(jnp.stack([enc_cls] + list(along)), encoded)
    crossed = [moved(own, "dp", m) for m in range(1, GROUP)]
    encoded = encode(1, encoded)
    crossed, encoded = tied(crossed, encoded)
    own = [own] + list(crossed)
    other = [moved(quad, "tower", 1) for quad in own]
    scores, losses, late_own, gctx, gpa, vec_mid = middle(
        idx, own, other, positives.reshape(1, -1), pre_attn, up, pre_ffn, w_back, w_in,
        w_out, gain_attn, gain_ffn,
    )
    gctx, early = tied(gctx, early)
    late = [late_own] + [moved(late_own, "dp", m) for m in range(1, GROUP)]
    back, send, keep = attn_back(
        idx, segment_ids, query_cls, gctx, gpa, vec_mid, x_rows, keys, values,
        w_query, w_key, w_value, places,
    )
    late, keep = tied(late, keep)
    send = moved(send, "tower", 1)
    weight_keep, weight_send = weights(idx, early, late, places, feature_dim, ff_dim)
    send, weight_keep, weight_send = tied(send, weight_keep, weight_send)
    weight_send = moved(weight_send, "tower", 1)
    paired = [keep[m].astype(F32) + send[m].astype(F32) for m in range(GROUP)]
    near_out = [part.astype(BF16) for part in paired[1:]]
    near_sent = [moved(near_out[m - 1], "dp", m) for m in range(1, GROUP)]
    weight_out = (weight_keep[1].astype(F32) + weight_send[1].astype(F32)).astype(BF16)
    weight_out, encoded = tied(weight_out, encoded)
    reach, arrived = 1, moved(weight_out, "dp", GROUP)
    encoded = encode(2, encoded)
    near_sent, arrived, encoded = tied(near_sent, arrived, encoded)
    weight_sum = weight_keep[0].astype(F32) + weight_send[0].astype(F32) + arrived.astype(F32)
    near = paired[0]
    for part in near_sent:
        near = near + part.astype(F32)
    far_out = [near[m].astype(BF16) for m in range(1, far)]
    while weight_sum.shape[0] > 1:
        reach = reach * 2
        half = weight_sum.reshape(weight_sum.shape[0] // 2, 2, *weight_sum.shape[1:])
        weight_out = half[:, 1].astype(BF16)
        last = reach == far // 2
        if last:
            far_out, weight_out, encoded = tied(far_out, weight_out, encoded)
            far_sent = [moved(far_out[m - 1], "dp", GROUP * m) for m in range(1, far)]
        arrived = moved(weight_out, "dp", GROUP * reach)
        if last:
            encoded = encode(3, encoded)
            far_sent, arrived, encoded = tied(far_sent, arrived, encoded)
        weight_sum = half[:, 0] + arrived.astype(F32)
    weight_sum = weight_sum[0]
    grad_qkv = near[0]
    for part in far_sent:
        grad_qkv = grad_qkv + part.astype(F32)
    grad_in = weight_sum[:, :ff_dim]
    grad_back = jnp.concatenate(
        [
            weight_sum[:, first : first + feature_dim]
            for first in range(ff_dim, 2 * ff_dim, feature_dim)
        ],
        axis=0,
    )
    grad_out = weight_sum[:, 2 * ff_dim : 2 * ff_dim + feature_dim]
    first = 2 * ff_dim + feature_dim
    b_i = weight_sum[:, first : first + ff_dim // feature_dim].T.reshape(-1)
    columns = grad_qkv[:, 3 * feature_dim : 3 * feature_dim + 8].T
    g_f, s_f, b_b, g_a, s_a, b_o, b_q, b_v = [columns[i] for i in range(8)]
    return (
        encoded.reshape(hidden_in.shape),
        scores.T,
        losses.reshape(-1),
        back.reshape(hidden_in.shape),
        grad_qkv[:, :feature_dim],
        b_q,
        grad_qkv[:, feature_dim : 2 * feature_dim],
        grad_qkv[:, 2 * feature_dim : 3 * feature_dim],
        b_v,
        grad_out,
        b_o,
        g_a,
        s_a,
        grad_in,
        b_i,
        grad_back,
        b_b,
        g_f,
        s_f,
    )


def solution(mesh):
    placed = (P("tower", "dp", None), P("tower", "dp", None)) + (P(),) * 16
    matrix, vector = P(("tower", "dp"), None), P(("tower", "dp"))
    return jax.shard_map(
        on_device,
        mesh=mesh,
        in_specs=placed,
        out_specs=(
            P("tower", "dp", None),
            P(None, "dp"),
            P(),
            P("tower", "dp", None),
            matrix,
            vector,
            matrix,
            matrix,
            vector,
            matrix,
            vector,
            vector,
            vector,
            matrix,
            vector,
            matrix,
            vector,
            vector,
            vector,
        ),
        check_vma=False,
    )
```

```python
import functools

import jax
import jax.numpy as jnp
from jax import lax
from jax.experimental import pallas as pl
from jax.experimental.pallas import tpu as pltpu
from jax.sharding import PartitionSpec as P

HEAD_DIM = 64
SEGS = 32
GROUP = 4
LANES = 128
FAR = float(2**30)
VMEM_BYTES = 60 * 1024 * 1024
F32 = jnp.float32
BF16 = jnp.bfloat16


def moved(value, axis, mask):
    pairs = [(source, source ^ mask) for source in range(lax.axis_size(axis))]
    return lax.ppermute(value, axis, pairs)


def dot_nn(a, b):
    return lax.dot_general(a, b, (((1,), (0,)), ((), ())), preferred_element_type=F32)


def dot_nt(a, b):
    return lax.dot_general(a, b, (((1,), (1,)), ((), ())), preferred_element_type=F32)


def dot_tn(a, b):
    return lax.dot_general(a, b, (((0,), (0,)), ((), ())), preferred_element_type=F32)


def iota(shape, dim):
    return lax.broadcasted_iota(jnp.int32, shape, dim)


def row_of(ref):
    return ref[...].astype(F32).reshape(1, -1)


def norm_parts(values):
    average = jnp.mean(values, axis=-1, keepdims=True)
    centered = values - average
    spread = jnp.mean(centered * centered, axis=-1, keepdims=True)
    inverse = lax.rsqrt(spread + 1e-12)
    return centered * inverse, inverse


def layer_norm(values, gain, shift):
    scaled, _ = norm_parts(values)
    return scaled * gain + shift


def layer_norm_back(values, gain, grad):
    scaled, inverse = norm_parts(values)
    inner = grad * gain
    mean_inner = jnp.mean(inner, axis=-1, keepdims=True)
    mean_scaled = jnp.mean(inner * scaled, axis=-1, keepdims=True)
    back = inverse * (inner - mean_inner - scaled * mean_scaled)
    return back, jnp.sum(grad * scaled, axis=0, keepdims=True), jnp.sum(grad, axis=0, keepdims=True)


def phi_of(values):
    return 0.5 * (1.0 + lax.erf(values * (2.0**-0.5)))


def gelu_exact(values):
    return values * phi_of(values)


def gelu_slope(values):
    bell = jnp.exp(-0.5 * values * values) * 0.3989422804014327
    return phi_of(values) + values * bell


def head_mask(head_count, segs, feature_dim):
    head_row = iota((head_count * segs, 1), 0) >> (segs.bit_length() - 1)
    head_col = iota((1, feature_dim), 1) >> (HEAD_DIM.bit_length() - 1)
    return jnp.where(head_row == head_col, 1.0, 0.0)


def block_heads(rows, mask, head_count):
    return jnp.concatenate([rows] * head_count, axis=0) * mask.astype(BF16)


def heads_to_rows(wide, mask, head_count, segs):
    kept = wide * mask
    total = kept[:segs]
    for head in range(1, head_count):
        total = total + kept[head * segs : (head + 1) * segs]
    return total


def split(values):
    high = values.astype(BF16)
    rest = values - high.astype(F32)
    second = rest.astype(BF16)
    return high, second, (rest - second.astype(F32)).astype(BF16)


def cls_onehot(seg_row, segs):
    shape = (segs, seg_row.shape[1])
    before = (seg_row < iota(shape, 0)).astype(F32)
    starts = jnp.sum(before, axis=1, keepdims=True).astype(jnp.int32)
    return iota(shape, 1) == starts


def cls_probs(query_wide, key_row, seg_row, head_count, segs):
    logits = dot_nt(query_wide, key_row)
    member = jnp.where(seg_row == iota((segs, seg_row.shape[1]), 0), 1.0, 0.0)
    member = jnp.concatenate([member] * head_count, axis=0)
    logits = jnp.where(member > 0.5, logits, -1000000000.0)
    top = jnp.max(logits, axis=1, keepdims=True)
    exponent = jnp.exp(logits - top)
    return exponent * (1.0 / jnp.sum(exponent, axis=1, keepdims=True))


def loads(pairs, sems):
    copies = [
        pltpu.make_async_copy(source, target, sems.at[index])
        for index, (source, target) in enumerate(pairs)
    ]
    for copy in copies:
        copy.start()
    return lambda index: copies[index].wait()


def front_kernel(
    idx_ref, seg_ref, bq, bv, bo, ga, sa, b_in, bb, gf, sf,
    x_hbm, wk_hbm, wv_hbm, wq_hbm, wo_hbm, w_in_hbm, w_back_hbm,
    k_hbm, v_hbm, pack_0, pack_1, pack_2, pack_3, qc_out, pre_attn_out, up_out, pre_ffn_out, enc_out, hot_out,
    x_s, wk, wv, wq, wo, w_in_v, w_back_v, k_s, v_s, sems, out_sems,
):
    rows, length, feature_dim = x_s.shape
    ff_dim = w_in_v.shape[1]
    head_count = feature_dim // HEAD_DIM
    wait = loads(
        [(x_hbm.at[0], x_s.at[0]), (wk_hbm, wk), (wv_hbm, wv), (wq_hbm, wq)]
        + [(x_hbm.at[row], x_s.at[row]) for row in range(1, rows)]
        + [(wo_hbm, wo), (w_in_hbm, w_in_v), (w_back_hbm, w_back_v)],
        sems,
    )
    mask = head_mask(head_count, SEGS, feature_dim)
    contexts, firsts, copies = [], [], []
    for row in range(rows):
        if row == 0:
            for index in range(3):
                wait(index)
        else:
            wait(3 + row)
        x = x_s[row]
        key_row = dot_nn(x, wk[...]).astype(BF16)
        k_s[row] = key_row
        value_row = (dot_nn(x, wv[...]) + row_of(bv)).astype(BF16)
        v_s[row] = value_row
        for kept, target in ((k_s, k_hbm), (v_s, v_hbm)):
            copy = pltpu.make_async_copy(kept.at[row], target.at[row], out_sems.at[len(copies)])
            copy.start()
            copies.append(copy)
        if row == 0:
            wait(3)
        seg_row = seg_ref[0, row : row + 1, :]
        first = jnp.where(cls_onehot(seg_row, SEGS), 1.0, 0.0).astype(BF16)
        x_cls = dot_nn(first, x).astype(BF16)
        query_cls = (dot_nn(x_cls, wq[...]) + row_of(bq)).astype(BF16)
        query_wide = block_heads((query_cls * (HEAD_DIM**-0.5)).astype(BF16), mask, head_count)
        probs = cls_probs(query_wide, key_row, seg_row, head_count, SEGS)
        context = heads_to_rows(dot_nn(probs.astype(BF16), value_row), mask, head_count, SEGS)
        contexts.append(context.astype(BF16))
        firsts.append(x_cls)
        qc_out[row * SEGS : (row + 1) * SEGS, :] = query_cls
        hot = jnp.where(seg_row == iota((LANES, length), 0), 1.0, 0.0)
        hot_out[row] = hot.T.astype(BF16)
    for index in range(3 + rows, 6 + rows):
        wait(index)
    if True:
        context_all = jnp.concatenate(contexts, axis=0)
        x_all = jnp.concatenate(firsts, axis=0)
        pre_attn = x_all.astype(F32) + (dot_nn(context_all, wo[...]) + row_of(bo))
        pre_attn_out[...] = pre_attn
        normed = layer_norm(pre_attn, row_of(ga), row_of(sa)).astype(BF16)
        up = dot_nn(normed, w_in_v[...]) + row_of(b_in)
        up_out[...] = up
        active = gelu_exact(up).astype(BF16)
        pre_ffn = normed.astype(F32) + (dot_nn(active, w_back_v[...]) + row_of(bb))
        pre_ffn_out[...] = pre_ffn
        enc_out[...] = layer_norm(pre_ffn, row_of(gf), row_of(sf)).astype(BF16)
        packs = (pack_0, pack_1, pack_2, pack_3)
        fill = pack_0.shape[1] - 2 * feature_dim
        group = ff_dim * LANES // fill
        size = group // GROUP
        if fill == ff_dim:
            for near in range(GROUP):
                packs[near][:, :ff_dim] = active
        else:
            for slot in range(fill // LANES):
                blocks = [
                    active[:, slot * group + size * b : slot * group + size * (b + 1)]
                    for b in range(GROUP)
                ]
                lanes = slot * LANES
                for near in range(GROUP):
                    source = (idx_ref[1] & (GROUP - 1)) ^ near
                    chosen = blocks[0]
                    for b in range(1, GROUP):
                        chosen = jnp.where(source == b, blocks[b], chosen)
                    packs[near][:, lanes : lanes + size] = chosen
                    packs[near][:, lanes + size : lanes + LANES] = jnp.zeros(
                        (active.shape[0], LANES - size), BF16
                    )
        for near in range(GROUP):
            packs[near][:, fill : fill + feature_dim] = normed
            packs[near][:, fill + feature_dim :] = context_all
    for copy in copies:
        copy.wait()


def full(shape):
    zeros = (0,) * len(shape)
    return pl.BlockSpec(shape, lambda *_: zeros)


ANY = pl.BlockSpec(memory_space=pl.ANY)


def active_width(places, ff_dim):
    group = GROUP * ff_dim // (2 * places)
    return ff_dim // group * LANES if group % LANES == 0 else ff_dim


def front(places, idx, segs, smalls, x_rows, mats):
    rows, length, feature_dim = x_rows.shape
    ff_dim = mats[-1].shape[0]
    cls = rows * SEGS
    shapes = (
        ((rows, length, feature_dim), BF16),
        ((rows, length, feature_dim), BF16),
        *(((cls, active_width(places, ff_dim) + 2 * feature_dim), BF16),) * GROUP,
        ((cls, feature_dim), BF16),
        ((cls, feature_dim), F32),
        ((cls, ff_dim), F32),
        ((cls, feature_dim), F32),
        ((cls, feature_dim), BF16),
        ((rows, length, LANES), BF16),
    )
    whole = pltpu.VMEM((rows, length, feature_dim), BF16)
    return pl.pallas_call(
        front_kernel,
        grid=(1,),
        in_specs=[pl.BlockSpec(memory_space=pltpu.SMEM)]
        + [full(a.shape) for a in (segs, *smalls)]
        + [ANY] * (1 + len(mats)),
        out_specs=[ANY, ANY] + [full(s) for s, _ in shapes[2:]],
        out_shape=[jax.ShapeDtypeStruct(s, d) for s, d in shapes],
        scratch_shapes=[whole]
        + [pltpu.VMEM(a.shape, BF16) for a in mats]
        + [
            whole,
            whole,
            pltpu.SemaphoreType.DMA((6 + rows,)),
            pltpu.SemaphoreType.DMA((2 * rows,)),
        ],
        compiler_params=pltpu.CompilerParams(vmem_limit_bytes=VMEM_BYTES),
        cost_estimate=pl.CostEstimate(
            flops=2 * rows * length * feature_dim * feature_dim * 3,
            bytes_accessed=30_000_000,
            transcendentals=rows * length * 384,
        ),
        name="front",
    )(idx, segs, *smalls, x_rows, *mats)


def encode_kernel_at(
    row, first, x_hbm, k_hbm, v_hbm, hot_hbm, wq_hbm, wo_hbm, w_in_hbm, w_back_hbm,
    bq, bo, ga, sa, b_in, bb, gf, sf, *refs
):
    enc_out, x_s, k_s, v_s, hot_s, wq, wo, w_in, w_back, sems = refs[-10:]
    tokens, feature_dim = x_s.shape
    held = k_s.shape[0]
    length = k_hbm.shape[1]
    ff_dim = w_in.shape[1]
    part, window = 128, 256
    low = max(0, min(first - 64, length - held))
    near = pl.ds(low, held)
    half = ff_dim // 2
    wait = loads(
        [
            (x_hbm.at[row, pl.ds(first, tokens)], x_s),
            (wq_hbm, wq),
            (hot_hbm.at[row, near], hot_s),
            (k_hbm.at[row, near], k_s),
            (v_hbm.at[row, near], v_s),
            (wo_hbm, wo),
            (w_in_hbm, w_in),
            (w_back_hbm, w_back),
        ],
        sems,
    )
    wait(0)
    wait(1)
    x = x_s[...]
    query = ((dot_nn(x, wq[...]) + row_of(bq)).astype(BF16) * (HEAD_DIM**-0.5)).astype(BF16)
    left = iota((part, 128), 1) < HEAD_DIM
    wait(2)
    wait(3)
    wait(4)
    contexts = []
    for sub in range(tokens // part):
        base = first + sub * part
        start = max(0, min(base - 64, length - window)) - low
        keys = k_s[start : start + window, :]
        values = v_s[start : start + window, :]
        apart = ((hot_s[start : start + window, :].astype(F32) - 1.0) * FAR).astype(BF16)
        hot_query = hot_s[base - low : base - low + part, :]
        pieces = []
        for pair in range(feature_dim // 128):
            lanes = slice(pair * 128, pair * 128 + 128)
            both = query[sub * part : (sub + 1) * part, lanes]
            zero = jnp.zeros_like(both)
            wide = jnp.concatenate(
                [
                    jnp.concatenate([jnp.where(left, both, zero), hot_query], axis=1),
                    jnp.concatenate([jnp.where(left, zero, both), hot_query], axis=1),
                ],
                axis=0,
            )
            logits = dot_nt(wide, jnp.concatenate([keys[:, lanes], apart], axis=1))
            top = jnp.max(logits, axis=1, keepdims=True)
            exponent = jnp.exp(logits - top)
            total = jnp.sum(exponent, axis=1, keepdims=True)
            out = dot_nn(exponent.astype(BF16), values[:, lanes]) * (1.0 / total)
            pieces.append(jnp.where(left, out[:part], out[part:]).astype(BF16))
        contexts.append(jnp.concatenate(pieces, axis=1))
    context = jnp.concatenate(contexts, axis=0)
    wait(5)
    pre_attn = x.astype(F32) + (dot_nn(context, wo[...]) + row_of(bo))
    normed = layer_norm(pre_attn, row_of(ga), row_of(sa)).astype(BF16)
    wait(6)
    wait(7)
    bias_in = row_of(b_in)
    total = normed.astype(F32) + row_of(bb)
    chunk = 768
    for start in range(0, ff_dim, chunk):
        cols = slice(start, start + chunk)
        up = dot_nn(normed, w_in[:, cols]) + bias_in[:, cols]
        total = total + dot_nn(gelu_exact(up).astype(BF16), w_back[cols, :])
    enc_out[0] = layer_norm(total, row_of(gf), row_of(sf)).astype(BF16)


def encode_part(part, parts, x_rows, keys, values, hot, mats, smalls, before):
    rows, length, feature_dim = x_rows.shape
    per_row = parts // rows
    row, tokens = part // per_row, length // per_row
    first = (part % per_row) * tokens
    held = min(length, tokens + 128)
    place = part % per_row
    extra = [] if before is None else [before]
    return pl.pallas_call(
        functools.partial(encode_kernel_at, row, first),
        grid=(1,),
        in_specs=[ANY] * (4 + len(mats)) + [full(a.shape) for a in smalls] + [ANY for _ in extra],
        out_specs=pl.BlockSpec((1, tokens, feature_dim), lambda i: (row, place, 0)),
        out_shape=jax.ShapeDtypeStruct((rows, length, feature_dim), BF16),
        input_output_aliases={} if before is None else {4 + len(mats) + len(smalls): 0},
        scratch_shapes=[
            pltpu.VMEM((tokens, feature_dim), BF16),
            pltpu.VMEM((held, feature_dim), BF16),
            pltpu.VMEM((held, feature_dim), BF16),
            pltpu.VMEM((held, hot.shape[2]), BF16),
        ]
        + [pltpu.VMEM(a.shape, BF16) for a in mats]
        + [pltpu.SemaphoreType.DMA((8,))],
        compiler_params=pltpu.CompilerParams(vmem_limit_bytes=56 * 1024 * 1024),
        cost_estimate=pl.CostEstimate(
            flops=tokens * feature_dim * feature_dim, bytes_accessed=1_000_000, transcendentals=0
        ),
        name="encode_part",
    )(x_rows, keys, values, hot, *mats, *smalls, *extra)


def middle_kernel(
    idx_ref, *refs
):
    own = refs[:GROUP]
    other = refs[GROUP : 2 * GROUP]
    (
        positives, pre_attn_ref, pre_ffn_ref, ga, gf, w_back_hbm, w_in_hbm, up_hbm, wo_hbm,
        scores_out, losses_out, late_out, gctx_out, gpa_out, vec_out,
        both, w_in_v, w_back_v, up_ref, wo, sems, wsems,
    ) = refs[2 * GROUP :]
    tower, place = idx_ref[0], idx_ref[1]
    far, cls, feature_dim = own[0].shape
    ff_dim = w_in_v.shape[1]
    copy_back = pltpu.make_async_copy(w_back_hbm, w_back_v, wsems.at[0])
    copy_in = pltpu.make_async_copy(w_in_hbm, w_in_v, wsems.at[1])
    copy_up = pltpu.make_async_copy(up_hbm, up_ref, wsems.at[2])
    copy_out = pltpu.make_async_copy(wo_hbm, wo, wsems.at[3])
    copies = []
    for side, group in ((tower, own), (1 - tower, other)):
        for near in range(GROUP):
            for slot in range(far):
                to = both.at[side, place ^ (slot * GROUP + near)]
                copies.append(
                    pltpu.make_async_copy(group[near].at[slot], to, sems.at[len(copies)])
                )
    for copy in copies:
        copy.start()
    copy_back.start()
    copy_up.start()
    copy_in.start()
    copy_out.start()
    for copy in copies:
        copy.wait()
    count = far * GROUP * cls
    scale = feature_dim**-0.5
    queries = both[0].reshape(count, feature_dim)
    positive_row = positives[...]
    block = min(count, max(64, (1 << 20) // count))

    def partial_of(first):
        passages = both[1, pl.ds(first // cls, block // cls)].reshape(block, feature_dim)
        scored = dot_nt(passages, queries) * scale
        top = jnp.max(scored, axis=0, keepdims=True)
        total = jnp.sum(jnp.exp(scored - top), axis=0, keepdims=True)
        hit = iota((block, count), 0) + first == positive_row
        return top, total, jnp.sum(jnp.where(hit, scored, 0.0), axis=0, keepdims=True)

    def joined(index, state):
        top, total, picked = partial_of(index * block)
        joint = jnp.maximum(state[0], top)
        return (
            joint,
            state[1] * jnp.exp(state[0] - joint) + total * jnp.exp(top - joint),
            state[2] + picked,
        )

    state = partial_of(0)
    if count // block > 1:
        state = lax.fori_loop(1, count // block, joined, state)
    row_log = state[0] + jnp.log(state[1])
    losses_out[...] = row_log - state[2]
    scores_out[...] = dot_nt(both[1, place], queries) * scale
    mine = both[tower, place]
    opposite = both[1 - tower].reshape(count, feature_dim)
    own_scores = dot_nt(mine, opposite) * scale
    own_top = jnp.max(own_scores, axis=1, keepdims=True)
    own_log = own_top + jnp.log(jnp.sum(jnp.exp(own_scores - own_top), axis=1, keepdims=True))
    lanes = iota((cls, count), 1)
    mine_index = iota((cls, count), 0) + place * cls
    spread_positive = jnp.broadcast_to(positive_row, (cls, count))
    own_positive = jnp.sum(
        jnp.where(lanes == mine_index, spread_positive.astype(F32), 0.0), axis=1, keepdims=True
    ).astype(jnp.int32)
    is_query = tower == 0
    log_used = jnp.where(is_query, jnp.broadcast_to(own_log, (cls, count)), row_log)
    hit_query = (lanes == own_positive).astype(F32)
    hit_passage = (spread_positive == mine_index).astype(F32)
    hit = jnp.where(is_query, hit_query, hit_passage)
    grad_scores = (jnp.exp(own_scores - log_used) - hit).astype(BF16)
    grad_cls = dot_nn(grad_scores, opposite) * scale
    grad_pre_ffn, grad_gf, grad_sf = layer_norm_back(pre_ffn_ref[...], row_of(gf), grad_cls)
    vec_out[0:1, :] = grad_gf
    vec_out[1:2, :] = grad_sf
    grad_down = grad_pre_ffn.astype(BF16)
    vec_out[2:3, :] = jnp.sum(grad_down.astype(F32), axis=0, keepdims=True)
    copy_back.wait()
    copy_up.wait()
    grad_up = (dot_nt(grad_down, w_back_v[...]) * gelu_slope(up_ref[...])).astype(BF16)
    late_out[:, :ff_dim] = grad_up
    late_out[:, ff_dim : ff_dim + feature_dim] = grad_down
    copy_in.wait()
    grad_normed = grad_pre_ffn + dot_nt(grad_up, w_in_v[...])
    grad_pre_attn, grad_ga, grad_sa = layer_norm_back(pre_attn_ref[...], row_of(ga), grad_normed)
    vec_out[3:4, :] = grad_ga
    vec_out[4:5, :] = grad_sa
    gpa_out[...] = grad_pre_attn
    grad_attended = grad_pre_attn.astype(BF16)
    late_out[:, ff_dim + feature_dim :] = grad_attended
    vec_out[5:6, :] = jnp.sum(grad_attended.astype(F32), axis=0, keepdims=True)
    copy_out.wait()
    gctx_out[...] = dot_nt(grad_attended, wo[...]).astype(BF16)


def middle(idx, own, other, positives, pre_attn, up, pre_ffn, w_back, w_in, wo, ga, gf):
    far, cls, feature_dim = own[0].shape
    ff_dim = w_in.shape[1]
    places = far * GROUP
    count = places * cls
    shapes = (
        ((cls, count), F32),
        ((1, count), F32),
        ((cls, ff_dim + 2 * feature_dim), BF16),
        ((cls, feature_dim), BF16),
        ((cls, feature_dim), F32),
        ((8, feature_dim), F32),
    )
    smalls = (positives, pre_attn, pre_ffn, ga, gf)
    return pl.pallas_call(
        middle_kernel,
        in_specs=[pl.BlockSpec(memory_space=pltpu.SMEM)]
        + [ANY] * (2 * GROUP)
        + [full(a.shape) for a in smalls]
        + [ANY] * 4,
        out_specs=[full(s) for s, _ in shapes],
        out_shape=[jax.ShapeDtypeStruct(s, d) for s, d in shapes],
        grid=(1,),
        scratch_shapes=[
            pltpu.VMEM((2, places, cls, feature_dim), BF16),
            pltpu.VMEM(w_in.shape, BF16),
            pltpu.VMEM(w_back.shape, BF16),
            pltpu.VMEM(up.shape, F32),
            pltpu.VMEM(wo.shape, BF16),
            pltpu.SemaphoreType.DMA((2 * places,)),
            pltpu.SemaphoreType.DMA((4,)),
        ],
        compiler_params=pltpu.CompilerParams(vmem_limit_bytes=56 * 1024 * 1024),
        cost_estimate=pl.CostEstimate(
            flops=2 * count * count * feature_dim, bytes_accessed=20_000_000, transcendentals=count * count
        ),
        name="loss",
    )(idx, *own, *other, *smalls, w_back, w_in, up, wo)


def spread_rows(shape, sizes, strides, masks, dim=0):
    rest = iota(shape, dim)
    total = jnp.zeros(shape, jnp.int32)
    for size, stride, mask in zip(reversed(sizes), reversed(strides), reversed(masks)):
        above = jnp.floor((rest.astype(F32) + 0.5) * (1.0 / size)).astype(jnp.int32)
        digit = rest - above * size
        total = total + (digit ^ mask) * stride
        rest = above
    return total


def attn_back_kernel(
    idx_ref, seg_ref, qc_ref, gctx_ref, gpa_ref, vec_ref, x_hbm, k_hbm, v_hbm, wq_hbm, wk_hbm, wv_hbm,
    back_hbm, send_hbm, keep_hbm,
    x_s, k_s, v_s, wq, wk, wv, mixed_s, back_s, send_s, keep_s, sems, out_sems,
):
    tower, place = idx_ref[0], idx_ref[1]
    towers = 2
    rows, length, feature_dim = x_s.shape
    head_count = feature_dim // HEAD_DIM
    pairs = []
    for row in range(rows):
        pairs += [(k_hbm.at[row], k_s.at[row]), (v_hbm.at[row], v_s.at[row]), (x_hbm.at[row], x_s.at[row])]
    pairs += [(wq_hbm, wq), (wk_hbm, wk), (wv_hbm, wv)]
    wait = loads(pairs, sems)
    mask = head_mask(head_count, SEGS, feature_dim)
    scale = HEAD_DIM**-0.5
    shape = (feature_dim, feature_dim)
    wide = head_count * SEGS
    far, block = keep_s.shape[1:3]
    source = spread_rows(
        (1, feature_dim),
        (towers, GROUP, far, block),
        (far * GROUP * block, block, GROUP * block, 1),
        (tower, place & (GROUP - 1), place // GROUP, 0),
        1,
    )
    order = jnp.where(iota(shape, 0) == source, 1.0, 0.0).astype(BF16)
    scatters, wides, drawn, drawn_cls, grads_q, biases = [], [], [], [], [], []
    for row in range(rows):
        here = slice(row * SEGS, (row + 1) * SEGS)
        seg_row = seg_ref[0, row : row + 1, :]
        query_wide = block_heads((qc_ref[here, :] * scale).astype(BF16), mask, head_count)
        gctx_wide = block_heads(gctx_ref[here, :], mask, head_count)
        wait(3 * row)
        key_row = k_s[row]
        probs = cls_probs(query_wide, key_row, seg_row, head_count, SEGS)
        wait(3 * row + 1)
        grad_probs = dot_nt(gctx_wide, v_s[row])
        inner = jnp.sum(probs * grad_probs, axis=1, keepdims=True)
        grad_logits = (probs * (grad_probs - inner)).astype(BF16)
        grad_query = heads_to_rows(dot_nn(grad_logits, key_row), mask, head_count, SEGS)
        grad_query = (grad_query * scale).astype(BF16)
        mixed = jnp.concatenate([grad_logits, probs.astype(BF16)], axis=0)
        mixed_s[row] = mixed
        wait(3 * row + 2)
        x = x_s[row]
        first = jnp.where(cls_onehot(seg_row, SEGS), 1.0, 0.0).astype(BF16)
        drawn.append(dot_nn(mixed, x).astype(BF16))
        drawn_cls.append(dot_nn(first, x).astype(BF16))
        grads_q.append(grad_query)
        bias_of_value = jnp.sum(
            gctx_wide.astype(F32) * jnp.sum(mixed[wide:].astype(F32), axis=1, keepdims=True),
            axis=0, keepdims=True,
        )
        biases.append((jnp.sum(grad_query.astype(F32), axis=0, keepdims=True), bias_of_value))
        if row == 0:
            wait(3 * rows)
        cls_back = gpa_ref[here, :] + dot_nt(grad_query, wq[...])
        scatters.append((jnp.concatenate([first] * 3, axis=0), jnp.concatenate(split(cls_back), axis=0)))
        wides.append((query_wide, gctx_wide))
    def over_rows(parts):
        return jnp.concatenate(parts, axis=0)

    turned_k = dot_nn(over_rows([part[:wide] for part in drawn]), order).astype(BF16)
    turned_v = dot_nn(over_rows([part[wide:] for part in drawn]), order).astype(BF16)
    turned_cls = dot_nn(over_rows(drawn_cls), order).astype(BF16)
    acc_q = dot_tn(turned_cls, over_rows(grads_q))
    acc_k = dot_tn(turned_k, over_rows([pair[0] for pair in wides]))
    acc_v = dot_tn(turned_v, over_rows([pair[1] for pair in wides]))
    bias_q, bias_v = biases[0]
    for more in biases[1:]:
        bias_q, bias_v = bias_q + more[0], bias_v + more[1]
    vectors = jnp.concatenate(
        [vec_ref[0:6, :], bias_q, bias_v, jnp.zeros((LANES - 8, feature_dim), F32)], axis=0
    )
    high, second, third = split(vectors)
    columns = (dot_nn(high, order) + (dot_nn(second, order) + dot_nn(third, order))).T
    half = feature_dim // towers
    place_at = 0
    for grad in (acc_q, acc_k, acc_v, columns):
        lanes = slice(place_at, place_at + grad.shape[1])
        cut = (GROUP, far, block, grad.shape[1])
        keep_s[:, :, :, lanes] = grad[:half].astype(BF16).reshape(cut)
        send_s[:, :, :, lanes] = grad[half:].astype(BF16).reshape(cut)
        place_at = lanes.stop
    copies = [
        pltpu.make_async_copy(send_s, send_hbm, out_sems.at[0]),
        pltpu.make_async_copy(keep_s, keep_hbm, out_sems.at[1]),
    ]
    for copy in copies:
        copy.start()
    wait(3 * rows + 1)
    wait(3 * rows + 2)
    part = length // 4
    for row in range(rows):
        first, pieces = scatters[row]
        query_wide, gctx_wide = wides[row]
        spread = jnp.concatenate(
            [dot_nt(query_wide, wk[...]).astype(BF16), dot_nt(gctx_wide, wv[...]).astype(BF16)], axis=0
        )
        for start in range(0, length, part):
            here = slice(start, start + part)
            back = dot_tn(mixed_s[row, :, here], spread)
            back_s[row, here, :] = back + dot_tn(first[:, here], pieces)
            copy = pltpu.make_async_copy(
                back_s.at[row, pl.ds(start, part)],
                back_hbm.at[row, pl.ds(start, part)],
                out_sems.at[len(copies)],
            )
            copy.start()
            copies.append(copy)
    for copy in copies:
        copy.wait()


def attn_back(idx, segs, qc, gctx, gpa, vectors, x_rows, keys, values, wq, wk, wv, places):
    rows, length, feature_dim = x_rows.shape
    block = feature_dim // (2 * places)
    half = (GROUP, places // GROUP, block, 3 * feature_dim + LANES)
    shapes = (((rows, length, feature_dim), F32), (half, BF16), (half, BF16))
    smalls = (segs, qc, gctx, gpa, vectors)
    square = pltpu.VMEM((feature_dim, feature_dim), BF16)
    whole = pltpu.VMEM((rows, length, feature_dim), BF16)
    return pl.pallas_call(
        attn_back_kernel,
        grid=(1,),
        in_specs=[pl.BlockSpec(memory_space=pltpu.SMEM)]
        + [full(a.shape) for a in smalls]
        + [ANY] * 6,
        out_specs=[ANY] * 3,
        out_shape=[jax.ShapeDtypeStruct(s, d) for s, d in shapes],
        scratch_shapes=[whole, whole, whole, square, square, square]
        + [
            pltpu.VMEM((rows, 2 * feature_dim // HEAD_DIM * SEGS, length), BF16),
            pltpu.VMEM((rows, length, feature_dim), F32),
            pltpu.VMEM(half, BF16),
            pltpu.VMEM(half, BF16),
            pltpu.SemaphoreType.DMA((3 * rows + 3,)),
            pltpu.SemaphoreType.DMA((2 + 4 * rows,)),
        ],
        compiler_params=pltpu.CompilerParams(vmem_limit_bytes=56 * 1024 * 1024),
        cost_estimate=pl.CostEstimate(
            flops=2 * rows * length * feature_dim * feature_dim * 6,
            bytes_accessed=30_000_000,
            transcendentals=rows * length * 384,
        ),
        name="attention_back",
    )(idx, *smalls, x_rows, keys, values, wq, wk, wv)


def weights_kernel(feature_dim, ff_dim, idx_ref, *refs):
    early = refs[:GROUP]
    late = refs[GROUP : 2 * GROUP]
    keep_out, send_out = refs[2 * GROUP :]
    tower, place = idx_ref[0], idx_ref[1]
    _, pairs, block, _ = send_out.shape
    far = 2 * pairs
    pieces = ff_dim // feature_dim
    fill = early[0].shape[1] - 2 * feature_dim

    def pick(group, near, columns):
        source = spread_rows(
            (2 * far * block, 1),
            (2, 2, pairs, block),
            (far * group, group, 2 * group, 1),
            (tower, place // GROUP & 1, place // (2 * GROUP), 0),
        )
        shape = (2 * far * block, columns)
        return jnp.where(iota(shape, 1) == source + near, 1.0, 0.0).astype(BF16)

    def stacked(parts, first, columns):
        return jnp.concatenate([ref[:, first : first + columns] for ref in parts], axis=0)

    def put(first, grad):
        columns = grad.shape[1]
        half = far * block
        shape = (2, pairs, block, columns)
        keep_out[:, :, :, first : first + columns] = grad[:half].astype(BF16).reshape(shape)
        send_out[:, :, :, first : first + columns] = grad[half:].astype(BF16).reshape(shape)

    near = place & (GROUP - 1)
    narrow = pick(GROUP * block, near * block, feature_dim)
    grad_up = stacked(late, 0, ff_dim)
    grad_down = stacked(late, ff_dim, feature_dim)
    grad_attended = stacked(late, ff_dim + feature_dim, feature_dim)
    active = stacked(early, 0, fill)
    normed = dot_nt(narrow, stacked(early, fill, feature_dim)).astype(BF16)
    context = dot_nt(narrow, stacked(early, fill + feature_dim, feature_dim)).astype(BF16)
    put(0, dot_nn(normed, grad_up))
    for piece in range(pieces):
        if fill == ff_dim:
            chosen = pick(GROUP * pieces * block, (near * pieces + piece) * block, fill)
        else:
            chosen = pick(LANES, piece * block, fill)
        turned = dot_nt(chosen, active).astype(BF16)
        put(ff_dim + piece * feature_dim, dot_nn(turned, grad_down))
    put(2 * ff_dim, dot_nn(context, grad_attended))
    bias = jnp.sum(grad_up.astype(F32), axis=0, keepdims=True)
    shifted = [
        jnp.concatenate([bias[:, piece * block :], bias[:, : piece * block]], axis=1)
        for piece in range(1, pieces)
    ]
    stack = jnp.concatenate([bias, *shifted, jnp.zeros((LANES - pieces, ff_dim), F32)], axis=0)
    high, second, third = split(stack)
    chosen = pick(GROUP * pieces * block, near * pieces * block, ff_dim)
    columns = dot_nt(chosen, high) + (dot_nt(chosen, second) + dot_nt(chosen, third))
    put(2 * ff_dim + feature_dim, columns)


def weights(idx, early, late, places, feature_dim, ff_dim):
    far = places // GROUP
    block = feature_dim // (2 * places)
    packed = 2 * ff_dim + feature_dim + LANES
    half = (2, far // 2, block, packed)
    return pl.pallas_call(
        functools.partial(weights_kernel, feature_dim, ff_dim),
        grid=(1,),
        in_specs=[pl.BlockSpec(memory_space=pltpu.SMEM)] + [full(a.shape) for a in (*early, *late)],
        out_specs=[full(half), full(half)],
        out_shape=[jax.ShapeDtypeStruct(half, BF16), jax.ShapeDtypeStruct(half, BF16)],
        compiler_params=pltpu.CompilerParams(vmem_limit_bytes=24 * 1024 * 1024),
        cost_estimate=pl.CostEstimate(
            flops=50_000_000_000, bytes_accessed=14_000_000, transcendentals=0
        ),
        name="weight_grads",
    )(idx, *early, *late)


def tied(*values):
    return lax.optimization_barrier(values)


def on_device(
    hidden_in, segment_ids, positives, w_query, b_query, w_key, w_value, b_value, w_out, b_out,
    gain_attn, shift_attn, w_in, b_in, w_back, b_back, gain_ffn, shift_ffn,
):
    feature_dim = hidden_in.shape[2]
    ff_dim = w_in.shape[1]
    rows, length = segment_ids.shape[1], segment_ids.shape[2]
    places = lax.axis_size("dp")
    far = places // GROUP
    tower, place = lax.axis_index("tower"), lax.axis_index("dp")
    idx = jnp.stack([tower, place, places]).astype(jnp.int32)
    x_rows = hidden_in.reshape(rows, length, feature_dim)
    keys, values, *pack, query_cls, pre_attn, up, pre_ffn, enc_cls, hot = front(
        places, idx, segment_ids,
        (b_query, b_value, b_out, gain_attn, shift_attn, b_in, b_back, gain_ffn, shift_ffn),
        x_rows, (w_key, w_value, w_query, w_out, w_in, w_back),
    )
    mats = (w_query, w_out, w_in, w_back)
    smalls = (b_query, b_out, gain_attn, shift_attn, b_in, b_back, gain_ffn, shift_ffn)

    def encode(part, before):
        return encode_part(part, 2 * rows, x_rows, keys, values, hot, mats, smalls, before)

    along = [moved(enc_cls, "dp", GROUP * m) for m in range(1, far)]
    early = [pack[0]] + [moved(pack[m], "dp", m) for m in range(1, GROUP)]
    encoded = encode(0, None)
    along, early[1:3], encoded = tied(along, early[1:3], encoded)
    own, encoded = tied(jnp.stack([enc_cls] + list(along)), encoded)
    crossed = [moved(own, "dp", m) for m in range(1, GROUP)]
    encoded = encode(1, encoded)
    crossed, encoded = tied(crossed, encoded)
    own = [own] + list(crossed)
    other = [moved(quad, "tower", 1) for quad in own]
    scores, losses, late_own, gctx, gpa, vec_mid = middle(
        idx, own, other, positives.reshape(1, -1), pre_attn, up, pre_ffn, w_back, w_in,
        w_out, gain_attn, gain_ffn,
    )
    gctx, early = tied(gctx, early)
    late = [late_own] + [moved(late_own, "dp", m) for m in range(1, GROUP)]
    back, send, keep = attn_back(
        idx, segment_ids, query_cls, gctx, gpa, vec_mid, x_rows, keys, values,
        w_query, w_key, w_value, places,
    )
    late, keep = tied(late, keep)
    send = moved(send, "tower", 1)
    weight_keep, weight_send = weights(idx, early, late, places, feature_dim, ff_dim)
    send, weight_keep, weight_send = tied(send, weight_keep, weight_send)
    paired = [keep[m].astype(F32) + send[m].astype(F32) for m in range(GROUP)]
    near_out = [part.astype(BF16) for part in paired[1:]]
    near_out, weight_keep, weight_send = tied(near_out, weight_keep, weight_send)
    weight_send = moved(weight_send, "tower", 1)
    near_sent = [moved(near_out[m - 1], "dp", m) for m in range(1, GROUP)]
    weight_out = (weight_keep[1].astype(F32) + weight_send[1].astype(F32)).astype(BF16)
    weight_out, encoded = tied(weight_out, encoded)
    reach, arrived = 1, moved(weight_out, "dp", GROUP)
    encoded = encode(2, encoded)
    arrived, encoded = tied(arrived, encoded)
    weight_sum = weight_keep[0].astype(F32) + weight_send[0].astype(F32) + arrived.astype(F32)
    near_sent, weight_sum, encoded = tied(near_sent, weight_sum, encoded)
    near = paired[0]
    for part in near_sent:
        near = near + part.astype(F32)
    far_out = [near[m].astype(BF16) for m in range(1, far)]
    while weight_sum.shape[0] > 1:
        reach = reach * 2
        half = weight_sum.reshape(weight_sum.shape[0] // 2, 2, *weight_sum.shape[1:])
        weight_out = half[:, 1].astype(BF16)
        last = reach == far // 2
        if last:
            far_out, weight_out, encoded = tied(far_out, weight_out, encoded)
            far_sent = [moved(far_out[m - 1], "dp", GROUP * m) for m in range(1, far)]
        arrived = moved(weight_out, "dp", GROUP * reach)
        if last:
            encoded = encode(3, encoded)
            far_sent, arrived, encoded = tied(far_sent, arrived, encoded)
        weight_sum = half[:, 0] + arrived.astype(F32)
    weight_sum = weight_sum[0]
    grad_qkv = near[0]
    for part in far_sent:
        grad_qkv = grad_qkv + part.astype(F32)
    grad_in = weight_sum[:, :ff_dim]
    grad_back = jnp.concatenate(
        [
            weight_sum[:, first : first + feature_dim]
            for first in range(ff_dim, 2 * ff_dim, feature_dim)
        ],
        axis=0,
    )
    grad_out = weight_sum[:, 2 * ff_dim : 2 * ff_dim + feature_dim]
    first = 2 * ff_dim + feature_dim
    b_i = weight_sum[:, first : first + ff_dim // feature_dim].T.reshape(-1)
    columns = grad_qkv[:, 3 * feature_dim : 3 * feature_dim + 8].T
    g_f, s_f, b_b, g_a, s_a, b_o, b_q, b_v = [columns[i] for i in range(8)]
    return (
        encoded.reshape(hidden_in.shape),
        scores.T,
        losses.reshape(-1),
        back.reshape(hidden_in.shape),
        grad_qkv[:, :feature_dim],
        b_q,
        grad_qkv[:, feature_dim : 2 * feature_dim],
        grad_qkv[:, 2 * feature_dim : 3 * feature_dim],
        b_v,
        grad_out,
        b_o,
        g_a,
        s_a,
        grad_in,
        b_i,
        grad_back,
        b_b,
        g_f,
        s_f,
    )


def solution(mesh):
    placed = (P("tower", "dp", None), P("tower", "dp", None)) + (P(),) * 16
    matrix, vector = P(("tower", "dp"), None), P(("tower", "dp"))
    return jax.shard_map(
        on_device,
        mesh=mesh,
        in_specs=placed,
        out_specs=(
            P("tower", "dp", None),
            P(None, "dp"),
            P(),
            P("tower", "dp", None),
            matrix,
            vector,
            matrix,
            matrix,
            vector,
            matrix,
            vector,
            vector,
            vector,
            matrix,
            vector,
            matrix,
            vector,
            vector,
            vector,
        ),
        check_vma=False,
    )
```

```python
import functools

import jax
import jax.numpy as jnp
from jax import lax
from jax.experimental import pallas as pl
from jax.experimental.pallas import tpu as pltpu
from jax.sharding import PartitionSpec as P

HEAD_DIM = 64
SEGS = 32
GROUP = 4
LANES = 128
FAR = float(2**30)
VMEM_BYTES = 60 * 1024 * 1024
F32 = jnp.float32
BF16 = jnp.bfloat16


def moved(value, axis, mask):
    pairs = [(source, source ^ mask) for source in range(lax.axis_size(axis))]
    return lax.ppermute(value, axis, pairs)


def dot_nn(a, b):
    return lax.dot_general(a, b, (((1,), (0,)), ((), ())), preferred_element_type=F32)


def dot_nt(a, b):
    return lax.dot_general(a, b, (((1,), (1,)), ((), ())), preferred_element_type=F32)


def dot_tn(a, b):
    return lax.dot_general(a, b, (((0,), (0,)), ((), ())), preferred_element_type=F32)


def iota(shape, dim):
    return lax.broadcasted_iota(jnp.int32, shape, dim)


def row_of(ref):
    return ref[...].astype(F32).reshape(1, -1)


def norm_parts(values):
    average = jnp.mean(values, axis=-1, keepdims=True)
    centered = values - average
    spread = jnp.mean(centered * centered, axis=-1, keepdims=True)
    inverse = lax.rsqrt(spread + 1e-12)
    return centered * inverse, inverse


def layer_norm(values, gain, shift):
    scaled, _ = norm_parts(values)
    return scaled * gain + shift


def layer_norm_back(values, gain, grad):
    scaled, inverse = norm_parts(values)
    inner = grad * gain
    mean_inner = jnp.mean(inner, axis=-1, keepdims=True)
    mean_scaled = jnp.mean(inner * scaled, axis=-1, keepdims=True)
    back = inverse * (inner - mean_inner - scaled * mean_scaled)
    return back, jnp.sum(grad * scaled, axis=0, keepdims=True), jnp.sum(grad, axis=0, keepdims=True)


def phi_of(values):
    return 0.5 * (1.0 + lax.erf(values * (2.0**-0.5)))


def gelu_exact(values):
    return values * phi_of(values)


def gelu_slope(values):
    bell = jnp.exp(-0.5 * values * values) * 0.3989422804014327
    return phi_of(values) + values * bell


def head_mask(head_count, segs, feature_dim):
    head_row = iota((head_count * segs, 1), 0) >> (segs.bit_length() - 1)
    head_col = iota((1, feature_dim), 1) >> (HEAD_DIM.bit_length() - 1)
    return jnp.where(head_row == head_col, 1.0, 0.0)


def block_heads(rows, mask, head_count):
    return jnp.concatenate([rows] * head_count, axis=0) * mask.astype(BF16)


def heads_to_rows(wide, mask, head_count, segs):
    kept = wide * mask
    total = kept[:segs]
    for head in range(1, head_count):
        total = total + kept[head * segs : (head + 1) * segs]
    return total


def split(values):
    high = values.astype(BF16)
    rest = values - high.astype(F32)
    second = rest.astype(BF16)
    return high, second, (rest - second.astype(F32)).astype(BF16)


def cls_onehot(seg_row, segs):
    shape = (segs, seg_row.shape[1])
    before = (seg_row < iota(shape, 0)).astype(F32)
    starts = jnp.sum(before, axis=1, keepdims=True).astype(jnp.int32)
    return iota(shape, 1) == starts


def cls_probs(query_wide, key_row, seg_row, head_count, segs):
    logits = dot_nt(query_wide, key_row)
    member = jnp.where(seg_row == iota((segs, seg_row.shape[1]), 0), 1.0, 0.0)
    member = jnp.concatenate([member] * head_count, axis=0)
    logits = jnp.where(member > 0.5, logits, -1000000000.0)
    top = jnp.max(logits, axis=1, keepdims=True)
    exponent = jnp.exp(logits - top)
    return exponent * (1.0 / jnp.sum(exponent, axis=1, keepdims=True))


def loads(pairs, sems):
    copies = [
        pltpu.make_async_copy(source, target, sems.at[index])
        for index, (source, target) in enumerate(pairs)
    ]
    for copy in copies:
        copy.start()
    return lambda index: copies[index].wait()


def front_kernel(
    idx_ref, seg_ref, bq, bv, bo, ga, sa, b_in, bb, gf, sf,
    x_hbm, wk_hbm, wv_hbm, wq_hbm, wo_hbm, w_in_hbm, w_back_hbm,
    k_hbm, v_hbm, pack_0, pack_1, pack_2, pack_3, qc_out, pre_attn_out, up_out, pre_ffn_out, enc_out, hot_out,
    x_s, wk, wv, wq, wo, w_in_v, w_back_v, k_s, v_s, sems, out_sems,
):
    rows, length, feature_dim = x_s.shape
    ff_dim = w_in_v.shape[1]
    head_count = feature_dim // HEAD_DIM
    wait = loads(
        [(x_hbm.at[0], x_s.at[0]), (wk_hbm, wk), (wv_hbm, wv), (wq_hbm, wq)]
        + [(x_hbm.at[row], x_s.at[row]) for row in range(1, rows)]
        + [(wo_hbm, wo), (w_in_hbm, w_in_v), (w_back_hbm, w_back_v)],
        sems,
    )
    mask = head_mask(head_count, SEGS, feature_dim)
    contexts, firsts, copies = [], [], []
    for row in range(rows):
        if row == 0:
            for index in range(3):
                wait(index)
        else:
            wait(3 + row)
        x = x_s[row]
        key_row = dot_nn(x, wk[...]).astype(BF16)
        k_s[row] = key_row
        value_row = (dot_nn(x, wv[...]) + row_of(bv)).astype(BF16)
        v_s[row] = value_row
        for kept, target in ((k_s, k_hbm), (v_s, v_hbm)):
            copy = pltpu.make_async_copy(kept.at[row], target.at[row], out_sems.at[len(copies)])
            copy.start()
            copies.append(copy)
        if row == 0:
            wait(3)
        seg_row = seg_ref[0, row : row + 1, :]
        first = jnp.where(cls_onehot(seg_row, SEGS), 1.0, 0.0).astype(BF16)
        x_cls = dot_nn(first, x).astype(BF16)
        query_cls = (dot_nn(x_cls, wq[...]) + row_of(bq)).astype(BF16)
        query_wide = block_heads((query_cls * (HEAD_DIM**-0.5)).astype(BF16), mask, head_count)
        probs = cls_probs(query_wide, key_row, seg_row, head_count, SEGS)
        context = heads_to_rows(dot_nn(probs.astype(BF16), value_row), mask, head_count, SEGS)
        contexts.append(context.astype(BF16))
        firsts.append(x_cls)
        qc_out[row * SEGS : (row + 1) * SEGS, :] = query_cls
        hot = jnp.where(seg_row == iota((LANES, length), 0), 1.0, 0.0)
        hot_out[row] = hot.T.astype(BF16)
    for index in range(3 + rows, 6 + rows):
        wait(index)
    if True:
        context_all = jnp.concatenate(contexts, axis=0)
        x_all = jnp.concatenate(firsts, axis=0)
        pre_attn = x_all.astype(F32) + (dot_nn(context_all, wo[...]) + row_of(bo))
        pre_attn_out[...] = pre_attn
        normed = layer_norm(pre_attn, row_of(ga), row_of(sa)).astype(BF16)
        up = dot_nn(normed, w_in_v[...]) + row_of(b_in)
        up_out[...] = up
        active = gelu_exact(up).astype(BF16)
        pre_ffn = normed.astype(F32) + (dot_nn(active, w_back_v[...]) + row_of(bb))
        pre_ffn_out[...] = pre_ffn
        enc_out[...] = layer_norm(pre_ffn, row_of(gf), row_of(sf)).astype(BF16)
        packs = (pack_0, pack_1, pack_2, pack_3)
        fill = pack_0.shape[1] - 2 * feature_dim
        group = ff_dim * LANES // fill
        size = group // GROUP
        if fill == ff_dim:
            for near in range(GROUP):
                packs[near][:, :ff_dim] = active
        else:
            for slot in range(fill // LANES):
                blocks = [
                    active[:, slot * group + size * b : slot * group + size * (b + 1)]
                    for b in range(GROUP)
                ]
                lanes = slot * LANES
                for near in range(GROUP):
                    source = (idx_ref[1] & (GROUP - 1)) ^ near
                    chosen = blocks[0]
                    for b in range(1, GROUP):
                        chosen = jnp.where(source == b, blocks[b], chosen)
                    packs[near][:, lanes : lanes + size] = chosen
                    packs[near][:, lanes + size : lanes + LANES] = jnp.zeros(
                        (active.shape[0], LANES - size), BF16
                    )
        for near in range(GROUP):
            packs[near][:, fill : fill + feature_dim] = normed
            packs[near][:, fill + feature_dim :] = context_all
    for copy in copies:
        copy.wait()


def full(shape):
    zeros = (0,) * len(shape)
    return pl.BlockSpec(shape, lambda *_: zeros)


ANY = pl.BlockSpec(memory_space=pl.ANY)


def active_width(places, ff_dim):
    group = GROUP * ff_dim // (2 * places)
    return ff_dim // group * LANES if group % LANES == 0 else ff_dim


def front(places, idx, segs, smalls, x_rows, mats):
    rows, length, feature_dim = x_rows.shape
    ff_dim = mats[-1].shape[0]
    cls = rows * SEGS
    shapes = (
        ((rows, length, feature_dim), BF16),
        ((rows, length, feature_dim), BF16),
        *(((cls, active_width(places, ff_dim) + 2 * feature_dim), BF16),) * GROUP,
        ((cls, feature_dim), BF16),
        ((cls, feature_dim), F32),
        ((cls, ff_dim), F32),
        ((cls, feature_dim), F32),
        ((cls, feature_dim), BF16),
        ((rows, length, LANES), BF16),
    )
    whole = pltpu.VMEM((rows, length, feature_dim), BF16)
    return pl.pallas_call(
        front_kernel,
        grid=(1,),
        in_specs=[pl.BlockSpec(memory_space=pltpu.SMEM)]
        + [full(a.shape) for a in (segs, *smalls)]
        + [ANY] * (1 + len(mats)),
        out_specs=[ANY, ANY] + [full(s) for s, _ in shapes[2:]],
        out_shape=[jax.ShapeDtypeStruct(s, d) for s, d in shapes],
        scratch_shapes=[whole]
        + [pltpu.VMEM(a.shape, BF16) for a in mats]
        + [
            whole,
            whole,
            pltpu.SemaphoreType.DMA((6 + rows,)),
            pltpu.SemaphoreType.DMA((2 * rows,)),
        ],
        compiler_params=pltpu.CompilerParams(vmem_limit_bytes=VMEM_BYTES),
        cost_estimate=pl.CostEstimate(
            flops=2 * rows * length * feature_dim * feature_dim * 3,
            bytes_accessed=30_000_000,
            transcendentals=rows * length * 384,
        ),
        name="front",
    )(idx, segs, *smalls, x_rows, *mats)


def segments_of(start, stop, length):
    found = []
    while start < stop:
        row, first = start // length, start % length
        tokens = min(stop - start, length - first)
        held = min(length, tokens + 128)
        found.append((row, first, tokens, max(0, min(first - 64, length - held)), held))
        start += tokens
    return found


def encode_kernel_at(
    segments, x_hbm, k_hbm, v_hbm, hot_hbm, wq_hbm, wo_hbm, w_in_hbm, w_back_hbm,
    bq, bo, ga, sa, b_in, bb, gf, sf, *refs
):
    enc_hbm, x_s, k_s, v_s, hot_s, enc_s, wq, wo, w_in, w_back, sems, out_sems = refs[-12:]
    feature_dim = x_s.shape[1]
    length = k_hbm.shape[1]
    ff_dim = w_in.shape[1]
    part, window = 128, 256
    count = len(segments)
    first_pairs, key_pairs, places, token_at, held_at = [], [], [], 0, 0
    for row, first, tokens, low, held in segments:
        near, kept = pl.ds(low, held), pl.ds(held_at, held)
        first_pairs.append((x_hbm.at[row, pl.ds(first, tokens)], x_s.at[pl.ds(token_at, tokens)]))
        key_pairs += [
            (hot_hbm.at[row, near], hot_s.at[kept]),
            (k_hbm.at[row, near], k_s.at[kept]),
            (v_hbm.at[row, near], v_s.at[kept]),
        ]
        places.append((token_at, held_at))
        token_at, held_at = token_at + tokens, held_at + held
    tail = [(wo_hbm, wo), (w_in_hbm, w_in), (w_back_hbm, w_back)]
    wait = loads([*first_pairs, (wq_hbm, wq), *key_pairs, *tail], sems)
    for index in range(count + 1):
        wait(index)
    x = x_s[...]
    query = ((dot_nn(x, wq[...]) + row_of(bq)).astype(BF16) * (HEAD_DIM**-0.5)).astype(BF16)
    left = iota((part, 128), 1) < HEAD_DIM
    for index in range(count + 1, 4 * count + 1):
        wait(index)
    contexts = []
    blocks = [
        (at + sub, first + sub, held_at - low)
        for (_, first, tokens, low, _), (at, held_at) in zip(segments, places)
        for sub in range(0, tokens, part)
    ]
    for at, base, shift in blocks:
        start = max(0, min(base - 64, length - window)) + shift
        keys = k_s[start : start + window, :]
        values = v_s[start : start + window, :]
        apart = ((hot_s[start : start + window, :].astype(F32) - 1.0) * FAR).astype(BF16)
        hot_query = hot_s[base + shift : base + shift + part, :]
        pieces = []
        for pair in range(feature_dim // 128):
            lanes = slice(pair * 128, pair * 128 + 128)
            both = query[at : at + part, lanes]
            zero = jnp.zeros_like(both)
            wide = jnp.concatenate(
                [
                    jnp.concatenate([jnp.where(left, both, zero), hot_query], axis=1),
                    jnp.concatenate([jnp.where(left, zero, both), hot_query], axis=1),
                ],
                axis=0,
            )
            logits = dot_nt(wide, jnp.concatenate([keys[:, lanes], apart], axis=1))
            top = jnp.max(logits, axis=1, keepdims=True)
            exponent = jnp.exp(logits - top)
            total = jnp.sum(exponent, axis=1, keepdims=True)
            out = dot_nn(exponent.astype(BF16), values[:, lanes]) * (1.0 / total)
            pieces.append(jnp.where(left, out[:part], out[part:]).astype(BF16))
        contexts.append(jnp.concatenate(pieces, axis=1))
    context = jnp.concatenate(contexts, axis=0)
    wait(4 * count + 1)
    pre_attn = x.astype(F32) + (dot_nn(context, wo[...]) + row_of(bo))
    normed = layer_norm(pre_attn, row_of(ga), row_of(sa)).astype(BF16)
    wait(4 * count + 2)
    wait(4 * count + 3)
    bias_in = row_of(b_in)
    total = normed.astype(F32) + row_of(bb)
    chunk = 768
    for start in range(0, ff_dim, chunk):
        cols = slice(start, start + chunk)
        up = dot_nn(normed, w_in[:, cols]) + bias_in[:, cols]
        total = total + dot_nn(gelu_exact(up).astype(BF16), w_back[cols, :])
    enc_s[...] = layer_norm(total, row_of(gf), row_of(sf)).astype(BF16)
    copies = [
        pltpu.make_async_copy(
            enc_s.at[pl.ds(at, tokens)], enc_hbm.at[row, pl.ds(first, tokens)], out_sems.at[index]
        )
        for index, ((row, first, tokens, _, _), (at, _)) in enumerate(zip(segments, places))
    ]
    for copy in copies:
        copy.start()
    for copy in copies:
        copy.wait()


def encode_part(start, stop, x_rows, keys, values, hot, mats, smalls, before):
    rows, length, feature_dim = x_rows.shape
    segments = segments_of(start, stop, length)
    tokens, held = stop - start, sum(segment[4] for segment in segments)
    extra = [] if before is None else [before]
    return pl.pallas_call(
        functools.partial(encode_kernel_at, segments),
        grid=(1,),
        in_specs=[ANY] * (4 + len(mats)) + [full(a.shape) for a in smalls] + [ANY for _ in extra],
        out_specs=ANY,
        out_shape=jax.ShapeDtypeStruct((rows, length, feature_dim), BF16),
        input_output_aliases={} if before is None else {4 + len(mats) + len(smalls): 0},
        scratch_shapes=[
            pltpu.VMEM((tokens, feature_dim), BF16),
            pltpu.VMEM((held, feature_dim), BF16),
            pltpu.VMEM((held, feature_dim), BF16),
            pltpu.VMEM((held, hot.shape[2]), BF16),
            pltpu.VMEM((tokens, feature_dim), BF16),
        ]
        + [pltpu.VMEM(a.shape, BF16) for a in mats]
        + [
            pltpu.SemaphoreType.DMA((4 * len(segments) + 4,)),
            pltpu.SemaphoreType.DMA((len(segments),)),
        ],
        compiler_params=pltpu.CompilerParams(vmem_limit_bytes=56 * 1024 * 1024),
        cost_estimate=pl.CostEstimate(
            flops=tokens * feature_dim * feature_dim, bytes_accessed=1_000_000, transcendentals=0
        ),
        name="encode_part",
    )(x_rows, keys, values, hot, *mats, *smalls, *extra)


def middle_kernel(
    idx_ref, *refs
):
    own = refs[:GROUP]
    other = refs[GROUP : 2 * GROUP]
    (
        positives, pre_attn_ref, pre_ffn_ref, ga, gf, w_back_hbm, w_in_hbm, up_hbm, wo_hbm,
        scores_out, losses_out, late_out, gctx_out, gpa_out, vec_out,
        both, w_in_v, w_back_v, up_ref, wo, sems, wsems,
    ) = refs[2 * GROUP :]
    tower, place = idx_ref[0], idx_ref[1]
    far, cls, feature_dim = own[0].shape
    ff_dim = w_in_v.shape[1]
    copy_back = pltpu.make_async_copy(w_back_hbm, w_back_v, wsems.at[0])
    copy_in = pltpu.make_async_copy(w_in_hbm, w_in_v, wsems.at[1])
    copy_up = pltpu.make_async_copy(up_hbm, up_ref, wsems.at[2])
    copy_out = pltpu.make_async_copy(wo_hbm, wo, wsems.at[3])
    copies = []
    for side, group in ((tower, own), (1 - tower, other)):
        for near in range(GROUP):
            for slot in range(far):
                to = both.at[side, place ^ (slot * GROUP + near)]
                copies.append(
                    pltpu.make_async_copy(group[near].at[slot], to, sems.at[len(copies)])
                )
    for copy in copies:
        copy.start()
    copy_back.start()
    copy_up.start()
    copy_in.start()
    copy_out.start()
    for copy in copies:
        copy.wait()
    count = far * GROUP * cls
    scale = feature_dim**-0.5
    queries = both[0].reshape(count, feature_dim)
    positive_row = positives[...]
    block = min(count, max(64, (1 << 20) // count))

    def partial_of(first):
        passages = both[1, pl.ds(first // cls, block // cls)].reshape(block, feature_dim)
        scored = dot_nt(passages, queries) * scale
        top = jnp.max(scored, axis=0, keepdims=True)
        total = jnp.sum(jnp.exp(scored - top), axis=0, keepdims=True)
        hit = iota((block, count), 0) + first == positive_row
        return top, total, jnp.sum(jnp.where(hit, scored, 0.0), axis=0, keepdims=True)

    def joined(index, state):
        top, total, picked = partial_of(index * block)
        joint = jnp.maximum(state[0], top)
        return (
            joint,
            state[1] * jnp.exp(state[0] - joint) + total * jnp.exp(top - joint),
            state[2] + picked,
        )

    state = partial_of(0)
    if count // block > 1:
        state = lax.fori_loop(1, count // block, joined, state)
    row_log = state[0] + jnp.log(state[1])
    losses_out[...] = row_log - state[2]
    scores_out[...] = dot_nt(both[1, place], queries) * scale
    mine = both[tower, place]
    opposite = both[1 - tower].reshape(count, feature_dim)
    own_scores = dot_nt(mine, opposite) * scale
    own_top = jnp.max(own_scores, axis=1, keepdims=True)
    own_log = own_top + jnp.log(jnp.sum(jnp.exp(own_scores - own_top), axis=1, keepdims=True))
    lanes = iota((cls, count), 1)
    mine_index = iota((cls, count), 0) + place * cls
    spread_positive = jnp.broadcast_to(positive_row, (cls, count))
    own_positive = jnp.sum(
        jnp.where(lanes == mine_index, spread_positive.astype(F32), 0.0), axis=1, keepdims=True
    ).astype(jnp.int32)
    is_query = tower == 0
    log_used = jnp.where(is_query, jnp.broadcast_to(own_log, (cls, count)), row_log)
    hit_query = (lanes == own_positive).astype(F32)
    hit_passage = (spread_positive == mine_index).astype(F32)
    hit = jnp.where(is_query, hit_query, hit_passage)
    grad_scores = (jnp.exp(own_scores - log_used) - hit).astype(BF16)
    grad_cls = dot_nn(grad_scores, opposite) * scale
    grad_pre_ffn, grad_gf, grad_sf = layer_norm_back(pre_ffn_ref[...], row_of(gf), grad_cls)
    vec_out[0:1, :] = grad_gf
    vec_out[1:2, :] = grad_sf
    grad_down = grad_pre_ffn.astype(BF16)
    vec_out[2:3, :] = jnp.sum(grad_down.astype(F32), axis=0, keepdims=True)
    copy_back.wait()
    copy_up.wait()
    grad_up = (dot_nt(grad_down, w_back_v[...]) * gelu_slope(up_ref[...])).astype(BF16)
    late_out[:, :ff_dim] = grad_up
    late_out[:, ff_dim : ff_dim + feature_dim] = grad_down
    copy_in.wait()
    grad_normed = grad_pre_ffn + dot_nt(grad_up, w_in_v[...])
    grad_pre_attn, grad_ga, grad_sa = layer_norm_back(pre_attn_ref[...], row_of(ga), grad_normed)
    vec_out[3:4, :] = grad_ga
    vec_out[4:5, :] = grad_sa
    gpa_out[...] = grad_pre_attn
    grad_attended = grad_pre_attn.astype(BF16)
    late_out[:, ff_dim + feature_dim :] = grad_attended
    vec_out[5:6, :] = jnp.sum(grad_attended.astype(F32), axis=0, keepdims=True)
    copy_out.wait()
    gctx_out[...] = dot_nt(grad_attended, wo[...]).astype(BF16)


def middle(idx, own, other, positives, pre_attn, up, pre_ffn, w_back, w_in, wo, ga, gf):
    far, cls, feature_dim = own[0].shape
    ff_dim = w_in.shape[1]
    places = far * GROUP
    count = places * cls
    shapes = (
        ((cls, count), F32),
        ((1, count), F32),
        ((cls, ff_dim + 2 * feature_dim), BF16),
        ((cls, feature_dim), BF16),
        ((cls, feature_dim), F32),
        ((8, feature_dim), F32),
    )
    smalls = (positives, pre_attn, pre_ffn, ga, gf)
    return pl.pallas_call(
        middle_kernel,
        in_specs=[pl.BlockSpec(memory_space=pltpu.SMEM)]
        + [ANY] * (2 * GROUP)
        + [full(a.shape) for a in smalls]
        + [ANY] * 4,
        out_specs=[full(s) for s, _ in shapes],
        out_shape=[jax.ShapeDtypeStruct(s, d) for s, d in shapes],
        grid=(1,),
        scratch_shapes=[
            pltpu.VMEM((2, places, cls, feature_dim), BF16),
            pltpu.VMEM(w_in.shape, BF16),
            pltpu.VMEM(w_back.shape, BF16),
            pltpu.VMEM(up.shape, F32),
            pltpu.VMEM(wo.shape, BF16),
            pltpu.SemaphoreType.DMA((2 * places,)),
            pltpu.SemaphoreType.DMA((4,)),
        ],
        compiler_params=pltpu.CompilerParams(vmem_limit_bytes=56 * 1024 * 1024),
        cost_estimate=pl.CostEstimate(
            flops=2 * count * count * feature_dim, bytes_accessed=20_000_000, transcendentals=count * count
        ),
        name="loss",
    )(idx, *own, *other, *smalls, w_back, w_in, up, wo)


def spread_rows(shape, sizes, strides, masks, dim=0):
    rest = iota(shape, dim)
    total = jnp.zeros(shape, jnp.int32)
    for size, stride, mask in zip(reversed(sizes), reversed(strides), reversed(masks)):
        above = jnp.floor((rest.astype(F32) + 0.5) * (1.0 / size)).astype(jnp.int32)
        digit = rest - above * size
        total = total + (digit ^ mask) * stride
        rest = above
    return total


def attn_back_kernel(
    idx_ref, seg_ref, qc_ref, gctx_ref, gpa_ref, vec_ref, x_hbm, k_hbm, v_hbm, wq_hbm, wk_hbm, wv_hbm,
    back_hbm, send_hbm, keep_hbm,
    x_s, k_s, v_s, wq, wk, wv, mixed_s, back_s, send_s, keep_s, sems, out_sems,
):
    tower, place = idx_ref[0], idx_ref[1]
    towers = 2
    rows, length, feature_dim = x_s.shape
    head_count = feature_dim // HEAD_DIM
    pairs = []
    for row in range(rows):
        pairs += [(k_hbm.at[row], k_s.at[row]), (v_hbm.at[row], v_s.at[row]), (x_hbm.at[row], x_s.at[row])]
    pairs += [(wq_hbm, wq), (wk_hbm, wk), (wv_hbm, wv)]
    wait = loads(pairs, sems)
    mask = head_mask(head_count, SEGS, feature_dim)
    scale = HEAD_DIM**-0.5
    shape = (feature_dim, feature_dim)
    wide = head_count * SEGS
    far, block = keep_s.shape[1:3]
    source = spread_rows(
        (1, feature_dim),
        (towers, GROUP, far, block),
        (far * GROUP * block, block, GROUP * block, 1),
        (tower, place & (GROUP - 1), place // GROUP, 0),
        1,
    )
    order = jnp.where(iota(shape, 0) == source, 1.0, 0.0).astype(BF16)
    scatters, wides, drawn, drawn_cls, grads_q, biases = [], [], [], [], [], []
    for row in range(rows):
        here = slice(row * SEGS, (row + 1) * SEGS)
        seg_row = seg_ref[0, row : row + 1, :]
        query_wide = block_heads((qc_ref[here, :] * scale).astype(BF16), mask, head_count)
        gctx_wide = block_heads(gctx_ref[here, :], mask, head_count)
        wait(3 * row)
        key_row = k_s[row]
        probs = cls_probs(query_wide, key_row, seg_row, head_count, SEGS)
        wait(3 * row + 1)
        grad_probs = dot_nt(gctx_wide, v_s[row])
        inner = jnp.sum(probs * grad_probs, axis=1, keepdims=True)
        grad_logits = (probs * (grad_probs - inner)).astype(BF16)
        grad_query = heads_to_rows(dot_nn(grad_logits, key_row), mask, head_count, SEGS)
        grad_query = (grad_query * scale).astype(BF16)
        mixed = jnp.concatenate([grad_logits, probs.astype(BF16)], axis=0)
        mixed_s[row] = mixed
        wait(3 * row + 2)
        x = x_s[row]
        first = jnp.where(cls_onehot(seg_row, SEGS), 1.0, 0.0).astype(BF16)
        drawn.append(dot_nn(mixed, x).astype(BF16))
        drawn_cls.append(dot_nn(first, x).astype(BF16))
        grads_q.append(grad_query)
        bias_of_value = jnp.sum(
            gctx_wide.astype(F32) * jnp.sum(mixed[wide:].astype(F32), axis=1, keepdims=True),
            axis=0, keepdims=True,
        )
        biases.append((jnp.sum(grad_query.astype(F32), axis=0, keepdims=True), bias_of_value))
        if row == 0:
            wait(3 * rows)
        cls_back = gpa_ref[here, :] + dot_nt(grad_query, wq[...])
        scatters.append((jnp.concatenate([first] * 3, axis=0), jnp.concatenate(split(cls_back), axis=0)))
        wides.append((query_wide, gctx_wide))
    def over_rows(parts):
        return jnp.concatenate(parts, axis=0)

    turned_k = dot_nn(over_rows([part[:wide] for part in drawn]), order).astype(BF16)
    turned_v = dot_nn(over_rows([part[wide:] for part in drawn]), order).astype(BF16)
    turned_cls = dot_nn(over_rows(drawn_cls), order).astype(BF16)
    acc_q = dot_tn(turned_cls, over_rows(grads_q))
    acc_k = dot_tn(turned_k, over_rows([pair[0] for pair in wides]))
    acc_v = dot_tn(turned_v, over_rows([pair[1] for pair in wides]))
    bias_q, bias_v = biases[0]
    for more in biases[1:]:
        bias_q, bias_v = bias_q + more[0], bias_v + more[1]
    vectors = jnp.concatenate(
        [vec_ref[0:6, :], bias_q, bias_v, jnp.zeros((LANES - 8, feature_dim), F32)], axis=0
    )
    high, second, third = split(vectors)
    columns = (dot_nn(high, order) + (dot_nn(second, order) + dot_nn(third, order))).T
    half = feature_dim // towers
    place_at = 0
    for grad in (acc_q, acc_k, acc_v, columns):
        lanes = slice(place_at, place_at + grad.shape[1])
        cut = (GROUP, far, block, grad.shape[1])
        keep_s[:, :, :, lanes] = grad[:half].astype(BF16).reshape(cut)
        send_s[:, :, :, lanes] = grad[half:].astype(BF16).reshape(cut)
        place_at = lanes.stop
    copies = [
        pltpu.make_async_copy(send_s, send_hbm, out_sems.at[0]),
        pltpu.make_async_copy(keep_s, keep_hbm, out_sems.at[1]),
    ]
    for copy in copies:
        copy.start()
    wait(3 * rows + 1)
    wait(3 * rows + 2)
    part = length // 4
    for row in range(rows):
        first, pieces = scatters[row]
        query_wide, gctx_wide = wides[row]
        spread = jnp.concatenate(
            [dot_nt(query_wide, wk[...]).astype(BF16), dot_nt(gctx_wide, wv[...]).astype(BF16)], axis=0
        )
        for start in range(0, length, part):
            here = slice(start, start + part)
            back = dot_tn(mixed_s[row, :, here], spread)
            back_s[row, here, :] = back + dot_tn(first[:, here], pieces)
            copy = pltpu.make_async_copy(
                back_s.at[row, pl.ds(start, part)],
                back_hbm.at[row, pl.ds(start, part)],
                out_sems.at[len(copies)],
            )
            copy.start()
            copies.append(copy)
    for copy in copies:
        copy.wait()


def attn_back(idx, segs, qc, gctx, gpa, vectors, x_rows, keys, values, wq, wk, wv, places):
    rows, length, feature_dim = x_rows.shape
    block = feature_dim // (2 * places)
    half = (GROUP, places // GROUP, block, 3 * feature_dim + LANES)
    shapes = (((rows, length, feature_dim), F32), (half, BF16), (half, BF16))
    smalls = (segs, qc, gctx, gpa, vectors)
    square = pltpu.VMEM((feature_dim, feature_dim), BF16)
    whole = pltpu.VMEM((rows, length, feature_dim), BF16)
    return pl.pallas_call(
        attn_back_kernel,
        grid=(1,),
        in_specs=[pl.BlockSpec(memory_space=pltpu.SMEM)]
        + [full(a.shape) for a in smalls]
        + [ANY] * 6,
        out_specs=[ANY] * 3,
        out_shape=[jax.ShapeDtypeStruct(s, d) for s, d in shapes],
        scratch_shapes=[whole, whole, whole, square, square, square]
        + [
            pltpu.VMEM((rows, 2 * feature_dim // HEAD_DIM * SEGS, length), BF16),
            pltpu.VMEM((rows, length, feature_dim), F32),
            pltpu.VMEM(half, BF16),
            pltpu.VMEM(half, BF16),
            pltpu.SemaphoreType.DMA((3 * rows + 3,)),
            pltpu.SemaphoreType.DMA((2 + 4 * rows,)),
        ],
        compiler_params=pltpu.CompilerParams(vmem_limit_bytes=56 * 1024 * 1024),
        cost_estimate=pl.CostEstimate(
            flops=2 * rows * length * feature_dim * feature_dim * 6,
            bytes_accessed=30_000_000,
            transcendentals=rows * length * 384,
        ),
        name="attention_back",
    )(idx, *smalls, x_rows, keys, values, wq, wk, wv)


def weights_kernel(feature_dim, ff_dim, idx_ref, *refs):
    early = refs[:GROUP]
    late = refs[GROUP : 2 * GROUP]
    keep_0, keep_1, send_0, send_1 = refs[2 * GROUP :]
    tower, place = idx_ref[0], idx_ref[1]
    pairs, block, _ = send_0.shape
    far = 2 * pairs
    pieces = ff_dim // feature_dim
    fill = early[0].shape[1] - 2 * feature_dim

    def pick(group, near, columns):
        source = spread_rows(
            (2 * far * block, 1),
            (2, 2, pairs, block),
            (far * group, group, 2 * group, 1),
            (tower, place // GROUP & 1, place // (2 * GROUP), 0),
        )
        shape = (2 * far * block, columns)
        return jnp.where(iota(shape, 1) == source + near, 1.0, 0.0).astype(BF16)

    def stacked(parts, first, columns):
        return jnp.concatenate([ref[:, first : first + columns] for ref in parts], axis=0)

    def put(first, grad):
        columns = grad.shape[1]
        half = pairs * block
        shape = (pairs, block, columns)
        for index, ref in enumerate((keep_0, keep_1, send_0, send_1)):
            rows = grad[index * half : (index + 1) * half]
            ref[:, :, first : first + columns] = rows.astype(BF16).reshape(shape)

    near = place & (GROUP - 1)
    narrow = pick(GROUP * block, near * block, feature_dim)
    grad_up = stacked(late, 0, ff_dim)
    grad_down = stacked(late, ff_dim, feature_dim)
    grad_attended = stacked(late, ff_dim + feature_dim, feature_dim)
    active = stacked(early, 0, fill)
    normed = dot_nt(narrow, stacked(early, fill, feature_dim)).astype(BF16)
    context = dot_nt(narrow, stacked(early, fill + feature_dim, feature_dim)).astype(BF16)
    put(0, dot_nn(normed, grad_up))
    for piece in range(pieces):
        if fill == ff_dim:
            chosen = pick(GROUP * pieces * block, (near * pieces + piece) * block, fill)
        else:
            chosen = pick(LANES, piece * block, fill)
        turned = dot_nt(chosen, active).astype(BF16)
        put(ff_dim + piece * feature_dim, dot_nn(turned, grad_down))
    put(2 * ff_dim, dot_nn(context, grad_attended))
    bias = jnp.sum(grad_up.astype(F32), axis=0, keepdims=True)
    shifted = [
        jnp.concatenate([bias[:, piece * block :], bias[:, : piece * block]], axis=1)
        for piece in range(1, pieces)
    ]
    stack = jnp.concatenate([bias, *shifted, jnp.zeros((LANES - pieces, ff_dim), F32)], axis=0)
    high, second, third = split(stack)
    chosen = pick(GROUP * pieces * block, near * pieces * block, ff_dim)
    columns = dot_nt(chosen, high) + (dot_nt(chosen, second) + dot_nt(chosen, third))
    put(2 * ff_dim + feature_dim, columns)


def weights(idx, early, late, places, feature_dim, ff_dim):
    far = places // GROUP
    block = feature_dim // (2 * places)
    packed = 2 * ff_dim + feature_dim + LANES
    half = (far // 2, block, packed)
    return pl.pallas_call(
        functools.partial(weights_kernel, feature_dim, ff_dim),
        grid=(1,),
        in_specs=[pl.BlockSpec(memory_space=pltpu.SMEM)] + [full(a.shape) for a in (*early, *late)],
        out_specs=[full(half)] * 4,
        out_shape=[jax.ShapeDtypeStruct(half, BF16)] * 4,
        compiler_params=pltpu.CompilerParams(vmem_limit_bytes=24 * 1024 * 1024),
        cost_estimate=pl.CostEstimate(
            flops=50_000_000_000, bytes_accessed=14_000_000, transcendentals=0
        ),
        name="weight_grads",
    )(idx, *early, *late)


def tied(*values):
    return lax.optimization_barrier(values)


def on_device(
    hidden_in, segment_ids, positives, w_query, b_query, w_key, w_value, b_value, w_out, b_out,
    gain_attn, shift_attn, w_in, b_in, w_back, b_back, gain_ffn, shift_ffn,
):
    feature_dim = hidden_in.shape[2]
    ff_dim = w_in.shape[1]
    rows, length = segment_ids.shape[1], segment_ids.shape[2]
    places = lax.axis_size("dp")
    far = places // GROUP
    tower, place = lax.axis_index("tower"), lax.axis_index("dp")
    idx = jnp.stack([tower, place, places]).astype(jnp.int32)
    x_rows = hidden_in.reshape(rows, length, feature_dim)
    keys, values, *pack, query_cls, pre_attn, up, pre_ffn, enc_cls, hot = front(
        places, idx, segment_ids,
        (b_query, b_value, b_out, gain_attn, shift_attn, b_in, b_back, gain_ffn, shift_ffn),
        x_rows, (w_key, w_value, w_query, w_out, w_in, w_back),
    )
    mats = (w_query, w_out, w_in, w_back)
    smalls = (b_query, b_out, gain_attn, shift_attn, b_in, b_back, gain_ffn, shift_ffn)

    quarter = rows * length // 4
    cuts = (0, 0, quarter, 5 * quarter // 2, 4 * quarter)

    def encode(part, before):
        return encode_part(
            cuts[part], cuts[part + 1], x_rows, keys, values, hot, mats, smalls, before
        )

    along = [moved(enc_cls, "dp", GROUP * m) for m in range(1, far)]
    early = [pack[0]] + [moved(pack[m], "dp", m) for m in range(1, GROUP)]
    own = jnp.stack([enc_cls] + list(along))
    own, early[1:3], hot = tied(own, early[1:3], hot)
    crossed = [moved(own, "dp", m) for m in range(1, GROUP)]
    encoded = encode(1, None)
    crossed, encoded = tied(crossed, encoded)
    own = [own] + list(crossed)
    other = [moved(quad, "tower", 1) for quad in own]
    scores, losses, late_own, gctx, gpa, vec_mid = middle(
        idx, own, other, positives.reshape(1, -1), pre_attn, up, pre_ffn, w_back, w_in,
        w_out, gain_attn, gain_ffn,
    )
    gctx, early = tied(gctx, early)
    late = [late_own] + [moved(late_own, "dp", m) for m in range(1, GROUP)]
    back, send, keep = attn_back(
        idx, segment_ids, query_cls, gctx, gpa, vec_mid, x_rows, keys, values,
        w_query, w_key, w_value, places,
    )
    late, keep = tied(late, keep)
    send = moved(send, "tower", 1)
    *weight_keep, first_send, last_send = weights(idx, early, late, places, feature_dim, ff_dim)
    weight_send = [first_send, last_send]
    send, weight_keep, weight_send = tied(send, weight_keep, weight_send)
    paired = [keep[m].astype(F32) + send[m].astype(F32) for m in range(GROUP)]
    near_out = [part.astype(BF16) for part in paired[1:]]
    near_out, weight_keep, weight_send = tied(near_out, weight_keep, weight_send)
    weight_send = [moved(weight_send[m], "tower", 1) for m in (1, 0)][::-1]
    near_sent = [moved(near_out[m - 1], "dp", m) for m in range(1, GROUP)]
    weight_out = (weight_keep[1].astype(F32) + weight_send[1].astype(F32)).astype(BF16)
    weight_out, encoded = tied(weight_out, encoded)
    reach, arrived = 1, moved(weight_out, "dp", GROUP)
    encoded = encode(2, encoded)
    arrived, encoded = tied(arrived, encoded)
    weight_sum = weight_keep[0].astype(F32) + weight_send[0].astype(F32) + arrived.astype(F32)
    near_sent, weight_sum, encoded = tied(near_sent, weight_sum, encoded)
    near = paired[0]
    for part in near_sent:
        near = near + part.astype(F32)
    far_out = [near[m].astype(BF16) for m in range(1, far)]
    while weight_sum.shape[0] > 1:
        reach = reach * 2
        half = weight_sum.reshape(weight_sum.shape[0] // 2, 2, *weight_sum.shape[1:])
        weight_out = half[:, 1].astype(BF16)
        last = reach == far // 2
        if last:
            far_out, weight_out, encoded = tied(far_out, weight_out, encoded)
            far_sent = [moved(far_out[m - 1], "dp", GROUP * m) for m in range(1, far)]
        arrived = moved(weight_out, "dp", GROUP * reach)
        if last:
            encoded = encode(3, encoded)
            far_sent, arrived, encoded = tied(far_sent, arrived, encoded)
        weight_sum = half[:, 0] + arrived.astype(F32)
    weight_sum = weight_sum[0]
    grad_qkv = near[0]
    for part in far_sent:
        grad_qkv = grad_qkv + part.astype(F32)
    grad_in = weight_sum[:, :ff_dim]
    grad_back = jnp.concatenate(
        [
            weight_sum[:, first : first + feature_dim]
            for first in range(ff_dim, 2 * ff_dim, feature_dim)
        ],
        axis=0,
    )
    grad_out = weight_sum[:, 2 * ff_dim : 2 * ff_dim + feature_dim]
    first = 2 * ff_dim + feature_dim
    b_i = weight_sum[:, first : first + ff_dim // feature_dim].T.reshape(-1)
    columns = grad_qkv[:, 3 * feature_dim : 3 * feature_dim + 8].T
    g_f, s_f, b_b, g_a, s_a, b_o, b_q, b_v = [columns[i] for i in range(8)]
    return (
        encoded.reshape(hidden_in.shape),
        scores.T,
        losses.reshape(-1),
        back.reshape(hidden_in.shape),
        grad_qkv[:, :feature_dim],
        b_q,
        grad_qkv[:, feature_dim : 2 * feature_dim],
        grad_qkv[:, 2 * feature_dim : 3 * feature_dim],
        b_v,
        grad_out,
        b_o,
        g_a,
        s_a,
        grad_in,
        b_i,
        grad_back,
        b_b,
        g_f,
        s_f,
    )


def solution(mesh):
    placed = (P("tower", "dp", None), P("tower", "dp", None)) + (P(),) * 16
    matrix, vector = P(("tower", "dp"), None), P(("tower", "dp"))
    return jax.shard_map(
        on_device,
        mesh=mesh,
        in_specs=placed,
        out_specs=(
            P("tower", "dp", None),
            P(None, "dp"),
            P(),
            P("tower", "dp", None),
            matrix,
            vector,
            matrix,
            matrix,
            vector,
            matrix,
            vector,
            vector,
            vector,
            matrix,
            vector,
            matrix,
            vector,
            vector,
            vector,
        ),
        check_vma=False,
    )
```

```python
import functools

import jax
import jax.numpy as jnp
from jax import lax
from jax.experimental import pallas as pl
from jax.experimental.pallas import tpu as pltpu
from jax.sharding import PartitionSpec as P

HEAD_DIM = 64
SEGS = 32
GROUP = 4
LANES = 128
FAR = float(2**30)
VMEM_BYTES = 60 * 1024 * 1024
F32 = jnp.float32
BF16 = jnp.bfloat16


def moved(value, axis, mask):
    pairs = [(source, source ^ mask) for source in range(lax.axis_size(axis))]
    return lax.ppermute(value, axis, pairs)


def dot_nn(a, b):
    return lax.dot_general(a, b, (((1,), (0,)), ((), ())), preferred_element_type=F32)


def dot_nt(a, b):
    return lax.dot_general(a, b, (((1,), (1,)), ((), ())), preferred_element_type=F32)


def dot_tn(a, b):
    return lax.dot_general(a, b, (((0,), (0,)), ((), ())), preferred_element_type=F32)


def iota(shape, dim):
    return lax.broadcasted_iota(jnp.int32, shape, dim)


def row_of(ref):
    return ref[...].astype(F32).reshape(1, -1)


def norm_parts(values):
    average = jnp.mean(values, axis=-1, keepdims=True)
    centered = values - average
    spread = jnp.mean(centered * centered, axis=-1, keepdims=True)
    inverse = lax.rsqrt(spread + 1e-12)
    return centered * inverse, inverse


def layer_norm(values, gain, shift):
    scaled, _ = norm_parts(values)
    return scaled * gain + shift


def layer_norm_back(values, gain, grad):
    scaled, inverse = norm_parts(values)
    inner = grad * gain
    mean_inner = jnp.mean(inner, axis=-1, keepdims=True)
    mean_scaled = jnp.mean(inner * scaled, axis=-1, keepdims=True)
    back = inverse * (inner - mean_inner - scaled * mean_scaled)
    return back, jnp.sum(grad * scaled, axis=0, keepdims=True), jnp.sum(grad, axis=0, keepdims=True)


def phi_of(values):
    return 0.5 * (1.0 + lax.erf(values * (2.0**-0.5)))


def gelu_exact(values):
    return values * phi_of(values)


def gelu_slope(values):
    bell = jnp.exp(-0.5 * values * values) * 0.3989422804014327
    return phi_of(values) + values * bell


def head_mask(head_count, segs, feature_dim):
    head_row = iota((head_count * segs, 1), 0) >> (segs.bit_length() - 1)
    head_col = iota((1, feature_dim), 1) >> (HEAD_DIM.bit_length() - 1)
    return jnp.where(head_row == head_col, 1.0, 0.0)


def block_heads(rows, mask, head_count):
    return jnp.concatenate([rows] * head_count, axis=0) * mask.astype(BF16)


def heads_to_rows(wide, mask, head_count, segs):
    kept = wide * mask
    total = kept[:segs]
    for head in range(1, head_count):
        total = total + kept[head * segs : (head + 1) * segs]
    return total


def split(values):
    high = values.astype(BF16)
    rest = values - high.astype(F32)
    second = rest.astype(BF16)
    return high, second, (rest - second.astype(F32)).astype(BF16)


def cls_onehot(seg_row, segs):
    shape = (segs, seg_row.shape[1])
    before = (seg_row < iota(shape, 0)).astype(F32)
    starts = jnp.sum(before, axis=1, keepdims=True).astype(jnp.int32)
    return iota(shape, 1) == starts


def cls_probs(query_wide, key_row, seg_row, head_count, segs):
    logits = dot_nt(query_wide, key_row)
    member = jnp.where(seg_row == iota((segs, seg_row.shape[1]), 0), 1.0, 0.0)
    member = jnp.concatenate([member] * head_count, axis=0)
    logits = jnp.where(member > 0.5, logits, -1000000000.0)
    top = jnp.max(logits, axis=1, keepdims=True)
    exponent = jnp.exp(logits - top)
    return exponent * (1.0 / jnp.sum(exponent, axis=1, keepdims=True))


def loads(pairs, sems):
    copies = [
        pltpu.make_async_copy(source, target, sems.at[index])
        for index, (source, target) in enumerate(pairs)
    ]
    for copy in copies:
        copy.start()
    return lambda index: copies[index].wait()


def front_kernel(
    idx_ref, seg_ref, bq, bv, bo, ga, sa, b_in, bb, gf, sf,
    x_hbm, wk_hbm, wv_hbm, wq_hbm, wo_hbm, w_in_hbm, w_back_hbm,
    k_hbm, v_hbm, pack_0, pack_1, pack_2, pack_3, qc_out, pre_attn_out, up_out, pre_ffn_out, enc_out, hot_out,
    x_s, wk, wv, wq, wo, w_in_v, w_back_v, k_s, v_s, sems, out_sems,
):
    rows, length, feature_dim = x_s.shape
    ff_dim = w_in_v.shape[1]
    head_count = feature_dim // HEAD_DIM
    wait = loads(
        [(x_hbm.at[0], x_s.at[0]), (wk_hbm, wk), (wv_hbm, wv), (wq_hbm, wq)]
        + [(x_hbm.at[row], x_s.at[row]) for row in range(1, rows)]
        + [(wo_hbm, wo), (w_in_hbm, w_in_v), (w_back_hbm, w_back_v)],
        sems,
    )
    mask = head_mask(head_count, SEGS, feature_dim)
    contexts, firsts, copies = [], [], []
    for row in range(rows):
        if row == 0:
            for index in range(3):
                wait(index)
        else:
            wait(3 + row)
        x = x_s[row]
        key_row = dot_nn(x, wk[...]).astype(BF16)
        k_s[row] = key_row
        value_row = (dot_nn(x, wv[...]) + row_of(bv)).astype(BF16)
        v_s[row] = value_row
        for kept, target in ((k_s, k_hbm), (v_s, v_hbm)):
            copy = pltpu.make_async_copy(kept.at[row], target.at[row], out_sems.at[len(copies)])
            copy.start()
            copies.append(copy)
        if row == 0:
            wait(3)
        seg_row = seg_ref[0, row : row + 1, :]
        first = jnp.where(cls_onehot(seg_row, SEGS), 1.0, 0.0).astype(BF16)
        x_cls = dot_nn(first, x).astype(BF16)
        query_cls = (dot_nn(x_cls, wq[...]) + row_of(bq)).astype(BF16)
        query_wide = block_heads((query_cls * (HEAD_DIM**-0.5)).astype(BF16), mask, head_count)
        probs = cls_probs(query_wide, key_row, seg_row, head_count, SEGS)
        context = heads_to_rows(dot_nn(probs.astype(BF16), value_row), mask, head_count, SEGS)
        contexts.append(context.astype(BF16))
        firsts.append(x_cls)
        qc_out[row * SEGS : (row + 1) * SEGS, :] = query_cls
        hot = jnp.where(seg_row == iota((LANES, length), 0), 1.0, 0.0)
        hot_out[row] = hot.T.astype(BF16)
    for index in range(3 + rows, 6 + rows):
        wait(index)
    if True:
        context_all = jnp.concatenate(contexts, axis=0)
        x_all = jnp.concatenate(firsts, axis=0)
        pre_attn = x_all.astype(F32) + (dot_nn(context_all, wo[...]) + row_of(bo))
        pre_attn_out[...] = pre_attn
        normed = layer_norm(pre_attn, row_of(ga), row_of(sa)).astype(BF16)
        up = dot_nn(normed, w_in_v[...]) + row_of(b_in)
        up_out[...] = up
        active = gelu_exact(up).astype(BF16)
        pre_ffn = normed.astype(F32) + (dot_nn(active, w_back_v[...]) + row_of(bb))
        pre_ffn_out[...] = pre_ffn
        enc_out[...] = layer_norm(pre_ffn, row_of(gf), row_of(sf)).astype(BF16)
        packs = (pack_0, pack_1, pack_2, pack_3)
        fill = pack_0.shape[1] - 2 * feature_dim
        group = ff_dim * LANES // fill
        size = group // GROUP
        if fill == ff_dim:
            for near in range(GROUP):
                packs[near][:, :ff_dim] = active
        else:
            for slot in range(fill // LANES):
                blocks = [
                    active[:, slot * group + size * b : slot * group + size * (b + 1)]
                    for b in range(GROUP)
                ]
                lanes = slot * LANES
                for near in range(GROUP):
                    source = (idx_ref[1] & (GROUP - 1)) ^ near
                    chosen = blocks[0]
                    for b in range(1, GROUP):
                        chosen = jnp.where(source == b, blocks[b], chosen)
                    packs[near][:, lanes : lanes + size] = chosen
                    packs[near][:, lanes + size : lanes + LANES] = jnp.zeros(
                        (active.shape[0], LANES - size), BF16
                    )
        for near in range(GROUP):
            packs[near][:, fill : fill + feature_dim] = normed
            packs[near][:, fill + feature_dim :] = context_all
    for copy in copies:
        copy.wait()


def full(shape):
    zeros = (0,) * len(shape)
    return pl.BlockSpec(shape, lambda *_: zeros)


ANY = pl.BlockSpec(memory_space=pl.ANY)


def active_width(places, ff_dim):
    group = GROUP * ff_dim // (2 * places)
    return ff_dim // group * LANES if group % LANES == 0 else ff_dim


def front(places, idx, segs, smalls, x_rows, mats):
    rows, length, feature_dim = x_rows.shape
    ff_dim = mats[-1].shape[0]
    cls = rows * SEGS
    shapes = (
        ((rows, length, feature_dim), BF16),
        ((rows, length, feature_dim), BF16),
        *(((cls, active_width(places, ff_dim) + 2 * feature_dim), BF16),) * GROUP,
        ((cls, feature_dim), BF16),
        ((cls, feature_dim), F32),
        ((cls, ff_dim), F32),
        ((cls, feature_dim), F32),
        ((cls, feature_dim), BF16),
        ((rows, length, LANES), BF16),
    )
    whole = pltpu.VMEM((rows, length, feature_dim), BF16)
    return pl.pallas_call(
        front_kernel,
        grid=(1,),
        in_specs=[pl.BlockSpec(memory_space=pltpu.SMEM)]
        + [full(a.shape) for a in (segs, *smalls)]
        + [ANY] * (1 + len(mats)),
        out_specs=[ANY, ANY] + [full(s) for s, _ in shapes[2:]],
        out_shape=[jax.ShapeDtypeStruct(s, d) for s, d in shapes],
        scratch_shapes=[whole]
        + [pltpu.VMEM(a.shape, BF16) for a in mats]
        + [
            whole,
            whole,
            pltpu.SemaphoreType.DMA((6 + rows,)),
            pltpu.SemaphoreType.DMA((2 * rows,)),
        ],
        compiler_params=pltpu.CompilerParams(vmem_limit_bytes=VMEM_BYTES),
        cost_estimate=pl.CostEstimate(
            flops=2 * rows * length * feature_dim * feature_dim * 3,
            bytes_accessed=30_000_000,
            transcendentals=rows * length * 384,
        ),
        name="front",
    )(idx, segs, *smalls, x_rows, *mats)


def segments_of(start, stop, length):
    found = []
    while start < stop:
        row, first = start // length, start % length
        tokens = min(stop - start, length - first)
        held = min(length, tokens + 128)
        found.append((row, first, tokens, max(0, min(first - 64, length - held)), held))
        start += tokens
    return found


def encode_kernel_at(
    segments, x_hbm, k_hbm, v_hbm, hot_hbm, wq_hbm, wo_hbm, w_in_hbm, w_back_hbm,
    bq, bo, ga, sa, b_in, bb, gf, sf, *refs
):
    enc_hbm, x_s, k_s, v_s, hot_s, enc_s, wq, wo, w_in, w_back, sems, out_sems = refs[-12:]
    feature_dim = x_s.shape[1]
    length = k_hbm.shape[1]
    ff_dim = w_in.shape[1]
    part, window = 128, 256
    count = len(segments)
    first_pairs, key_pairs, places, token_at, held_at = [], [], [], 0, 0
    for row, first, tokens, low, held in segments:
        near, kept = pl.ds(low, held), pl.ds(held_at, held)
        first_pairs.append((x_hbm.at[row, pl.ds(first, tokens)], x_s.at[pl.ds(token_at, tokens)]))
        key_pairs += [
            (hot_hbm.at[row, near], hot_s.at[kept]),
            (k_hbm.at[row, near], k_s.at[kept]),
            (v_hbm.at[row, near], v_s.at[kept]),
        ]
        places.append((token_at, held_at))
        token_at, held_at = token_at + tokens, held_at + held
    tail = [(wo_hbm, wo), (w_in_hbm, w_in), (w_back_hbm, w_back)]
    wait = loads([*first_pairs, (wq_hbm, wq), *key_pairs, *tail], sems)
    for index in range(count + 1):
        wait(index)
    x = x_s[...]
    query = ((dot_nn(x, wq[...]) + row_of(bq)).astype(BF16) * (HEAD_DIM**-0.5)).astype(BF16)
    left = iota((part, 128), 1) < HEAD_DIM
    for index in range(count + 1, 4 * count + 1):
        wait(index)
    contexts = []
    blocks = [
        (at + sub, first + sub, held_at - low)
        for (_, first, tokens, low, _), (at, held_at) in zip(segments, places)
        for sub in range(0, tokens, part)
    ]
    for at, base, shift in blocks:
        start = max(0, min(base - 64, length - window)) + shift
        keys = k_s[start : start + window, :]
        values = v_s[start : start + window, :]
        apart = ((hot_s[start : start + window, :].astype(F32) - 1.0) * FAR).astype(BF16)
        hot_query = hot_s[base + shift : base + shift + part, :]
        pieces = []
        for pair in range(feature_dim // 128):
            lanes = slice(pair * 128, pair * 128 + 128)
            both = query[at : at + part, lanes]
            zero = jnp.zeros_like(both)
            wide = jnp.concatenate(
                [
                    jnp.concatenate([jnp.where(left, both, zero), hot_query], axis=1),
                    jnp.concatenate([jnp.where(left, zero, both), hot_query], axis=1),
                ],
                axis=0,
            )
            logits = dot_nt(wide, jnp.concatenate([keys[:, lanes], apart], axis=1))
            top = jnp.max(logits, axis=1, keepdims=True)
            exponent = jnp.exp(logits - top)
            total = jnp.sum(exponent, axis=1, keepdims=True)
            out = dot_nn(exponent.astype(BF16), values[:, lanes]) * (1.0 / total)
            pieces.append(jnp.where(left, out[:part], out[part:]).astype(BF16))
        contexts.append(jnp.concatenate(pieces, axis=1))
    context = jnp.concatenate(contexts, axis=0)
    wait(4 * count + 1)
    pre_attn = x.astype(F32) + (dot_nn(context, wo[...]) + row_of(bo))
    normed = layer_norm(pre_attn, row_of(ga), row_of(sa)).astype(BF16)
    wait(4 * count + 2)
    wait(4 * count + 3)
    bias_in = row_of(b_in)
    total = normed.astype(F32) + row_of(bb)
    chunk = 768
    for start in range(0, ff_dim, chunk):
        cols = slice(start, start + chunk)
        up = dot_nn(normed, w_in[:, cols]) + bias_in[:, cols]
        total = total + dot_nn(gelu_exact(up).astype(BF16), w_back[cols, :])
    enc_s[...] = layer_norm(total, row_of(gf), row_of(sf)).astype(BF16)
    copies = [
        pltpu.make_async_copy(
            enc_s.at[pl.ds(at, tokens)], enc_hbm.at[row, pl.ds(first, tokens)], out_sems.at[index]
        )
        for index, ((row, first, tokens, _, _), (at, _)) in enumerate(zip(segments, places))
    ]
    for copy in copies:
        copy.start()
    for copy in copies:
        copy.wait()


def encode_part(start, stop, x_rows, keys, values, hot, mats, smalls, before):
    rows, length, feature_dim = x_rows.shape
    segments = segments_of(start, stop, length)
    tokens, held = stop - start, sum(segment[4] for segment in segments)
    extra = [] if before is None else [before]
    return pl.pallas_call(
        functools.partial(encode_kernel_at, segments),
        grid=(1,),
        in_specs=[ANY] * (4 + len(mats)) + [full(a.shape) for a in smalls] + [ANY for _ in extra],
        out_specs=ANY,
        out_shape=jax.ShapeDtypeStruct((rows, length, feature_dim), BF16),
        input_output_aliases={} if before is None else {4 + len(mats) + len(smalls): 0},
        scratch_shapes=[
            pltpu.VMEM((tokens, feature_dim), BF16),
            pltpu.VMEM((held, feature_dim), BF16),
            pltpu.VMEM((held, feature_dim), BF16),
            pltpu.VMEM((held, hot.shape[2]), BF16),
            pltpu.VMEM((tokens, feature_dim), BF16),
        ]
        + [pltpu.VMEM(a.shape, BF16) for a in mats]
        + [
            pltpu.SemaphoreType.DMA((4 * len(segments) + 4,)),
            pltpu.SemaphoreType.DMA((len(segments),)),
        ],
        compiler_params=pltpu.CompilerParams(vmem_limit_bytes=(56 if before is None else 40) * 1024 * 1024),
        cost_estimate=pl.CostEstimate(
            flops=tokens * feature_dim * feature_dim, bytes_accessed=1_000_000, transcendentals=0
        ),
        name="encode_part",
    )(x_rows, keys, values, hot, *mats, *smalls, *extra)


def middle_kernel(
    idx_ref, *refs
):
    own = refs[:GROUP]
    other = refs[GROUP : 2 * GROUP]
    (
        positives, pre_attn_ref, pre_ffn_ref, ga, gf, w_back_hbm, w_in_hbm, up_hbm, wo_hbm,
        scores_out, losses_out, late_out, gctx_out, gpa_out, vec_out,
        both, w_in_v, w_back_v, up_ref, wo, sems, wsems,
    ) = refs[2 * GROUP :]
    tower, place = idx_ref[0], idx_ref[1]
    far, cls, feature_dim = own[0].shape
    ff_dim = w_in_v.shape[1]
    copy_back = pltpu.make_async_copy(w_back_hbm, w_back_v, wsems.at[0])
    copy_in = pltpu.make_async_copy(w_in_hbm, w_in_v, wsems.at[1])
    copy_up = pltpu.make_async_copy(up_hbm, up_ref, wsems.at[2])
    copy_out = pltpu.make_async_copy(wo_hbm, wo, wsems.at[3])
    copies = []
    for side, group in ((tower, own), (1 - tower, other)):
        for near in range(GROUP):
            for slot in range(far):
                to = both.at[side, place ^ (slot * GROUP + near)]
                copies.append(
                    pltpu.make_async_copy(group[near].at[slot], to, sems.at[len(copies)])
                )
    for copy in copies:
        copy.start()
    copy_back.start()
    copy_up.start()
    copy_in.start()
    copy_out.start()
    for copy in copies:
        copy.wait()
    count = far * GROUP * cls
    scale = feature_dim**-0.5
    queries = both[0].reshape(count, feature_dim)
    positive_row = positives[...]
    block = min(count, max(64, (1 << 20) // count))

    def partial_of(first):
        passages = both[1, pl.ds(first // cls, block // cls)].reshape(block, feature_dim)
        scored = dot_nt(passages, queries) * scale
        top = jnp.max(scored, axis=0, keepdims=True)
        total = jnp.sum(jnp.exp(scored - top), axis=0, keepdims=True)
        hit = iota((block, count), 0) + first == positive_row
        return top, total, jnp.sum(jnp.where(hit, scored, 0.0), axis=0, keepdims=True)

    def joined(index, state):
        top, total, picked = partial_of(index * block)
        joint = jnp.maximum(state[0], top)
        return (
            joint,
            state[1] * jnp.exp(state[0] - joint) + total * jnp.exp(top - joint),
            state[2] + picked,
        )

    state = partial_of(0)
    if count // block > 1:
        state = lax.fori_loop(1, count // block, joined, state)
    row_log = state[0] + jnp.log(state[1])
    losses_out[...] = row_log - state[2]
    scores_out[...] = dot_nt(both[1, place], queries) * scale
    mine = both[tower, place]
    opposite = both[1 - tower].reshape(count, feature_dim)
    own_scores = dot_nt(mine, opposite) * scale
    own_top = jnp.max(own_scores, axis=1, keepdims=True)
    own_log = own_top + jnp.log(jnp.sum(jnp.exp(own_scores - own_top), axis=1, keepdims=True))
    lanes = iota((cls, count), 1)
    mine_index = iota((cls, count), 0) + place * cls
    spread_positive = jnp.broadcast_to(positive_row, (cls, count))
    own_positive = jnp.sum(
        jnp.where(lanes == mine_index, spread_positive.astype(F32), 0.0), axis=1, keepdims=True
    ).astype(jnp.int32)
    is_query = tower == 0
    log_used = jnp.where(is_query, jnp.broadcast_to(own_log, (cls, count)), row_log)
    hit_query = (lanes == own_positive).astype(F32)
    hit_passage = (spread_positive == mine_index).astype(F32)
    hit = jnp.where(is_query, hit_query, hit_passage)
    grad_scores = (jnp.exp(own_scores - log_used) - hit).astype(BF16)
    grad_cls = dot_nn(grad_scores, opposite) * scale
    grad_pre_ffn, grad_gf, grad_sf = layer_norm_back(pre_ffn_ref[...], row_of(gf), grad_cls)
    vec_out[0:1, :] = grad_gf
    vec_out[1:2, :] = grad_sf
    grad_down = grad_pre_ffn.astype(BF16)
    vec_out[2:3, :] = jnp.sum(grad_down.astype(F32), axis=0, keepdims=True)
    copy_back.wait()
    copy_up.wait()
    grad_up = (dot_nt(grad_down, w_back_v[...]) * gelu_slope(up_ref[...])).astype(BF16)
    late_out[:, :ff_dim] = grad_up
    late_out[:, ff_dim : ff_dim + feature_dim] = grad_down
    copy_in.wait()
    grad_normed = grad_pre_ffn + dot_nt(grad_up, w_in_v[...])
    grad_pre_attn, grad_ga, grad_sa = layer_norm_back(pre_attn_ref[...], row_of(ga), grad_normed)
    vec_out[3:4, :] = grad_ga
    vec_out[4:5, :] = grad_sa
    gpa_out[...] = grad_pre_attn
    grad_attended = grad_pre_attn.astype(BF16)
    late_out[:, ff_dim + feature_dim :] = grad_attended
    vec_out[5:6, :] = jnp.sum(grad_attended.astype(F32), axis=0, keepdims=True)
    copy_out.wait()
    gctx_out[...] = dot_nt(grad_attended, wo[...]).astype(BF16)


def middle(idx, own, other, positives, pre_attn, up, pre_ffn, w_back, w_in, wo, ga, gf):
    far, cls, feature_dim = own[0].shape
    ff_dim = w_in.shape[1]
    places = far * GROUP
    count = places * cls
    shapes = (
        ((cls, count), F32),
        ((1, count), F32),
        ((cls, ff_dim + 2 * feature_dim), BF16),
        ((cls, feature_dim), BF16),
        ((cls, feature_dim), F32),
        ((8, feature_dim), F32),
    )
    smalls = (positives, pre_attn, pre_ffn, ga, gf)
    return pl.pallas_call(
        middle_kernel,
        in_specs=[pl.BlockSpec(memory_space=pltpu.SMEM)]
        + [ANY] * (2 * GROUP)
        + [full(a.shape) for a in smalls]
        + [ANY] * 4,
        out_specs=[full(s) for s, _ in shapes],
        out_shape=[jax.ShapeDtypeStruct(s, d) for s, d in shapes],
        grid=(1,),
        scratch_shapes=[
            pltpu.VMEM((2, places, cls, feature_dim), BF16),
            pltpu.VMEM(w_in.shape, BF16),
            pltpu.VMEM(w_back.shape, BF16),
            pltpu.VMEM(up.shape, F32),
            pltpu.VMEM(wo.shape, BF16),
            pltpu.SemaphoreType.DMA((2 * places,)),
            pltpu.SemaphoreType.DMA((4,)),
        ],
        compiler_params=pltpu.CompilerParams(vmem_limit_bytes=56 * 1024 * 1024),
        cost_estimate=pl.CostEstimate(
            flops=2 * count * count * feature_dim, bytes_accessed=20_000_000, transcendentals=count * count
        ),
        name="loss",
    )(idx, *own, *other, *smalls, w_back, w_in, up, wo)


def spread_rows(shape, sizes, strides, masks, dim=0):
    rest = iota(shape, dim)
    total = jnp.zeros(shape, jnp.int32)
    for size, stride, mask in zip(reversed(sizes), reversed(strides), reversed(masks)):
        above = jnp.floor((rest.astype(F32) + 0.5) * (1.0 / size)).astype(jnp.int32)
        digit = rest - above * size
        total = total + (digit ^ mask) * stride
        rest = above
    return total


def attn_back_kernel(
    idx_ref, seg_ref, qc_ref, gctx_ref, gpa_ref, vec_ref, x_hbm, k_hbm, v_hbm, wq_hbm, wk_hbm, wv_hbm,
    back_hbm, send_hbm, keep_hbm,
    x_s, k_s, v_s, wq, wk, wv, mixed_s, back_s, send_s, keep_s, sems, out_sems,
):
    tower, place = idx_ref[0], idx_ref[1]
    towers = 2
    rows, length, feature_dim = x_s.shape
    head_count = feature_dim // HEAD_DIM
    pairs = []
    for row in range(rows):
        pairs += [(k_hbm.at[row], k_s.at[row]), (v_hbm.at[row], v_s.at[row]), (x_hbm.at[row], x_s.at[row])]
    pairs += [(wq_hbm, wq), (wk_hbm, wk), (wv_hbm, wv)]
    wait = loads(pairs, sems)
    mask = head_mask(head_count, SEGS, feature_dim)
    scale = HEAD_DIM**-0.5
    shape = (feature_dim, feature_dim)
    wide = head_count * SEGS
    far, block = keep_s.shape[1:3]
    source = spread_rows(
        (1, feature_dim),
        (towers, GROUP, far, block),
        (far * GROUP * block, block, GROUP * block, 1),
        (tower, place & (GROUP - 1), place // GROUP, 0),
        1,
    )
    order = jnp.where(iota(shape, 0) == source, 1.0, 0.0).astype(BF16)
    scatters, wides, drawn, drawn_cls, grads_q, biases = [], [], [], [], [], []
    for row in range(rows):
        here = slice(row * SEGS, (row + 1) * SEGS)
        seg_row = seg_ref[0, row : row + 1, :]
        query_wide = block_heads((qc_ref[here, :] * scale).astype(BF16), mask, head_count)
        gctx_wide = block_heads(gctx_ref[here, :], mask, head_count)
        wait(3 * row)
        key_row = k_s[row]
        probs = cls_probs(query_wide, key_row, seg_row, head_count, SEGS)
        wait(3 * row + 1)
        grad_probs = dot_nt(gctx_wide, v_s[row])
        inner = jnp.sum(probs * grad_probs, axis=1, keepdims=True)
        grad_logits = (probs * (grad_probs - inner)).astype(BF16)
        grad_query = heads_to_rows(dot_nn(grad_logits, key_row), mask, head_count, SEGS)
        grad_query = (grad_query * scale).astype(BF16)
        mixed = jnp.concatenate([grad_logits, probs.astype(BF16)], axis=0)
        mixed_s[row] = mixed
        wait(3 * row + 2)
        x = x_s[row]
        first = jnp.where(cls_onehot(seg_row, SEGS), 1.0, 0.0).astype(BF16)
        drawn.append(dot_nn(mixed, x).astype(BF16))
        drawn_cls.append(dot_nn(first, x).astype(BF16))
        grads_q.append(grad_query)
        bias_of_value = jnp.sum(
            gctx_wide.astype(F32) * jnp.sum(mixed[wide:].astype(F32), axis=1, keepdims=True),
            axis=0, keepdims=True,
        )
        biases.append((jnp.sum(grad_query.astype(F32), axis=0, keepdims=True), bias_of_value))
        if row == 0:
            wait(3 * rows)
        cls_back = gpa_ref[here, :] + dot_nt(grad_query, wq[...])
        scatters.append((jnp.concatenate([first] * 3, axis=0), jnp.concatenate(split(cls_back), axis=0)))
        wides.append((query_wide, gctx_wide))
    def over_rows(parts):
        return jnp.concatenate(parts, axis=0)

    turned_k = dot_nn(over_rows([part[:wide] for part in drawn]), order).astype(BF16)
    turned_v = dot_nn(over_rows([part[wide:] for part in drawn]), order).astype(BF16)
    turned_cls = dot_nn(over_rows(drawn_cls), order).astype(BF16)
    acc_q = dot_tn(turned_cls, over_rows(grads_q))
    acc_k = dot_tn(turned_k, over_rows([pair[0] for pair in wides]))
    acc_v = dot_tn(turned_v, over_rows([pair[1] for pair in wides]))
    bias_q, bias_v = biases[0]
    for more in biases[1:]:
        bias_q, bias_v = bias_q + more[0], bias_v + more[1]
    vectors = jnp.concatenate(
        [vec_ref[0:6, :], bias_q, bias_v, jnp.zeros((LANES - 8, feature_dim), F32)], axis=0
    )
    high, second, third = split(vectors)
    columns = (dot_nn(high, order) + (dot_nn(second, order) + dot_nn(third, order))).T
    half = feature_dim // towers
    place_at = 0
    for grad in (acc_q, acc_k, acc_v, columns):
        lanes = slice(place_at, place_at + grad.shape[1])
        cut = (GROUP, far, block, grad.shape[1])
        keep_s[:, :, :, lanes] = grad[:half].astype(BF16).reshape(cut)
        send_s[:, :, :, lanes] = grad[half:].astype(BF16).reshape(cut)
        place_at = lanes.stop
    copies = [
        pltpu.make_async_copy(send_s, send_hbm, out_sems.at[0]),
        pltpu.make_async_copy(keep_s, keep_hbm, out_sems.at[1]),
    ]
    for copy in copies:
        copy.start()
    wait(3 * rows + 1)
    wait(3 * rows + 2)
    part = length // 4
    for row in range(rows):
        first, pieces = scatters[row]
        query_wide, gctx_wide = wides[row]
        spread = jnp.concatenate(
            [dot_nt(query_wide, wk[...]).astype(BF16), dot_nt(gctx_wide, wv[...]).astype(BF16)], axis=0
        )
        for start in range(0, length, part):
            here = slice(start, start + part)
            back = dot_tn(mixed_s[row, :, here], spread)
            back_s[row, here, :] = back + dot_tn(first[:, here], pieces)
            copy = pltpu.make_async_copy(
                back_s.at[row, pl.ds(start, part)],
                back_hbm.at[row, pl.ds(start, part)],
                out_sems.at[len(copies)],
            )
            copy.start()
            copies.append(copy)
    for copy in copies:
        copy.wait()


def attn_back(idx, segs, qc, gctx, gpa, vectors, x_rows, keys, values, wq, wk, wv, places):
    rows, length, feature_dim = x_rows.shape
    block = feature_dim // (2 * places)
    half = (GROUP, places // GROUP, block, 3 * feature_dim + LANES)
    shapes = (((rows, length, feature_dim), F32), (half, BF16), (half, BF16))
    smalls = (segs, qc, gctx, gpa, vectors)
    square = pltpu.VMEM((feature_dim, feature_dim), BF16)
    whole = pltpu.VMEM((rows, length, feature_dim), BF16)
    return pl.pallas_call(
        attn_back_kernel,
        grid=(1,),
        in_specs=[pl.BlockSpec(memory_space=pltpu.SMEM)]
        + [full(a.shape) for a in smalls]
        + [ANY] * 6,
        out_specs=[ANY] * 3,
        out_shape=[jax.ShapeDtypeStruct(s, d) for s, d in shapes],
        scratch_shapes=[whole, whole, whole, square, square, square]
        + [
            pltpu.VMEM((rows, 2 * feature_dim // HEAD_DIM * SEGS, length), BF16),
            pltpu.VMEM((rows, length, feature_dim), F32),
            pltpu.VMEM(half, BF16),
            pltpu.VMEM(half, BF16),
            pltpu.SemaphoreType.DMA((3 * rows + 3,)),
            pltpu.SemaphoreType.DMA((2 + 4 * rows,)),
        ],
        compiler_params=pltpu.CompilerParams(vmem_limit_bytes=56 * 1024 * 1024),
        cost_estimate=pl.CostEstimate(
            flops=2 * rows * length * feature_dim * feature_dim * 6,
            bytes_accessed=30_000_000,
            transcendentals=rows * length * 384,
        ),
        name="attention_back",
    )(idx, *smalls, x_rows, keys, values, wq, wk, wv)


def weights_kernel(feature_dim, ff_dim, idx_ref, *refs):
    early = refs[:GROUP]
    late = refs[GROUP : 2 * GROUP]
    keep_0, keep_1, send_0, send_1 = refs[2 * GROUP :]
    tower, place = idx_ref[0], idx_ref[1]
    pairs, block, _ = send_0.shape
    far = 2 * pairs
    pieces = ff_dim // feature_dim
    fill = early[0].shape[1] - 2 * feature_dim

    def pick(group, near, columns):
        source = spread_rows(
            (2 * far * block, 1),
            (2, 2, pairs, block),
            (far * group, group, 2 * group, 1),
            (tower, place // GROUP & 1, place // (2 * GROUP), 0),
        )
        shape = (2 * far * block, columns)
        return jnp.where(iota(shape, 1) == source + near, 1.0, 0.0).astype(BF16)

    def stacked(parts, first, columns):
        return jnp.concatenate([ref[:, first : first + columns] for ref in parts], axis=0)

    def put(first, grad):
        columns = grad.shape[1]
        half = pairs * block
        shape = (pairs, block, columns)
        for index, ref in enumerate((keep_0, keep_1, send_0, send_1)):
            rows = grad[index * half : (index + 1) * half]
            ref[:, :, first : first + columns] = rows.astype(BF16).reshape(shape)

    near = place & (GROUP - 1)
    narrow = pick(GROUP * block, near * block, feature_dim)
    grad_up = stacked(late, 0, ff_dim)
    grad_down = stacked(late, ff_dim, feature_dim)
    grad_attended = stacked(late, ff_dim + feature_dim, feature_dim)
    active = stacked(early, 0, fill)
    normed = dot_nt(narrow, stacked(early, fill, feature_dim)).astype(BF16)
    context = dot_nt(narrow, stacked(early, fill + feature_dim, feature_dim)).astype(BF16)
    put(0, dot_nn(normed, grad_up))
    for piece in range(pieces):
        if fill == ff_dim:
            chosen = pick(GROUP * pieces * block, (near * pieces + piece) * block, fill)
        else:
            chosen = pick(LANES, piece * block, fill)
        turned = dot_nt(chosen, active).astype(BF16)
        put(ff_dim + piece * feature_dim, dot_nn(turned, grad_down))
    put(2 * ff_dim, dot_nn(context, grad_attended))
    bias = jnp.sum(grad_up.astype(F32), axis=0, keepdims=True)
    shifted = [
        jnp.concatenate([bias[:, piece * block :], bias[:, : piece * block]], axis=1)
        for piece in range(1, pieces)
    ]
    stack = jnp.concatenate([bias, *shifted, jnp.zeros((LANES - pieces, ff_dim), F32)], axis=0)
    high, second, third = split(stack)
    chosen = pick(GROUP * pieces * block, near * pieces * block, ff_dim)
    columns = dot_nt(chosen, high) + (dot_nt(chosen, second) + dot_nt(chosen, third))
    put(2 * ff_dim + feature_dim, columns)


def weights(idx, early, late, places, feature_dim, ff_dim):
    far = places // GROUP
    block = feature_dim // (2 * places)
    packed = 2 * ff_dim + feature_dim + LANES
    half = (far // 2, block, packed)
    return pl.pallas_call(
        functools.partial(weights_kernel, feature_dim, ff_dim),
        grid=(1,),
        in_specs=[pl.BlockSpec(memory_space=pltpu.SMEM)] + [full(a.shape) for a in (*early, *late)],
        out_specs=[full(half)] * 4,
        out_shape=[jax.ShapeDtypeStruct(half, BF16)] * 4,
        compiler_params=pltpu.CompilerParams(vmem_limit_bytes=24 * 1024 * 1024),
        cost_estimate=pl.CostEstimate(
            flops=50_000_000_000, bytes_accessed=14_000_000, transcendentals=0
        ),
        name="weight_grads",
    )(idx, *early, *late)


def tied(*values):
    return lax.optimization_barrier(values)


def on_device(
    hidden_in, segment_ids, positives, w_query, b_query, w_key, w_value, b_value, w_out, b_out,
    gain_attn, shift_attn, w_in, b_in, w_back, b_back, gain_ffn, shift_ffn,
):
    feature_dim = hidden_in.shape[2]
    ff_dim = w_in.shape[1]
    rows, length = segment_ids.shape[1], segment_ids.shape[2]
    places = lax.axis_size("dp")
    far = places // GROUP
    tower, place = lax.axis_index("tower"), lax.axis_index("dp")
    idx = jnp.stack([tower, place, places]).astype(jnp.int32)
    x_rows = hidden_in.reshape(rows, length, feature_dim)
    keys, values, *pack, query_cls, pre_attn, up, pre_ffn, enc_cls, hot = front(
        places, idx, segment_ids,
        (b_query, b_value, b_out, gain_attn, shift_attn, b_in, b_back, gain_ffn, shift_ffn),
        x_rows, (w_key, w_value, w_query, w_out, w_in, w_back),
    )
    mats = (w_query, w_out, w_in, w_back)
    smalls = (b_query, b_out, gain_attn, shift_attn, b_in, b_back, gain_ffn, shift_ffn)

    quarter = rows * length // 4
    cuts = (0, 0, quarter, 5 * quarter // 2, 4 * quarter)

    def encode(part, before):
        return encode_part(
            cuts[part], cuts[part + 1], x_rows, keys, values, hot, mats, smalls, before
        )

    along = [moved(enc_cls, "dp", GROUP * m) for m in range(1, far)]
    early = [pack[0]] + [moved(pack[m], "dp", m) for m in range(1, GROUP)]
    own = jnp.stack([enc_cls] + list(along))
    own, early[1:3], hot = tied(own, early[1:3], hot)
    crossed = [moved(own, "dp", m) for m in range(1, GROUP)]
    encoded = encode(1, None)
    crossed, encoded = tied(crossed, encoded)
    own = [own] + list(crossed)
    other = [moved(quad, "tower", 1) for quad in own]
    scores, losses, late_own, gctx, gpa, vec_mid = middle(
        idx, own, other, positives.reshape(1, -1), pre_attn, up, pre_ffn, w_back, w_in,
        w_out, gain_attn, gain_ffn,
    )
    gctx, early = tied(gctx, early)
    late = [late_own] + [moved(late_own, "dp", m) for m in range(1, GROUP)]
    back, send, keep = attn_back(
        idx, segment_ids, query_cls, gctx, gpa, vec_mid, x_rows, keys, values,
        w_query, w_key, w_value, places,
    )
    late, keep = tied(late, keep)
    send = moved(send, "tower", 1)
    *weight_keep, first_send, last_send = weights(idx, early, late, places, feature_dim, ff_dim)
    weight_send = [first_send, last_send]
    send, weight_keep, weight_send = tied(send, weight_keep, weight_send)
    paired = [keep[m].astype(F32) + send[m].astype(F32) for m in range(GROUP)]
    near_out = [part.astype(BF16) for part in paired[1:]]
    near_out, weight_keep, weight_send = tied(near_out, weight_keep, weight_send)
    weight_send = [moved(weight_send[m], "tower", 1) for m in (1, 0)][::-1]
    near_sent = [moved(near_out[m - 1], "dp", m) for m in range(1, GROUP)]
    weight_out = (weight_keep[1].astype(F32) + weight_send[1].astype(F32)).astype(BF16)
    weight_out, encoded = tied(weight_out, encoded)
    reach, arrived = 1, moved(weight_out, "dp", GROUP)
    encoded = encode(2, encoded)
    arrived, encoded = tied(arrived, encoded)
    weight_sum = weight_keep[0].astype(F32) + weight_send[0].astype(F32) + arrived.astype(F32)
    near_sent, weight_sum, encoded = tied(near_sent, weight_sum, encoded)
    near = paired[0]
    for part in near_sent:
        near = near + part.astype(F32)
    far_out = [near[m].astype(BF16) for m in range(1, far)]
    while weight_sum.shape[0] > 1:
        reach = reach * 2
        half = weight_sum.reshape(weight_sum.shape[0] // 2, 2, *weight_sum.shape[1:])
        weight_out = half[:, 1].astype(BF16)
        last = reach == far // 2
        if last:
            far_out, weight_out, encoded = tied(far_out, weight_out, encoded)
            far_sent = [moved(far_out[m - 1], "dp", GROUP * m) for m in range(1, far)]
        arrived = moved(weight_out, "dp", GROUP * reach)
        if last:
            encoded = encode(3, encoded)
            far_sent, arrived, encoded = tied(far_sent, arrived, encoded)
        weight_sum = half[:, 0] + arrived.astype(F32)
    weight_sum = weight_sum[0]
    grad_qkv = near[0]
    for part in far_sent:
        grad_qkv = grad_qkv + part.astype(F32)
    grad_in = weight_sum[:, :ff_dim]
    grad_back = jnp.concatenate(
        [
            weight_sum[:, first : first + feature_dim]
            for first in range(ff_dim, 2 * ff_dim, feature_dim)
        ],
        axis=0,
    )
    grad_out = weight_sum[:, 2 * ff_dim : 2 * ff_dim + feature_dim]
    first = 2 * ff_dim + feature_dim
    b_i = weight_sum[:, first : first + ff_dim // feature_dim].T.reshape(-1)
    columns = grad_qkv[:, 3 * feature_dim : 3 * feature_dim + 8].T
    g_f, s_f, b_b, g_a, s_a, b_o, b_q, b_v = [columns[i] for i in range(8)]
    return (
        encoded.reshape(hidden_in.shape),
        scores.T,
        losses.reshape(-1),
        back.reshape(hidden_in.shape),
        grad_qkv[:, :feature_dim],
        b_q,
        grad_qkv[:, feature_dim : 2 * feature_dim],
        grad_qkv[:, 2 * feature_dim : 3 * feature_dim],
        b_v,
        grad_out,
        b_o,
        g_a,
        s_a,
        grad_in,
        b_i,
        grad_back,
        b_b,
        g_f,
        s_f,
    )


def solution(mesh):
    placed = (P("tower", "dp", None), P("tower", "dp", None)) + (P(),) * 16
    matrix, vector = P(("tower", "dp"), None), P(("tower", "dp"))
    return jax.shard_map(
        on_device,
        mesh=mesh,
        in_specs=placed,
        out_specs=(
            P("tower", "dp", None),
            P(None, "dp"),
            P(),
            P("tower", "dp", None),
            matrix,
            vector,
            matrix,
            matrix,
            vector,
            matrix,
            vector,
            vector,
            vector,
            matrix,
            vector,
            matrix,
            vector,
            vector,
            vector,
        ),
        check_vma=False,
    )
```

```python
import functools

import jax
import jax.numpy as jnp
from jax import lax
from jax.experimental import pallas as pl
from jax.experimental.pallas import tpu as pltpu
from jax.sharding import PartitionSpec as P

HEAD_DIM = 64
SEGS = 32
GROUP = 4
LANES = 128
FAR = float(2**30)
VMEM_BYTES = 60 * 1024 * 1024
F32 = jnp.float32
BF16 = jnp.bfloat16


def moved(value, axis, mask):
    pairs = [(source, source ^ mask) for source in range(lax.axis_size(axis))]
    return lax.ppermute(value, axis, pairs)


def dot_nn(a, b):
    return lax.dot_general(a, b, (((1,), (0,)), ((), ())), preferred_element_type=F32)


def dot_nt(a, b):
    return lax.dot_general(a, b, (((1,), (1,)), ((), ())), preferred_element_type=F32)


def dot_tn(a, b):
    return lax.dot_general(a, b, (((0,), (0,)), ((), ())), preferred_element_type=F32)


def iota(shape, dim):
    return lax.broadcasted_iota(jnp.int32, shape, dim)


def row_of(ref):
    return ref[...].astype(F32).reshape(1, -1)


def norm_parts(values):
    average = jnp.mean(values, axis=-1, keepdims=True)
    centered = values - average
    spread = jnp.mean(centered * centered, axis=-1, keepdims=True)
    inverse = lax.rsqrt(spread + 1e-12)
    return centered * inverse, inverse


def layer_norm(values, gain, shift):
    scaled, _ = norm_parts(values)
    return scaled * gain + shift


def layer_norm_back(values, gain, grad):
    scaled, inverse = norm_parts(values)
    inner = grad * gain
    mean_inner = jnp.mean(inner, axis=-1, keepdims=True)
    mean_scaled = jnp.mean(inner * scaled, axis=-1, keepdims=True)
    back = inverse * (inner - mean_inner - scaled * mean_scaled)
    return back, jnp.sum(grad * scaled, axis=0, keepdims=True), jnp.sum(grad, axis=0, keepdims=True)


def phi_of(values):
    return 0.5 * (1.0 + lax.erf(values * (2.0**-0.5)))


def gelu_exact(values):
    return values * phi_of(values)


def gelu_slope(values):
    bell = jnp.exp(-0.5 * values * values) * 0.3989422804014327
    return phi_of(values) + values * bell


def head_mask(head_count, segs, feature_dim):
    head_row = iota((head_count * segs, 1), 0) >> (segs.bit_length() - 1)
    head_col = iota((1, feature_dim), 1) >> (HEAD_DIM.bit_length() - 1)
    return jnp.where(head_row == head_col, 1.0, 0.0)


def block_heads(rows, mask, head_count):
    return jnp.concatenate([rows] * head_count, axis=0) * mask.astype(BF16)


def heads_to_rows(wide, mask, head_count, segs):
    kept = wide * mask
    total = kept[:segs]
    for head in range(1, head_count):
        total = total + kept[head * segs : (head + 1) * segs]
    return total


def split(values):
    high = values.astype(BF16)
    rest = values - high.astype(F32)
    second = rest.astype(BF16)
    return high, second, (rest - second.astype(F32)).astype(BF16)


def cls_onehot(seg_row, segs):
    shape = (segs, seg_row.shape[1])
    before = (seg_row < iota(shape, 0)).astype(F32)
    starts = jnp.sum(before, axis=1, keepdims=True).astype(jnp.int32)
    return iota(shape, 1) == starts


def cls_probs(query_wide, key_row, seg_row, head_count, segs):
    logits = dot_nt(query_wide, key_row)
    member = jnp.where(seg_row == iota((segs, seg_row.shape[1]), 0), 1.0, 0.0)
    member = jnp.concatenate([member] * head_count, axis=0)
    logits = jnp.where(member > 0.5, logits, -1000000000.0)
    top = jnp.max(logits, axis=1, keepdims=True)
    exponent = jnp.exp(logits - top)
    return exponent * (1.0 / jnp.sum(exponent, axis=1, keepdims=True))


def loads(pairs, sems):
    copies = [
        pltpu.make_async_copy(source, target, sems.at[index])
        for index, (source, target) in enumerate(pairs)
    ]
    for copy in copies:
        copy.start()
    return lambda index: copies[index].wait()


def front_kernel(
    idx_ref, seg_ref, bq, bv, bo, ga, sa, b_in, bb, gf, sf,
    x_hbm, wk_hbm, wv_hbm, wq_hbm, wo_hbm, w_in_hbm, w_back_hbm,
    k_hbm, v_hbm, pack_0, pack_1, pack_2, pack_3, qc_out, pre_attn_out, up_out, pre_ffn_out, enc_out, hot_out,
    x_s, wk, wv, wq, wo, w_in_v, w_back_v, k_s, v_s, sems, out_sems,
):
    rows, length, feature_dim = x_s.shape
    ff_dim = w_in_v.shape[1]
    head_count = feature_dim // HEAD_DIM
    wait = loads(
        [(x_hbm.at[0], x_s.at[0]), (wk_hbm, wk), (wv_hbm, wv), (wq_hbm, wq)]
        + [(x_hbm.at[row], x_s.at[row]) for row in range(1, rows)]
        + [(wo_hbm, wo), (w_in_hbm, w_in_v), (w_back_hbm, w_back_v)],
        sems,
    )
    mask = head_mask(head_count, SEGS, feature_dim)
    contexts, firsts, copies = [], [], []
    for row in range(rows):
        if row == 0:
            for index in range(3):
                wait(index)
        else:
            wait(3 + row)
        x = x_s[row]
        key_row = dot_nn(x, wk[...]).astype(BF16)
        k_s[row] = key_row
        value_row = (dot_nn(x, wv[...]) + row_of(bv)).astype(BF16)
        v_s[row] = value_row
        for kept, target in ((k_s, k_hbm), (v_s, v_hbm)):
            copy = pltpu.make_async_copy(kept.at[row], target.at[row], out_sems.at[len(copies)])
            copy.start()
            copies.append(copy)
        if row == 0:
            wait(3)
        seg_row = seg_ref[0, row : row + 1, :]
        first = jnp.where(cls_onehot(seg_row, SEGS), 1.0, 0.0).astype(BF16)
        x_cls = dot_nn(first, x).astype(BF16)
        query_cls = (dot_nn(x_cls, wq[...]) + row_of(bq)).astype(BF16)
        query_wide = block_heads((query_cls * (HEAD_DIM**-0.5)).astype(BF16), mask, head_count)
        probs = cls_probs(query_wide, key_row, seg_row, head_count, SEGS)
        context = heads_to_rows(dot_nn(probs.astype(BF16), value_row), mask, head_count, SEGS)
        contexts.append(context.astype(BF16))
        firsts.append(x_cls)
        qc_out[row * SEGS : (row + 1) * SEGS, :] = query_cls
        hot = jnp.where(seg_row == iota((LANES, length), 0), 1.0, 0.0)
        hot_out[row] = hot.T.astype(BF16)
    for index in range(3 + rows, 6 + rows):
        wait(index)
    if True:
        context_all = jnp.concatenate(contexts, axis=0)
        x_all = jnp.concatenate(firsts, axis=0)
        pre_attn = x_all.astype(F32) + (dot_nn(context_all, wo[...]) + row_of(bo))
        pre_attn_out[...] = pre_attn
        normed = layer_norm(pre_attn, row_of(ga), row_of(sa)).astype(BF16)
        up = dot_nn(normed, w_in_v[...]) + row_of(b_in)
        up_out[...] = up
        active = gelu_exact(up).astype(BF16)
        pre_ffn = normed.astype(F32) + (dot_nn(active, w_back_v[...]) + row_of(bb))
        pre_ffn_out[...] = pre_ffn
        enc_out[...] = layer_norm(pre_ffn, row_of(gf), row_of(sf)).astype(BF16)
        packs = (pack_0, pack_1, pack_2, pack_3)
        fill = pack_0.shape[1] - 2 * feature_dim
        group = ff_dim * LANES // fill
        size = group // GROUP
        if fill == ff_dim:
            for near in range(GROUP):
                packs[near][:, :ff_dim] = active
        else:
            for slot in range(fill // LANES):
                blocks = [
                    active[:, slot * group + size * b : slot * group + size * (b + 1)]
                    for b in range(GROUP)
                ]
                lanes = slot * LANES
                for near in range(GROUP):
                    source = (idx_ref[1] & (GROUP - 1)) ^ near
                    chosen = blocks[0]
                    for b in range(1, GROUP):
                        chosen = jnp.where(source == b, blocks[b], chosen)
                    packs[near][:, lanes : lanes + size] = chosen
                    packs[near][:, lanes + size : lanes + LANES] = jnp.zeros(
                        (active.shape[0], LANES - size), BF16
                    )
        for near in range(GROUP):
            packs[near][:, fill : fill + feature_dim] = normed
            packs[near][:, fill + feature_dim :] = context_all
    for copy in copies:
        copy.wait()


def full(shape):
    zeros = (0,) * len(shape)
    return pl.BlockSpec(shape, lambda *_: zeros)


ANY = pl.BlockSpec(memory_space=pl.ANY)


def active_width(places, ff_dim):
    group = GROUP * ff_dim // (2 * places)
    return ff_dim // group * LANES if group % LANES == 0 else ff_dim


def front(places, idx, segs, smalls, x_rows, mats):
    rows, length, feature_dim = x_rows.shape
    ff_dim = mats[-1].shape[0]
    cls = rows * SEGS
    shapes = (
        ((rows, length, feature_dim), BF16),
        ((rows, length, feature_dim), BF16),
        *(((cls, active_width(places, ff_dim) + 2 * feature_dim), BF16),) * GROUP,
        ((cls, feature_dim), BF16),
        ((cls, feature_dim), F32),
        ((cls, ff_dim), F32),
        ((cls, feature_dim), F32),
        ((cls, feature_dim), BF16),
        ((rows, length, LANES), BF16),
    )
    whole = pltpu.VMEM((rows, length, feature_dim), BF16)
    return pl.pallas_call(
        front_kernel,
        grid=(1,),
        in_specs=[pl.BlockSpec(memory_space=pltpu.SMEM)]
        + [full(a.shape) for a in (segs, *smalls)]
        + [ANY] * (1 + len(mats)),
        out_specs=[ANY, ANY] + [full(s) for s, _ in shapes[2:]],
        out_shape=[jax.ShapeDtypeStruct(s, d) for s, d in shapes],
        scratch_shapes=[whole]
        + [pltpu.VMEM(a.shape, BF16) for a in mats]
        + [
            whole,
            whole,
            pltpu.SemaphoreType.DMA((6 + rows,)),
            pltpu.SemaphoreType.DMA((2 * rows,)),
        ],
        compiler_params=pltpu.CompilerParams(vmem_limit_bytes=VMEM_BYTES),
        cost_estimate=pl.CostEstimate(
            flops=2 * rows * length * feature_dim * feature_dim * 3,
            bytes_accessed=30_000_000,
            transcendentals=rows * length * 384,
        ),
        name="front",
    )(idx, segs, *smalls, x_rows, *mats)


def segments_of(start, stop, length):
    found = []
    while start < stop:
        row, first = start // length, start % length
        tokens = min(stop - start, length - first)
        held = min(length, tokens + 128)
        found.append((row, first, tokens, max(0, min(first - 64, length - held)), held))
        start += tokens
    return found


def encode_kernel_at(
    segments, x_hbm, k_hbm, v_hbm, hot_hbm, wq_hbm, wo_hbm, w_in_hbm, w_back_hbm,
    bq, bo, ga, sa, b_in, bb, gf, sf, *refs
):
    enc_hbm, x_s, k_s, v_s, hot_s, enc_s, wq, wo, w_in, w_back, sems, out_sems = refs[-12:]
    feature_dim = x_s.shape[1]
    length = k_hbm.shape[1]
    ff_dim = w_in.shape[1]
    part, window = 128, 256
    count = len(segments)
    first_pairs, key_pairs, places, token_at, held_at = [], [], [], 0, 0
    for row, first, tokens, low, held in segments:
        near, kept = pl.ds(low, held), pl.ds(held_at, held)
        first_pairs.append((x_hbm.at[row, pl.ds(first, tokens)], x_s.at[pl.ds(token_at, tokens)]))
        key_pairs += [
            (hot_hbm.at[row, near], hot_s.at[kept]),
            (k_hbm.at[row, near], k_s.at[kept]),
            (v_hbm.at[row, near], v_s.at[kept]),
        ]
        places.append((token_at, held_at))
        token_at, held_at = token_at + tokens, held_at + held
    tail = [(wo_hbm, wo), (w_in_hbm, w_in), (w_back_hbm, w_back)]
    wait = loads([*first_pairs, (wq_hbm, wq), *key_pairs, *tail], sems)
    for index in range(count + 1):
        wait(index)
    x = x_s[...]
    query = ((dot_nn(x, wq[...]) + row_of(bq)).astype(BF16) * (HEAD_DIM**-0.5)).astype(BF16)
    left = iota((part, 128), 1) < HEAD_DIM
    for index in range(count + 1, 4 * count + 1):
        wait(index)
    contexts = []
    blocks = [
        (at + sub, first + sub, held_at - low)
        for (_, first, tokens, low, _), (at, held_at) in zip(segments, places)
        for sub in range(0, tokens, part)
    ]
    for at, base, shift in blocks:
        start = max(0, min(base - 64, length - window)) + shift
        keys = k_s[start : start + window, :]
        values = v_s[start : start + window, :]
        apart = ((hot_s[start : start + window, :].astype(F32) - 1.0) * FAR).astype(BF16)
        hot_query = hot_s[base + shift : base + shift + part, :]
        pieces = []
        for pair in range(feature_dim // 128):
            lanes = slice(pair * 128, pair * 128 + 128)
            both = query[at : at + part, lanes]
            zero = jnp.zeros_like(both)
            wide = jnp.concatenate(
                [
                    jnp.concatenate([jnp.where(left, both, zero), hot_query], axis=1),
                    jnp.concatenate([jnp.where(left, zero, both), hot_query], axis=1),
                ],
                axis=0,
            )
            logits = dot_nt(wide, jnp.concatenate([keys[:, lanes], apart], axis=1))
            top = jnp.max(logits, axis=1, keepdims=True)
            exponent = jnp.exp(logits - top)
            total = jnp.sum(exponent, axis=1, keepdims=True)
            out = dot_nn(exponent.astype(BF16), values[:, lanes]) * (1.0 / total)
            pieces.append(jnp.where(left, out[:part], out[part:]).astype(BF16))
        contexts.append(jnp.concatenate(pieces, axis=1))
    context = jnp.concatenate(contexts, axis=0)
    wait(4 * count + 1)
    pre_attn = x.astype(F32) + (dot_nn(context, wo[...]) + row_of(bo))
    normed = layer_norm(pre_attn, row_of(ga), row_of(sa)).astype(BF16)
    wait(4 * count + 2)
    wait(4 * count + 3)
    bias_in = row_of(b_in)
    total = normed.astype(F32) + row_of(bb)
    chunk = 768
    for start in range(0, ff_dim, chunk):
        cols = slice(start, start + chunk)
        up = dot_nn(normed, w_in[:, cols]) + bias_in[:, cols]
        total = total + dot_nn(gelu_exact(up).astype(BF16), w_back[cols, :])
    enc_s[...] = layer_norm(total, row_of(gf), row_of(sf)).astype(BF16)
    copies = [
        pltpu.make_async_copy(
            enc_s.at[pl.ds(at, tokens)], enc_hbm.at[row, pl.ds(first, tokens)], out_sems.at[index]
        )
        for index, ((row, first, tokens, _, _), (at, _)) in enumerate(zip(segments, places))
    ]
    for copy in copies:
        copy.start()
    for copy in copies:
        copy.wait()


def encode_part(start, stop, x_rows, keys, values, hot, mats, smalls, before):
    rows, length, feature_dim = x_rows.shape
    segments = segments_of(start, stop, length)
    tokens, held = stop - start, sum(segment[4] for segment in segments)
    extra = [] if before is None else [before]
    return pl.pallas_call(
        functools.partial(encode_kernel_at, segments),
        grid=(1,),
        in_specs=[ANY] * (4 + len(mats)) + [full(a.shape) for a in smalls] + [ANY for _ in extra],
        out_specs=ANY,
        out_shape=jax.ShapeDtypeStruct((rows, length, feature_dim), BF16),
        input_output_aliases={} if before is None else {4 + len(mats) + len(smalls): 0},
        scratch_shapes=[
            pltpu.VMEM((tokens, feature_dim), BF16),
            pltpu.VMEM((held, feature_dim), BF16),
            pltpu.VMEM((held, feature_dim), BF16),
            pltpu.VMEM((held, hot.shape[2]), BF16),
            pltpu.VMEM((tokens, feature_dim), BF16),
        ]
        + [pltpu.VMEM(a.shape, BF16) for a in mats]
        + [
            pltpu.SemaphoreType.DMA((4 * len(segments) + 4,)),
            pltpu.SemaphoreType.DMA((len(segments),)),
        ],
        compiler_params=pltpu.CompilerParams(vmem_limit_bytes=(56 if before is None else 32) * 1024 * 1024),
        cost_estimate=pl.CostEstimate(
            flops=tokens * feature_dim * feature_dim, bytes_accessed=1_000_000, transcendentals=0
        ),
        name="encode_part",
    )(x_rows, keys, values, hot, *mats, *smalls, *extra)


def middle_kernel(
    idx_ref, *refs
):
    own = refs[:GROUP]
    other = refs[GROUP : 2 * GROUP]
    (
        positives, pre_attn_ref, pre_ffn_ref, ga, gf, w_back_hbm, w_in_hbm, up_hbm, wo_hbm,
        scores_out, losses_out, late_out, gctx_out, gpa_out, vec_out,
        both, w_in_v, w_back_v, up_ref, wo, sems, wsems,
    ) = refs[2 * GROUP :]
    tower, place = idx_ref[0], idx_ref[1]
    far, cls, feature_dim = own[0].shape
    ff_dim = w_in_v.shape[1]
    copy_back = pltpu.make_async_copy(w_back_hbm, w_back_v, wsems.at[0])
    copy_in = pltpu.make_async_copy(w_in_hbm, w_in_v, wsems.at[1])
    copy_up = pltpu.make_async_copy(up_hbm, up_ref, wsems.at[2])
    copy_out = pltpu.make_async_copy(wo_hbm, wo, wsems.at[3])
    copies = []
    for side, group in ((tower, own), (1 - tower, other)):
        for near in range(GROUP):
            for slot in range(far):
                to = both.at[side, place ^ (slot * GROUP + near)]
                copies.append(
                    pltpu.make_async_copy(group[near].at[slot], to, sems.at[len(copies)])
                )
    for copy in copies:
        copy.start()
    copy_back.start()
    copy_up.start()
    copy_in.start()
    copy_out.start()
    for copy in copies:
        copy.wait()
    count = far * GROUP * cls
    scale = feature_dim**-0.5
    queries = both[0].reshape(count, feature_dim)
    positive_row = positives[...]
    block = min(count, max(64, (1 << 20) // count))

    def partial_of(first):
        passages = both[1, pl.ds(first // cls, block // cls)].reshape(block, feature_dim)
        scored = dot_nt(passages, queries) * scale
        top = jnp.max(scored, axis=0, keepdims=True)
        total = jnp.sum(jnp.exp(scored - top), axis=0, keepdims=True)
        hit = iota((block, count), 0) + first == positive_row
        return top, total, jnp.sum(jnp.where(hit, scored, 0.0), axis=0, keepdims=True)

    def joined(index, state):
        top, total, picked = partial_of(index * block)
        joint = jnp.maximum(state[0], top)
        return (
            joint,
            state[1] * jnp.exp(state[0] - joint) + total * jnp.exp(top - joint),
            state[2] + picked,
        )

    state = partial_of(0)
    if count // block > 1:
        state = lax.fori_loop(1, count // block, joined, state)
    row_log = state[0] + jnp.log(state[1])
    losses_out[...] = row_log - state[2]
    scores_out[...] = dot_nt(both[1, place], queries) * scale
    mine = both[tower, place]
    opposite = both[1 - tower].reshape(count, feature_dim)
    own_scores = dot_nt(mine, opposite) * scale
    own_top = jnp.max(own_scores, axis=1, keepdims=True)
    own_log = own_top + jnp.log(jnp.sum(jnp.exp(own_scores - own_top), axis=1, keepdims=True))
    lanes = iota((cls, count), 1)
    mine_index = iota((cls, count), 0) + place * cls
    spread_positive = jnp.broadcast_to(positive_row, (cls, count))
    own_positive = jnp.sum(
        jnp.where(lanes == mine_index, spread_positive.astype(F32), 0.0), axis=1, keepdims=True
    ).astype(jnp.int32)
    is_query = tower == 0
    log_used = jnp.where(is_query, jnp.broadcast_to(own_log, (cls, count)), row_log)
    hit_query = (lanes == own_positive).astype(F32)
    hit_passage = (spread_positive == mine_index).astype(F32)
    hit = jnp.where(is_query, hit_query, hit_passage)
    grad_scores = (jnp.exp(own_scores - log_used) - hit).astype(BF16)
    grad_cls = dot_nn(grad_scores, opposite) * scale
    grad_pre_ffn, grad_gf, grad_sf = layer_norm_back(pre_ffn_ref[...], row_of(gf), grad_cls)
    vec_out[0:1, :] = grad_gf
    vec_out[1:2, :] = grad_sf
    grad_down = grad_pre_ffn.astype(BF16)
    vec_out[2:3, :] = jnp.sum(grad_down.astype(F32), axis=0, keepdims=True)
    copy_back.wait()
    copy_up.wait()
    grad_up = (dot_nt(grad_down, w_back_v[...]) * gelu_slope(up_ref[...])).astype(BF16)
    late_out[:, :ff_dim] = grad_up
    late_out[:, ff_dim : ff_dim + feature_dim] = grad_down
    copy_in.wait()
    grad_normed = grad_pre_ffn + dot_nt(grad_up, w_in_v[...])
    grad_pre_attn, grad_ga, grad_sa = layer_norm_back(pre_attn_ref[...], row_of(ga), grad_normed)
    vec_out[3:4, :] = grad_ga
    vec_out[4:5, :] = grad_sa
    gpa_out[...] = grad_pre_attn
    grad_attended = grad_pre_attn.astype(BF16)
    late_out[:, ff_dim + feature_dim :] = grad_attended
    vec_out[5:6, :] = jnp.sum(grad_attended.astype(F32), axis=0, keepdims=True)
    copy_out.wait()
    gctx_out[...] = dot_nt(grad_attended, wo[...]).astype(BF16)


def middle(idx, own, other, positives, pre_attn, up, pre_ffn, w_back, w_in, wo, ga, gf):
    far, cls, feature_dim = own[0].shape
    ff_dim = w_in.shape[1]
    places = far * GROUP
    count = places * cls
    shapes = (
        ((cls, count), F32),
        ((1, count), F32),
        ((cls, ff_dim + 2 * feature_dim), BF16),
        ((cls, feature_dim), BF16),
        ((cls, feature_dim), F32),
        ((8, feature_dim), F32),
    )
    smalls = (positives, pre_attn, pre_ffn, ga, gf)
    return pl.pallas_call(
        middle_kernel,
        in_specs=[pl.BlockSpec(memory_space=pltpu.SMEM)]
        + [ANY] * (2 * GROUP)
        + [full(a.shape) for a in smalls]
        + [ANY] * 4,
        out_specs=[full(s) for s, _ in shapes],
        out_shape=[jax.ShapeDtypeStruct(s, d) for s, d in shapes],
        grid=(1,),
        scratch_shapes=[
            pltpu.VMEM((2, places, cls, feature_dim), BF16),
            pltpu.VMEM(w_in.shape, BF16),
            pltpu.VMEM(w_back.shape, BF16),
            pltpu.VMEM(up.shape, F32),
            pltpu.VMEM(wo.shape, BF16),
            pltpu.SemaphoreType.DMA((2 * places,)),
            pltpu.SemaphoreType.DMA((4,)),
        ],
        compiler_params=pltpu.CompilerParams(vmem_limit_bytes=56 * 1024 * 1024),
        cost_estimate=pl.CostEstimate(
            flops=2 * count * count * feature_dim, bytes_accessed=20_000_000, transcendentals=count * count
        ),
        name="loss",
    )(idx, *own, *other, *smalls, w_back, w_in, up, wo)


def spread_rows(shape, sizes, strides, masks, dim=0):
    rest = iota(shape, dim)
    total = jnp.zeros(shape, jnp.int32)
    for size, stride, mask in zip(reversed(sizes), reversed(strides), reversed(masks)):
        above = jnp.floor((rest.astype(F32) + 0.5) * (1.0 / size)).astype(jnp.int32)
        digit = rest - above * size
        total = total + (digit ^ mask) * stride
        rest = above
    return total


def attn_back_kernel(
    idx_ref, seg_ref, qc_ref, gctx_ref, gpa_ref, vec_ref, x_hbm, k_hbm, v_hbm, wq_hbm, wk_hbm, wv_hbm,
    back_hbm, send_hbm, keep_hbm,
    x_s, k_s, v_s, wq, wk, wv, mixed_s, back_s, send_s, keep_s, sems, out_sems,
):
    tower, place = idx_ref[0], idx_ref[1]
    towers = 2
    rows, length, feature_dim = x_s.shape
    head_count = feature_dim // HEAD_DIM
    pairs = []
    for row in range(rows):
        pairs += [(k_hbm.at[row], k_s.at[row]), (v_hbm.at[row], v_s.at[row]), (x_hbm.at[row], x_s.at[row])]
    pairs += [(wq_hbm, wq), (wk_hbm, wk), (wv_hbm, wv)]
    wait = loads(pairs, sems)
    mask = head_mask(head_count, SEGS, feature_dim)
    scale = HEAD_DIM**-0.5
    shape = (feature_dim, feature_dim)
    wide = head_count * SEGS
    far, block = keep_s.shape[1:3]
    source = spread_rows(
        (1, feature_dim),
        (towers, GROUP, far, block),
        (far * GROUP * block, block, GROUP * block, 1),
        (tower, place & (GROUP - 1), place // GROUP, 0),
        1,
    )
    order = jnp.where(iota(shape, 0) == source, 1.0, 0.0).astype(BF16)
    scatters, wides, drawn, drawn_cls, grads_q, biases = [], [], [], [], [], []
    for row in range(rows):
        here = slice(row * SEGS, (row + 1) * SEGS)
        seg_row = seg_ref[0, row : row + 1, :]
        query_wide = block_heads((qc_ref[here, :] * scale).astype(BF16), mask, head_count)
        gctx_wide = block_heads(gctx_ref[here, :], mask, head_count)
        wait(3 * row)
        key_row = k_s[row]
        probs = cls_probs(query_wide, key_row, seg_row, head_count, SEGS)
        wait(3 * row + 1)
        grad_probs = dot_nt(gctx_wide, v_s[row])
        inner = jnp.sum(probs * grad_probs, axis=1, keepdims=True)
        grad_logits = (probs * (grad_probs - inner)).astype(BF16)
        grad_query = heads_to_rows(dot_nn(grad_logits, key_row), mask, head_count, SEGS)
        grad_query = (grad_query * scale).astype(BF16)
        mixed = jnp.concatenate([grad_logits, probs.astype(BF16)], axis=0)
        mixed_s[row] = mixed
        wait(3 * row + 2)
        x = x_s[row]
        first = jnp.where(cls_onehot(seg_row, SEGS), 1.0, 0.0).astype(BF16)
        drawn.append(dot_nn(mixed, x).astype(BF16))
        drawn_cls.append(dot_nn(first, x).astype(BF16))
        grads_q.append(grad_query)
        bias_of_value = jnp.sum(
            gctx_wide.astype(F32) * jnp.sum(mixed[wide:].astype(F32), axis=1, keepdims=True),
            axis=0, keepdims=True,
        )
        biases.append((jnp.sum(grad_query.astype(F32), axis=0, keepdims=True), bias_of_value))
        if row == 0:
            wait(3 * rows)
        cls_back = gpa_ref[here, :] + dot_nt(grad_query, wq[...])
        scatters.append((jnp.concatenate([first] * 3, axis=0), jnp.concatenate(split(cls_back), axis=0)))
        wides.append((query_wide, gctx_wide))
    def over_rows(parts):
        return jnp.concatenate(parts, axis=0)

    turned_k = dot_nn(over_rows([part[:wide] for part in drawn]), order).astype(BF16)
    turned_v = dot_nn(over_rows([part[wide:] for part in drawn]), order).astype(BF16)
    turned_cls = dot_nn(over_rows(drawn_cls), order).astype(BF16)
    acc_q = dot_tn(turned_cls, over_rows(grads_q))
    acc_k = dot_tn(turned_k, over_rows([pair[0] for pair in wides]))
    acc_v = dot_tn(turned_v, over_rows([pair[1] for pair in wides]))
    bias_q, bias_v = biases[0]
    for more in biases[1:]:
        bias_q, bias_v = bias_q + more[0], bias_v + more[1]
    vectors = jnp.concatenate(
        [vec_ref[0:6, :], bias_q, bias_v, jnp.zeros((LANES - 8, feature_dim), F32)], axis=0
    )
    high, second, third = split(vectors)
    columns = (dot_nn(high, order) + (dot_nn(second, order) + dot_nn(third, order))).T
    half = feature_dim // towers
    place_at = 0
    for grad in (acc_q, acc_k, acc_v, columns):
        lanes = slice(place_at, place_at + grad.shape[1])
        cut = (GROUP, far, block, grad.shape[1])
        keep_s[:, :, :, lanes] = grad[:half].astype(BF16).reshape(cut)
        send_s[:, :, :, lanes] = grad[half:].astype(BF16).reshape(cut)
        place_at = lanes.stop
    copies = [
        pltpu.make_async_copy(send_s, send_hbm, out_sems.at[0]),
        pltpu.make_async_copy(keep_s, keep_hbm, out_sems.at[1]),
    ]
    for copy in copies:
        copy.start()
    wait(3 * rows + 1)
    wait(3 * rows + 2)
    part = length // 4
    for row in range(rows):
        first, pieces = scatters[row]
        query_wide, gctx_wide = wides[row]
        spread = jnp.concatenate(
            [dot_nt(query_wide, wk[...]).astype(BF16), dot_nt(gctx_wide, wv[...]).astype(BF16)], axis=0
        )
        for start in range(0, length, part):
            here = slice(start, start + part)
            back = dot_tn(mixed_s[row, :, here], spread)
            back_s[row, here, :] = back + dot_tn(first[:, here], pieces)
            copy = pltpu.make_async_copy(
                back_s.at[row, pl.ds(start, part)],
                back_hbm.at[row, pl.ds(start, part)],
                out_sems.at[len(copies)],
            )
            copy.start()
            copies.append(copy)
    for copy in copies:
        copy.wait()


def attn_back(idx, segs, qc, gctx, gpa, vectors, x_rows, keys, values, wq, wk, wv, places):
    rows, length, feature_dim = x_rows.shape
    block = feature_dim // (2 * places)
    half = (GROUP, places // GROUP, block, 3 * feature_dim + LANES)
    shapes = (((rows, length, feature_dim), F32), (half, BF16), (half, BF16))
    smalls = (segs, qc, gctx, gpa, vectors)
    square = pltpu.VMEM((feature_dim, feature_dim), BF16)
    whole = pltpu.VMEM((rows, length, feature_dim), BF16)
    return pl.pallas_call(
        attn_back_kernel,
        grid=(1,),
        in_specs=[pl.BlockSpec(memory_space=pltpu.SMEM)]
        + [full(a.shape) for a in smalls]
        + [ANY] * 6,
        out_specs=[ANY] * 3,
        out_shape=[jax.ShapeDtypeStruct(s, d) for s, d in shapes],
        scratch_shapes=[whole, whole, whole, square, square, square]
        + [
            pltpu.VMEM((rows, 2 * feature_dim // HEAD_DIM * SEGS, length), BF16),
            pltpu.VMEM((rows, length, feature_dim), F32),
            pltpu.VMEM(half, BF16),
            pltpu.VMEM(half, BF16),
            pltpu.SemaphoreType.DMA((3 * rows + 3,)),
            pltpu.SemaphoreType.DMA((2 + 4 * rows,)),
        ],
        compiler_params=pltpu.CompilerParams(vmem_limit_bytes=56 * 1024 * 1024),
        cost_estimate=pl.CostEstimate(
            flops=2 * rows * length * feature_dim * feature_dim * 6,
            bytes_accessed=30_000_000,
            transcendentals=rows * length * 384,
        ),
        name="attention_back",
    )(idx, *smalls, x_rows, keys, values, wq, wk, wv)


def weights_kernel(feature_dim, ff_dim, idx_ref, *refs):
    early = refs[:GROUP]
    late = refs[GROUP : 2 * GROUP]
    keep_0, keep_1, send_0, send_1 = refs[2 * GROUP :]
    tower, place = idx_ref[0], idx_ref[1]
    pairs, block, _ = send_0.shape
    far = 2 * pairs
    pieces = ff_dim // feature_dim
    fill = early[0].shape[1] - 2 * feature_dim

    def pick(group, near, columns):
        source = spread_rows(
            (2 * far * block, 1),
            (2, 2, pairs, block),
            (far * group, group, 2 * group, 1),
            (tower, place // GROUP & 1, place // (2 * GROUP), 0),
        )
        shape = (2 * far * block, columns)
        return jnp.where(iota(shape, 1) == source + near, 1.0, 0.0).astype(BF16)

    def stacked(parts, first, columns):
        return jnp.concatenate([ref[:, first : first + columns] for ref in parts], axis=0)

    def put(first, grad):
        columns = grad.shape[1]
        half = pairs * block
        shape = (pairs, block, columns)
        for index, ref in enumerate((keep_0, keep_1, send_0, send_1)):
            rows = grad[index * half : (index + 1) * half]
            ref[:, :, first : first + columns] = rows.astype(BF16).reshape(shape)

    near = place & (GROUP - 1)
    narrow = pick(GROUP * block, near * block, feature_dim)
    grad_up = stacked(late, 0, ff_dim)
    grad_down = stacked(late, ff_dim, feature_dim)
    grad_attended = stacked(late, ff_dim + feature_dim, feature_dim)
    active = stacked(early, 0, fill)
    normed = dot_nt(narrow, stacked(early, fill, feature_dim)).astype(BF16)
    context = dot_nt(narrow, stacked(early, fill + feature_dim, feature_dim)).astype(BF16)
    put(0, dot_nn(normed, grad_up))
    for piece in range(pieces):
        if fill == ff_dim:
            chosen = pick(GROUP * pieces * block, (near * pieces + piece) * block, fill)
        else:
            chosen = pick(LANES, piece * block, fill)
        turned = dot_nt(chosen, active).astype(BF16)
        put(ff_dim + piece * feature_dim, dot_nn(turned, grad_down))
    put(2 * ff_dim, dot_nn(context, grad_attended))
    bias = jnp.sum(grad_up.astype(F32), axis=0, keepdims=True)
    shifted = [
        jnp.concatenate([bias[:, piece * block :], bias[:, : piece * block]], axis=1)
        for piece in range(1, pieces)
    ]
    stack = jnp.concatenate([bias, *shifted, jnp.zeros((LANES - pieces, ff_dim), F32)], axis=0)
    high, second, third = split(stack)
    chosen = pick(GROUP * pieces * block, near * pieces * block, ff_dim)
    columns = dot_nt(chosen, high) + (dot_nt(chosen, second) + dot_nt(chosen, third))
    put(2 * ff_dim + feature_dim, columns)


def weights(idx, early, late, places, feature_dim, ff_dim):
    far = places // GROUP
    block = feature_dim // (2 * places)
    packed = 2 * ff_dim + feature_dim + LANES
    half = (far // 2, block, packed)
    return pl.pallas_call(
        functools.partial(weights_kernel, feature_dim, ff_dim),
        grid=(1,),
        in_specs=[pl.BlockSpec(memory_space=pltpu.SMEM)] + [full(a.shape) for a in (*early, *late)],
        out_specs=[full(half)] * 4,
        out_shape=[jax.ShapeDtypeStruct(half, BF16)] * 4,
        compiler_params=pltpu.CompilerParams(vmem_limit_bytes=24 * 1024 * 1024),
        cost_estimate=pl.CostEstimate(
            flops=50_000_000_000, bytes_accessed=14_000_000, transcendentals=0
        ),
        name="weight_grads",
    )(idx, *early, *late)


def tied(*values):
    return lax.optimization_barrier(values)


def on_device(
    hidden_in, segment_ids, positives, w_query, b_query, w_key, w_value, b_value, w_out, b_out,
    gain_attn, shift_attn, w_in, b_in, w_back, b_back, gain_ffn, shift_ffn,
):
    feature_dim = hidden_in.shape[2]
    ff_dim = w_in.shape[1]
    rows, length = segment_ids.shape[1], segment_ids.shape[2]
    places = lax.axis_size("dp")
    far = places // GROUP
    tower, place = lax.axis_index("tower"), lax.axis_index("dp")
    idx = jnp.stack([tower, place, places]).astype(jnp.int32)
    x_rows = hidden_in.reshape(rows, length, feature_dim)
    keys, values, *pack, query_cls, pre_attn, up, pre_ffn, enc_cls, hot = front(
        places, idx, segment_ids,
        (b_query, b_value, b_out, gain_attn, shift_attn, b_in, b_back, gain_ffn, shift_ffn),
        x_rows, (w_key, w_value, w_query, w_out, w_in, w_back),
    )
    mats = (w_query, w_out, w_in, w_back)
    smalls = (b_query, b_out, gain_attn, shift_attn, b_in, b_back, gain_ffn, shift_ffn)

    quarter = rows * length // 4
    cuts = (0, 0, quarter, 5 * quarter // 2, 4 * quarter)

    def encode(part, before):
        return encode_part(
            cuts[part], cuts[part + 1], x_rows, keys, values, hot, mats, smalls, before
        )

    along = [moved(enc_cls, "dp", GROUP * m) for m in range(1, far)]
    early = [pack[0]] + [moved(pack[m], "dp", m) for m in range(1, GROUP)]
    own = jnp.stack([enc_cls] + list(along))
    own, early[1:3], hot = tied(own, early[1:3], hot)
    crossed = [moved(own, "dp", m) for m in range(1, GROUP)]
    encoded = encode(1, None)
    crossed, encoded = tied(crossed, encoded)
    own = [own] + list(crossed)
    other = [moved(quad, "tower", 1) for quad in own]
    scores, losses, late_own, gctx, gpa, vec_mid = middle(
        idx, own, other, positives.reshape(1, -1), pre_attn, up, pre_ffn, w_back, w_in,
        w_out, gain_attn, gain_ffn,
    )
    gctx, early = tied(gctx, early)
    late = [late_own] + [moved(late_own, "dp", m) for m in range(1, GROUP)]
    back, send, keep = attn_back(
        idx, segment_ids, query_cls, gctx, gpa, vec_mid, x_rows, keys, values,
        w_query, w_key, w_value, places,
    )
    late, keep = tied(late, keep)
    send = moved(send, "tower", 1)
    *weight_keep, first_send, last_send = weights(idx, early, late, places, feature_dim, ff_dim)
    weight_send = [first_send, last_send]
    send, weight_keep, weight_send = tied(send, weight_keep, weight_send)
    paired = [keep[m].astype(F32) + send[m].astype(F32) for m in range(GROUP)]
    near_out = [part.astype(BF16) for part in paired[1:]]
    near_out, weight_keep, weight_send = tied(near_out, weight_keep, weight_send)
    weight_send = [moved(weight_send[m], "tower", 1) for m in (1, 0)][::-1]
    near_sent = [moved(near_out[m - 1], "dp", m) for m in range(1, GROUP)]
    weight_out = (weight_keep[1].astype(F32) + weight_send[1].astype(F32)).astype(BF16)
    weight_out, encoded = tied(weight_out, encoded)
    reach, arrived = 1, moved(weight_out, "dp", GROUP)
    encoded = encode(2, encoded)
    arrived, encoded = tied(arrived, encoded)
    weight_sum = weight_keep[0].astype(F32) + weight_send[0].astype(F32) + arrived.astype(F32)
    near_sent, weight_sum, encoded = tied(near_sent, weight_sum, encoded)
    near = paired[0]
    for part in near_sent:
        near = near + part.astype(F32)
    far_out = [near[m].astype(BF16) for m in range(1, far)]
    while weight_sum.shape[0] > 1:
        reach = reach * 2
        half = weight_sum.reshape(weight_sum.shape[0] // 2, 2, *weight_sum.shape[1:])
        weight_out = half[:, 1].astype(BF16)
        last = reach == far // 2
        if last:
            far_out, weight_out, encoded = tied(far_out, weight_out, encoded)
            far_sent = [moved(far_out[m - 1], "dp", GROUP * m) for m in range(1, far)]
        arrived = moved(weight_out, "dp", GROUP * reach)
        if last:
            encoded = encode(3, encoded)
            far_sent, arrived, encoded = tied(far_sent, arrived, encoded)
        weight_sum = half[:, 0] + arrived.astype(F32)
    weight_sum = weight_sum[0]
    grad_qkv = near[0]
    for part in far_sent:
        grad_qkv = grad_qkv + part.astype(F32)
    grad_in = weight_sum[:, :ff_dim]
    grad_back = jnp.concatenate(
        [
            weight_sum[:, first : first + feature_dim]
            for first in range(ff_dim, 2 * ff_dim, feature_dim)
        ],
        axis=0,
    )
    grad_out = weight_sum[:, 2 * ff_dim : 2 * ff_dim + feature_dim]
    first = 2 * ff_dim + feature_dim
    b_i = weight_sum[:, first : first + ff_dim // feature_dim].T.reshape(-1)
    columns = grad_qkv[:, 3 * feature_dim : 3 * feature_dim + 8].T
    g_f, s_f, b_b, g_a, s_a, b_o, b_q, b_v = [columns[i] for i in range(8)]
    return (
        encoded.reshape(hidden_in.shape),
        scores.T,
        losses.reshape(-1),
        back.reshape(hidden_in.shape),
        grad_qkv[:, :feature_dim],
        b_q,
        grad_qkv[:, feature_dim : 2 * feature_dim],
        grad_qkv[:, 2 * feature_dim : 3 * feature_dim],
        b_v,
        grad_out,
        b_o,
        g_a,
        s_a,
        grad_in,
        b_i,
        grad_back,
        b_b,
        g_f,
        s_f,
    )


def solution(mesh):
    placed = (P("tower", "dp", None), P("tower", "dp", None)) + (P(),) * 16
    matrix, vector = P(("tower", "dp"), None), P(("tower", "dp"))
    return jax.shard_map(
        on_device,
        mesh=mesh,
        in_specs=placed,
        out_specs=(
            P("tower", "dp", None),
            P(None, "dp"),
            P(),
            P("tower", "dp", None),
            matrix,
            vector,
            matrix,
            matrix,
            vector,
            matrix,
            vector,
            vector,
            vector,
            matrix,
            vector,
            matrix,
            vector,
            vector,
            vector,
        ),
        check_vma=False,
    )
```
